32 devices in a mesh: section: 4 (over y, x), dom: 8 (over z, core).
Axes of the slice: x: 2, y: 2, z: 4, core: 2. Of those that a mesh axis runs over, the one named last changes fastest.
Arguments:
- features: bfloat16 [4, 16384, 128], P(None, 'dom'), may hold values from -6 to 6
- sources: int32 [4, 16384, 8], P(None, 'dom'), may hold values from 0 to 2111, as said below
- send_index: int32 [4, 512], P(None, 'dom'), may hold values from 0 to 2047, as said below
- labels: int32 [4, 16384], P(None, 'dom'), may hold values from 0 to 39
- label_mask: int32 [4, 16384], P(None, 'dom'), may hold values from 0 to 1, as said below
- w_in: float32 [128, 256], P('dom'), may hold values from -0.5 to 0.5
- w_gat: float32 [2, 2, 256, 256], P(None, None, 'dom'), may hold values from -0.375 to 0.375
- w_out: float32 [64, 40], P('dom'), may hold values from -0.75 to 0.75
- small_params: float32 [1128], replicated, may hold values from -1 to 1
- stat_l_in: float32 [128, 128], P('dom')
- stat_r_in: float32 [256, 256], replicated
- stat_l_gat: float32 [2, 2, 256, 256], P(None, None, 'dom')
- stat_r_gat: float32 [2, 2, 256, 256], replicated, as said below
- stat_l_out: float32 [64, 64], P('dom')
- stat_r_out: float32 [40, 40], replicated
- root_l_in: float32 [128, 128], P('dom')
- root_r_in: float32 [256, 256], replicated
- root_l_gat: float32 [2, 2, 256, 256], P(None, None, 'dom')
- root_r_gat: float32 [2, 2, 256, 256], replicated, as said below
- root_l_out: float32 [64, 64], P('dom')
- root_r_out: float32 [40, 40], replicated
- adam_first: float32 [1128], replicated
- adam_second: float32 [1128], replicated
- ema_in: float32 [128, 256], P('dom'), may hold values from -0.5 to 0.5
- ema_gat: float32 [2, 2, 256, 256], P(None, None, 'dom'), may hold values from -0.375 to 0.375
- ema_out: float32 [64, 40], P('dom'), may hold values from -0.75 to 0.75
- ema_small: float32 [1128], replicated, may hold values from -1 to 1
Outputs:
- new_w_in: float32 [128, 256], P('dom')
- new_w_gat: float32 [2, 2, 256, 256], P(None, None, 'dom')
- new_w_out: float32 [64, 40], P('dom')
- new_small: float32 [1128], replicated
- new_l_in: float32 [128, 128], P('dom')
- new_r_in: float32 [256, 256], replicated
- new_l_gat: float32 [2, 2, 256, 256], P(None, None, 'dom')
- new_r_gat: float32 [2, 2, 256, 256], replicated
- new_l_out: float32 [64, 64], P('dom')
- new_r_out: float32 [40, 40], replicated
- new_first: float32 [1128], replicated
- new_second: float32 [1128], replicated
- new_ema_in: float32 [128, 256], P('dom')
- new_ema_gat: float32 [2, 2, 256, 256], P(None, None, 'dom')
- new_ema_out: float32 [64, 40], P('dom')
- new_ema_small: float32 [1128], replicated
- mean_loss: float32 [], replicated
- grad_norm: float32 [], replicated
The draws below stay inside these ranges and needn't reach their ends.
Inputs may be any that keep to these rules, and one draw needn't show every extreme that they name: `sources`: every source is a node of the same graph: graphs of 64 nodes, 32 of them on either side of each partition boundary; entries below 2048 are the partition's own nodes, 2048 + j the j-th extended row from the previous partition, 2080 + j the j-th from the next. `send_index`: per partition the first 32 entries are its nodes 0 to 31 in some order, the last 32 its nodes 2016 to 2047 in some order. `label_mask`: node 0 of every micro-batch counts. `stat_r_gat`: symmetric. `root_r_gat`: symmetric.
All inputs are finite; a program needn't handle non-finite values.
Results may differ from the reference program's by a relative error of at most 0.014.
Values may be sent and summed in bfloat16 or wider, within the bound.
No kernel may reach another device: no remote copies, remote signals or barrier semaphores. Data moves between devices by JAX's collectives and lax.ppermute only.
A program may use at most 384 MiB of HBM per device.

```python
import math
import jax
import jax.numpy as jnp
from jax import lax

FEAT = 128
HEADS = 4
HSIZE = 64
CLASSES = 40
NODE_DEV = 2048
GRAPH = 64
DEG = 8
MICRO = 4
STEPS = 5
HID = 256
HALF = 32
NODES = 16384
SMALL = 1128
PARAMS = 298600
N_DOM = 8


clip_norm = 0.001


def grad_entry():
    return clip_norm / math.sqrt(PARAMS)


def shuffled(key, count_items, lead_shape):
    scores = jax.random.randint(key, lead_shape + (count_items,), 0, 1 << 20) * count_items
    scores = scores + jnp.arange(count_items, dtype=jnp.int32)
    return jnp.argsort(scores, axis=-1).astype(jnp.int32)


def draw_sources(key, part):
    key = jax.random.fold_in(key, 101)
    node_local = jnp.arange(NODES, dtype=jnp.int32) % NODE_DEV
    graph_no = (node_local + HALF) // GRAPH
    graph_start = graph_no * GRAPH - HALF
    candidate = jax.random.randint(key, (MICRO, NODES, DEG), 0, GRAPH) + graph_start[None, :, None]
    picked = jnp.where(candidate < 0, candidate + NODE_DEV + HALF, jnp.where(candidate >= NODE_DEV, candidate + HALF, candidate))
    column = jnp.arange(DEG, dtype=jnp.int32)[None, None, :]
    row_local = node_local[None, :, None]
    picked = jnp.where((column == 0) & (row_local == NODE_DEV - 1), NODE_DEV + 2 * HALF - 1, picked)
    picked = jnp.where((column == 0) & (row_local == 1), 0, picked)
    return picked.astype(jnp.int32)


def draw_send_index(key, part):
    key = jax.random.fold_in(key, 102)
    part_count = NODES // NODE_DEV
    key_one, key_two = jax.random.split(key)
    lower_half = shuffled(key_one, HALF, (MICRO, part_count))
    upper_half = shuffled(key_two, HALF, (MICRO, part_count)) + (NODE_DEV - HALF)
    joined = jnp.concatenate([lower_half, upper_half], axis=2)
    return joined.reshape(MICRO, part_count * 2 * HALF).astype(jnp.int32)


def draw_label_mask(key, part):
    key = jax.random.fold_in(key, 103)
    part_count = NODES // NODE_DEV
    owner_part = jnp.arange(NODES, dtype=jnp.int32) // NODE_DEV
    keep_limit = 200 + 600 * owner_part // max(part_count - 1, 1)
    chosen = (jax.random.randint(key, (MICRO, NODES), 0, 1000) < keep_limit[None, :]).astype(jnp.int32)
    return chosen.at[:, 0].set(1)


def symmetric_draw(key, lead_shape, order_size, factor, diag_low, diag_high, off_share):
    key_one, key_two = jax.random.split(key)
    diagonal = jax.random.uniform(key_one, lead_shape + (order_size,), jnp.float32, diag_low, diag_high)
    noise_part = jax.random.normal(key_two, lead_shape + (order_size, order_size), jnp.float32)
    noise_part = (noise_part + jnp.swapaxes(noise_part, -1, -2)) * (off_share / math.sqrt(2.0 * order_size))
    identity = jnp.eye(order_size, dtype=jnp.float32)
    return factor * (noise_part + identity * diagonal[..., :, None])


def stat_draw(key, salt, lead_shape, order_size):
    key = jax.random.fold_in(key, salt)
    return symmetric_draw(key, lead_shape, order_size, order_size * grad_entry() ** 2, 0.5, 2.0, 0.3)


def root_draw(key, salt, lead_shape, order_size):
    key = jax.random.fold_in(key, salt)
    return symmetric_draw(key, lead_shape, order_size, (order_size * grad_entry() ** 2) ** (-0.25), 0.75, 1.25, 0.3)


def draw_stat_l_in(key, part):
    return stat_draw(key, 201, (), FEAT)


def draw_stat_r_in(key, part):
    return stat_draw(key, 202, (), HID)


def draw_stat_l_gat(key, part):
    return stat_draw(key, 203, (2, 2), HID)


def draw_stat_r_gat(key, part):
    return stat_draw(key, 204, (2, 2), HID)


def draw_stat_l_out(key, part):
    return stat_draw(key, 205, (), HSIZE)


def draw_stat_r_out(key, part):
    return stat_draw(key, 206, (), CLASSES)


def draw_root_l_in(key, part):
    return root_draw(key, 301, (), FEAT)


def draw_root_r_in(key, part):
    return root_draw(key, 302, (), HID)


def draw_root_l_gat(key, part):
    return root_draw(key, 303, (2, 2), HID)


def draw_root_r_gat(key, part):
    return root_draw(key, 304, (2, 2), HID)


def draw_root_l_out(key, part):
    return root_draw(key, 305, (), HSIZE)


def draw_root_r_out(key, part):
    return root_draw(key, 306, (), CLASSES)


def draw_adam_first(key, part):
    key = jax.random.fold_in(key, 401)
    return 0.11 * 3.0 * grad_entry() * jax.random.normal(key, (SMALL,), jnp.float32)


def draw_adam_second(key, part):
    key = jax.random.fold_in(key, 402)
    return jax.random.uniform(key, (SMALL,), jnp.float32, 1.0, 4.0) * (0.001 * (3.0 * grad_entry()) ** 2)


def with_ends(values, own_key, least, top_value):
    shape = values.shape
    spot = [jax.random.randint(jax.random.fold_in(own_key, axis), (), 0, shape[axis]) for axis in range(len(shape))]
    values = values.at[tuple(spot)].set(least)
    longest = shape.index(max(shape))
    spot[longest] = (spot[longest] + 1) % shape[longest]
    return values.at[tuple(spot)].set(top_value)


def level_of(own_key, shape, cuts, least, top_value):
    def one(position, shards_of):
        steps = jax.random.uniform(jax.random.fold_in(jax.random.fold_in(own_key, 6), position), (shards_of,), jnp.float32, least / len(cuts), top_value / len(cuts))
        return jnp.repeat(jnp.exp(steps), shape[position] // shards_of).reshape((-1,) + (1,) * (len(shape) - position - 1))

    factor_of = one(*cuts[0])
    for cut in cuts[1:]:
        factor_of = factor_of * one(*cut)
    return factor_of


def bell_draw(rng, shape, width, limit, cuts=(), kind=jnp.bfloat16):
    entries = jax.random.normal(rng, shape, jnp.float32) * width
    if len(cuts) > 0:
        entries = level_of(rng, shape, cuts, -0.22, 0.18) * entries
    return jnp.clip(entries, min=-limit, max=limit).astype(kind)


def setup_inputs(seed: int = 0) -> dict:
    keys = jax.random.split(jax.random.key(seed), 28)
    return {
        "features": bell_draw(keys[0], (MICRO, NODES, FEAT), 1.0, 6.0, ((1, 8),)),
        "sources": draw_sources(jax.random.fold_in(keys[27], 71), 0),
        "send_index": draw_send_index(jax.random.fold_in(keys[27], 71), 0),
        "labels": with_ends(jax.random.randint(keys[3], (MICRO, NODES), 0, CLASSES), jax.random.fold_in(keys[3], 1), 0, CLASSES - 1).astype(jnp.int32),
        "label_mask": draw_label_mask(jax.random.fold_in(keys[27], 71), 0),
        "w_in": bell_draw(keys[5], (FEAT, HID), FEAT ** -0.5, 0.5, ((0, 8),), jnp.float32),
        "w_gat": bell_draw(keys[6], (2, 2, HID, HID), HID ** -0.5, 0.375, ((2, 8),), jnp.float32),
        "w_out": bell_draw(keys[7], (HSIZE, CLASSES), HSIZE ** -0.5, 0.75, ((0, 8),), jnp.float32),
        "small_params": bell_draw(keys[8], (SMALL,), 0.25, 1.0, (), jnp.float32),
        "stat_l_in": draw_stat_l_in(jax.random.fold_in(keys[27], 71), 0),
        "stat_r_in": draw_stat_r_in(jax.random.fold_in(keys[27], 71), 0),
        "stat_l_gat": draw_stat_l_gat(jax.random.fold_in(keys[27], 71), 0),
        "stat_r_gat": draw_stat_r_gat(jax.random.fold_in(keys[27], 71), 0),
        "stat_l_out": draw_stat_l_out(jax.random.fold_in(keys[27], 71), 0),
        "stat_r_out": draw_stat_r_out(jax.random.fold_in(keys[27], 71), 0),
        "root_l_in": draw_root_l_in(jax.random.fold_in(keys[27], 71), 0),
        "root_r_in": draw_root_r_in(jax.random.fold_in(keys[27], 71), 0),
        "root_l_gat": draw_root_l_gat(jax.random.fold_in(keys[27], 71), 0),
        "root_r_gat": draw_root_r_gat(jax.random.fold_in(keys[27], 71), 0),
        "root_l_out": draw_root_l_out(jax.random.fold_in(keys[27], 71), 0),
        "root_r_out": draw_root_r_out(jax.random.fold_in(keys[27], 71), 0),
        "adam_first": draw_adam_first(jax.random.fold_in(keys[27], 71), 0),
        "adam_second": draw_adam_second(jax.random.fold_in(keys[27], 71), 0),
        "ema_in": bell_draw(keys[23], (FEAT, HID), FEAT ** -0.5, 0.5, ((0, 8),), jnp.float32),
        "ema_gat": bell_draw(keys[24], (2, 2, HID, HID), HID ** -0.5, 0.375, ((2, 8),), jnp.float32),
        "ema_out": bell_draw(keys[25], (HSIZE, CLASSES), HSIZE ** -0.5, 0.75, ((0, 8),), jnp.float32),
        "ema_small": bell_draw(keys[26], (SMALL,), 0.25, 1.0, (), jnp.float32),
    }


highest = lax.Precision.HIGHEST
leak_slope = 0.2
smooth = 0.1
clip_norm = 0.001
shampoo_rate = 0.3
shampoo_decay = 0.5
weight_decay = 0.0001
adam_rate = 0.1
beta_one = 0.9
beta_two = 0.999
adam_eps = 1e-08
adam_decay = 0.01
ema_keep = 0.9

@jax.custom_vjp
def low(v):
    return lax.optimization_barrier(v.astype(jnp.bfloat16)).astype(jnp.float32)

@jax.custom_vjp
def low_back(v):
    return v

def low_keep(v):
    return (low(v), None)

def low_pass(kept, grad):
    return (grad,)

def back_keep(v):
    return (v, None)

def back_low(kept, grad):
    return (low(grad),)
low.defvjp(low_keep, low_pass)
low_back.defvjp(back_keep, back_low)

def leaky_relu(values):
    return jnp.where(values > 0, values, leak_slope * values)

def attend(left_rows, right_rows, attention, sources_all):
    count_nodes = right_rows.shape[0]
    picked = left_rows[sources_all]
    mixed_rows = leaky_relu(picked + right_rows[:, None, :])
    heads_view = mixed_rows.reshape(count_nodes, -1, HEADS, HSIZE)
    scores = jnp.einsum('nkhd,hd->nkh', heads_view, attention, precision=highest)
    weights = jnp.exp(scores)
    weights = weights / lax.optimization_barrier(jnp.sum(weights, axis=1, keepdims=True))
    values = picked.reshape(count_nodes, -1, HEADS, HSIZE)
    result = jnp.einsum('nkh,nkhd->nhd', weights, values, precision=highest)
    return result.reshape(count_nodes, HEADS * HSIZE)

def split_small(small_params):
    bias_in = small_params[0:HID]
    attention = small_params[HID:3 * HID].reshape(2, HEADS, HSIZE)
    bias_one = small_params[3 * HID:4 * HID]
    bias_two = small_params[4 * HID:4 * HID + HSIZE]
    bias_out = small_params[4 * HID + HSIZE:]
    return (bias_in, attention, bias_one, bias_two, bias_out)

def gat_layer(hidden, halo_index, sources_all, weights, attention):
    halo_rows = low_back(hidden[halo_index])
    own_rows = hidden.reshape(N_DOM, NODE_DEV, -1)
    extended = jnp.concatenate([own_rows, halo_rows], axis=1)
    left_proj = low_back(low(jnp.einsum('pnf,fg->png', extended, weights[0], precision=highest)))
    right_proj = low_back(low(jnp.einsum('pnf,fg->png', own_rows, weights[1], precision=highest)))
    layer_out = jax.vmap(attend, in_axes=(0, 0, None, 0))(left_proj, right_proj, attention, sources_all)
    return layer_out.reshape(N_DOM * NODE_DEV, -1)

def model_loss(w_in, w_gat, w_out, small_params, feat_all, sources, send_index, labels, label_mask, label_count):
    bias_in, attention, bias_one, bias_two, bias_out = split_small(small_params)
    low_in = low(w_in)
    low_gat = low(w_gat)
    low_out = low(w_out)
    part_ids = jnp.arange(N_DOM, dtype=jnp.int32)
    self_index = jnp.broadcast_to(jnp.arange(NODE_DEV, dtype=jnp.int32)[None, :, None], (N_DOM, NODE_DEV, 1))
    loss_total = jnp.zeros((), jnp.float32)
    for micro_no in range(MICRO):
        send_rows = send_index[micro_no].reshape(N_DOM, 2 * HALF)
        from_left = jnp.roll(send_rows, 1, axis=0)[:, HALF:] + (jnp.roll(part_ids, 1) * NODE_DEV)[:, None]
        from_right = jnp.roll(send_rows, -1, axis=0)[:, :HALF] + (jnp.roll(part_ids, -1) * NODE_DEV)[:, None]
        halo_index = jnp.concatenate([from_left, from_right], axis=1).astype(jnp.int32)
        local_src = sources[micro_no].reshape(N_DOM, NODE_DEV, DEG)
        sources_all = jnp.concatenate([self_index, local_src], axis=2).astype(jnp.int32)
        pre_act = low_back(jnp.dot(feat_all[micro_no], low_in, precision=highest) + bias_in)
        hidden = low_back(low(jax.nn.elu(pre_act)))
        for layer_no in range(2):
            layer_out = gat_layer(hidden, halo_index, sources_all, low_gat[layer_no], attention[layer_no])
            if layer_no == 0:
                hidden = low_back(low(jax.nn.elu(layer_out + bias_one)))
            else:
                hidden = low_back(low(layer_out))
        head_view = hidden.reshape(-1, HEADS, HSIZE)
        pooled = low(lax.optimization_barrier(jnp.mean(head_view, axis=1)) + bias_two)
        logits = low_back(jnp.dot(pooled, low_out, precision=highest) + bias_out)
        log_prob = jax.nn.log_softmax(logits, axis=-1)
        picked = jnp.take_along_axis(log_prob, labels[micro_no][:, None], axis=1)[:, 0]
        per_node = -((1.0 - smooth) * picked + smooth / CLASSES * lax.optimization_barrier(jnp.sum(log_prob, axis=1)))
        loss_total = loss_total + jnp.sum(per_node * label_mask[micro_no].astype(jnp.float32))
    return loss_total / label_count

def precondition(gradient, weight_rows, stat_rows, stat_right, root_rows, root_right, start):
    count_rows = weight_rows.shape[-2]
    grad_rows = lax.dynamic_slice_in_dim(gradient, start, count_rows, gradient.ndim - 2)
    flipped = jnp.swapaxes(gradient, -1, -2)
    new_left = shampoo_decay * stat_rows + (1.0 - shampoo_decay) * jnp.matmul(grad_rows, flipped, precision=highest)
    new_right = shampoo_decay * stat_right + (1.0 - shampoo_decay) * jnp.matmul(flipped, gradient, precision=highest)
    update = jnp.matmul(root_rows, jnp.matmul(gradient, root_right, precision=highest), precision=highest)
    new_weight = weight_rows - shampoo_rate * (update + weight_decay * weight_rows)
    return (new_weight, new_left, new_right)

def adamw_step(parameter, gradient, moment_one, moment_two):
    moment_one = beta_one * moment_one + (1.0 - beta_one) * gradient
    moment_two = beta_two * moment_two + (1.0 - beta_two) * gradient * gradient
    corr_one = 1.0 - beta_one ** STEPS
    corr_two = 1.0 - beta_two ** STEPS
    update = moment_one / corr_one / (jnp.sqrt(moment_two / corr_two) + adam_eps)
    return (parameter - adam_rate * (update + adam_decay * parameter), moment_one, moment_two)

def average(old_value, new_value):
    return ema_keep * old_value + (1.0 - ema_keep) * new_value

def reference(features, sources, send_index, labels, label_mask, w_in, w_gat, w_out, small_params, stat_l_in, stat_r_in, stat_l_gat, stat_r_gat, stat_l_out, stat_r_out, root_l_in, root_r_in, root_l_gat, root_r_gat, root_l_out, root_r_out, adam_first, adam_second, ema_in, ema_gat, ema_out, ema_small):
    label_count = jnp.sum(label_mask.astype(jnp.float32))
    feat_all = features.astype(jnp.float32)

    def loss_of(weight_in, weight_gat, weight_out, small_now):
        return model_loss(weight_in, weight_gat, weight_out, small_now, feat_all, sources, send_index, labels, label_mask, label_count)
    mean_loss, pullback = jax.vjp(loss_of, w_in, w_gat, w_out, small_params)
    grad_in, grad_gat, grad_out, grad_small = pullback(jnp.ones((), jnp.float32))
    grad_norm = jnp.sqrt(jnp.sum(grad_in * grad_in) + jnp.sum(grad_gat * grad_gat) + jnp.sum(grad_out * grad_out) + jnp.sum(grad_small * grad_small))
    clip_scale = jnp.minimum(1.0, clip_norm / grad_norm)
    new_w_in, new_l_in, new_r_in = precondition(grad_in * clip_scale, w_in, stat_l_in, stat_r_in, root_l_in, root_r_in, 0)
    new_w_gat, new_l_gat, new_r_gat = precondition(grad_gat * clip_scale, w_gat, stat_l_gat, stat_r_gat, root_l_gat, root_r_gat, 0)
    new_w_out, new_l_out, new_r_out = precondition(grad_out * clip_scale, w_out, stat_l_out, stat_r_out, root_l_out, root_r_out, 0)
    new_small, new_first, new_second = adamw_step(small_params, grad_small * clip_scale, adam_first, adam_second)
    return (new_w_in, new_w_gat, new_w_out, new_small, new_l_in, new_r_in, new_l_gat, new_r_gat, new_l_out, new_r_out, new_first, new_second, average(ema_in, new_w_in), average(ema_gat, new_w_gat), average(ema_out, new_w_out), average(ema_small, new_small), mean_loss, grad_norm)
```

```python
import jax
import jax.numpy as jnp
from jax import lax
from jax.experimental import pallas as pl
from jax.experimental.pallas import tpu as pltpu
from jax.sharding import PartitionSpec as P

FEAT = 128
HEADS = 4
HSIZE = 64
CLASSES = 40
STEPS = 5
HID = 256
SMALL = 1128


highest = lax.Precision.HIGHEST
leak_slope = 0.2
smooth = 0.1
clip_norm = 0.001
shampoo_rate = 0.3
shampoo_decay = 0.5
weight_decay = 0.0001
adam_rate = 0.1
beta_one = 0.9
beta_two = 0.999
adam_eps = 1e-08
adam_decay = 0.01
ema_keep = 0.9


def split_small(small_params):
    bias_in = small_params[0:HID]
    attention = small_params[HID : 3 * HID].reshape(2, HEADS, HSIZE)
    bias_one = small_params[3 * HID : 4 * HID]
    bias_two = small_params[4 * HID : 4 * HID + HSIZE]
    bias_out = small_params[4 * HID + HSIZE :]
    return (bias_in, attention, bias_one, bias_two, bias_out)


GRAPH = 64
LANES = 128
DEG = 8
SLOTS = DEG + 1
ROWS = 1280
ROW_IN = 4 * HID
ROW_OUT = ROW_IN + FEAT
ROW_MISC = ROW_OUT + HSIZE

bf16 = jnp.bfloat16
f32 = jnp.float32


def dot_nn(a, b):
    return lax.dot_general(a, b, (((1,), (0,)), ((), ())), preferred_element_type=f32)


def dot_nt(a, b):
    return lax.dot_general(a, b, (((1,), (1,)), ((), ())), preferred_element_type=f32)


def tile_of(k):
    return slice(k * LANES, (k + 1) * LANES)


def head_of(h):
    return slice(h * HSIZE, (h + 1) * HSIZE)


def model_kernel(
    src_ref,
    lab_ref,
    msk_ref,
    feat_ref,
    wi_ref,
    wgt_ref,
    wg_ref,
    wot_ref,
    wo_ref,
    col_ref,
    am_ref,
    out_ref,
    e_ref,
    t_ref,
    al_ref,
    h_ref,
    slope_ref,
    xlr_ref,
    dx_ref,
    do_ref,
    pool_ref,
    dlog_ref,
    dt_ref,
    q_ref,
    ab_ref,
    da_ref,
    gb_ref,
    loss_ref,
):
    nodes = feat_ref.shape[0]
    blocks = nodes // LANES
    chunk = 4 * LANES
    chunks = nodes // chunk
    mixed = DEG * LANES

    row_id = lax.broadcasted_iota(jnp.int32, (LANES, LANES), 0)
    lane_id = lax.broadcasted_iota(jnp.int32, (LANES, LANES), 1)
    eye = jnp.where(row_id == lane_id, 1.0, 0.0).astype(bf16)
    head_row = lax.broadcasted_iota(jnp.int32, (16, HID), 0)
    head_col = lax.broadcasted_iota(jnp.int32, (16, HID), 1)
    head_mask = jnp.where(head_col // HSIZE == head_row, 1.0, 0.0).astype(bf16)

    bias_in = col_ref[:, 0:1]
    bias_one = col_ref[:, 1:2]
    bias_two = col_ref[0:HSIZE, 4:5]
    bias_out = col_ref[HSIZE : HSIZE + CLASSES, 4:5]
    for layer in range(2):
        wide = jnp.broadcast_to(col_ref[:, 2 + layer : 3 + layer], (HID, LANES))
        ab_ref[layer, 0] = wide.astype(bf16)
        ab_ref[layer, 1] = (leak_slope * wide).astype(bf16)
    da_ref[...] = jnp.zeros_like(da_ref)
    gb_ref[...] = jnp.zeros_like(gb_ref)
    loss_ref[...] = jnp.zeros_like(loss_ref)

    def lanes_of(i, width):
        return pl.ds(pl.multiple_of(i * width, width), width)

    @pl.loop(0, chunks)
    def _(c):
        at = lanes_of(c, chunk)
        pre = dot_nt(wi_ref[...], feat_ref[at, :]) + bias_in
        grown = jnp.exp(jnp.minimum(pre, 0.0))
        h_ref[0, :, at] = jnp.where(pre > 0, pre, grown - 1.0).astype(bf16)
        slope_ref[0, :, at] = jnp.where(pre > 0, 1.0, grown)

    for layer in range(2):

        @pl.loop(0, chunks)
        def _(c):
            at = lanes_of(c, chunk)
            xlr_ref[:, at] = dot_nn(wgt_ref[layer], h_ref[layer, :, at]).astype(bf16)

        @pl.loop(0, blocks)
        def _(i):
            at = lanes_of(i, LANES)
            if layer == 0:
                for k in range(DEG):
                    hit = row_id == src_ref[k : k + 1, at]
                    e_ref[i, 0:LANES, tile_of(k)] = jnp.where(hit, 1.0, 0.0).astype(bf16)
                    e_ref[i, LANES : 2 * LANES, tile_of(k)] = eye
            left = xlr_ref[0:HID, at]
            right = xlr_ref[HID : 2 * HID, at]
            both = jnp.concatenate([left, right], axis=1)
            t_ref[layer, i, :, 0:mixed] = dot_nn(both, e_ref[i]).astype(bf16)
            t_ref[layer, i, :, tile_of(DEG)] = left + right
            t = t_ref[layer, i]
            z = jnp.maximum(t, t * leak_slope)
            scores = dot_nn(am_ref[layer], z)
            grown = jnp.exp(scores[0:8] + scores[8:16])
            total = grown[:, tile_of(0)]
            for k in range(1, SLOTS):
                total = total + grown[:, tile_of(k)]
            inverse = 1.0 / total
            for k in range(SLOTS):
                al_ref[layer, i, :, tile_of(k)] = grown[:, tile_of(k)] * inverse
            pooled = None
            for h in range(HEADS):
                total = -right[head_of(h)].astype(f32).reshape(8, 8, LANES)
                for k in range(SLOTS):
                    part = jnp.broadcast_to(al_ref[layer, i, h : h + 1, tile_of(k)], (8, LANES))
                    value = t_ref[layer, i, head_of(h), tile_of(k)].astype(f32)
                    total = total + value.reshape(8, 8, LANES) * part[None]
                total = total.reshape(HSIZE, LANES)
                if layer == 0:
                    pre = total + bias_one[head_of(h)]
                    grown_one = jnp.exp(jnp.minimum(pre, 0.0))
                    h_ref[1, head_of(h), at] = jnp.where(pre > 0, pre, grown_one - 1.0).astype(bf16)
                    slope_ref[1, head_of(h), at] = jnp.where(pre > 0, 1.0, grown_one)
                else:
                    rounded = total.astype(bf16).astype(f32)
                    pooled = rounded if pooled is None else pooled + rounded
            if layer == 1:
                pool_ref[:, at] = (pooled * (1.0 / HEADS) + bias_two).astype(bf16)

    inv_count = col_ref[0:1, 5:6]

    @pl.loop(0, chunks)
    def _(c):
        at = lanes_of(c, chunk)
        logits = dot_nn(wot_ref[...], pool_ref[:, at]) + bias_out
        shifted = logits - jnp.max(logits, axis=0, keepdims=True)
        log_prob = shifted - jnp.log(jnp.sum(jnp.exp(shifted), axis=0, keepdims=True))
        class_id = lax.broadcasted_iota(jnp.int32, (CLASSES, chunk), 0)
        onehot = jnp.where(class_id == lab_ref[0:1, at], 1.0, 0.0)
        share = msk_ref[0:1, at].astype(f32) * inv_count
        term = jnp.sum(((smooth - 1.0) * onehot - smooth / CLASSES) * log_prob, axis=0, keepdims=True)
        loss_ref[...] += term * share
        d_logits = (jnp.exp(log_prob) - (1.0 - smooth) * onehot - smooth / CLASSES) * share
        d_logits = d_logits.astype(bf16)
        dlog_ref[:, at] = d_logits
        d_pooled = (dot_nn(wo_ref[...], d_logits) * (1.0 / HEADS)).astype(bf16)
        for h in range(HEADS):
            do_ref[head_of(h), at] = d_pooled

    for layer in (1, 0):

        @pl.loop(0, blocks)
        def _(i):
            at = lanes_of(i, LANES)
            d_out = do_ref[:, at]
            for k in range(SLOTS):
                q_ref[:, tile_of(k)] = t_ref[layer, i, :, tile_of(k)] * d_out
            d_alpha = dot_nn(head_mask, q_ref[...])[0:8]
            alpha = al_ref[layer, i]
            weighted = alpha * d_alpha
            total = weighted[:, tile_of(0)]
            for k in range(1, SLOTS):
                total = total + weighted[:, tile_of(k)]
            d_score = [
                weighted[:, tile_of(k)] - alpha[:, tile_of(k)] * total for k in range(SLOTS)
            ]
            for h in range(HEADS):
                d_head = d_out[head_of(h)].reshape(4, 16, LANES)
                slope_one = ab_ref[layer, 0, head_of(h)]
                slope_two = ab_ref[layer, 1, head_of(h)]
                for k in range(SLOTS):
                    ds = jnp.broadcast_to(d_score[k][h : h + 1], (16, LANES)).astype(bf16)
                    part = jnp.broadcast_to(alpha[h : h + 1, tile_of(k)], (16, LANES)).astype(bf16)
                    t = t_ref[layer, i, head_of(h), tile_of(k)]
                    slope = jnp.where(t > 0, slope_one, slope_two).reshape(4, 16, LANES)
                    dt_ref[head_of(h), tile_of(k)] = (slope * ds[None]).reshape(HSIZE, LANES)
                    q_ref[head_of(h), tile_of(k)] = (d_head * part[None]).reshape(HSIZE, LANES)
            t = t_ref[layer, i]
            z = jnp.maximum(t, t * leak_slope)
            ds_all = jnp.concatenate(d_score, axis=1)
            ds_all = jnp.concatenate([ds_all, jnp.zeros_like(ds_all)], axis=0).astype(bf16)
            da_ref[layer] += dot_nt(z, ds_all)
            spread = dot_nt(dt_ref[:, 0:mixed], e_ref[i])
            d_left = spread[:, 0:LANES] + dot_nt(q_ref[:, 0:mixed], e_ref[i, 0:LANES, :])
            self_dt = dt_ref[:, tile_of(DEG)].astype(f32)
            self_q = q_ref[:, tile_of(DEG)].astype(f32)
            dx_ref[layer, 0:HID, at] = (d_left + self_dt + self_q).astype(bf16)
            dx_ref[layer, HID : 2 * HID, at] = (spread[:, LANES : 2 * LANES] + self_dt).astype(bf16)

        @pl.loop(0, chunks)
        def _(c):
            at = lanes_of(c, chunk)
            d_in = dot_nn(wg_ref[layer], dx_ref[layer, :, at]).astype(bf16).astype(f32)
            d_in = d_in * slope_ref[layer, :, at]
            do_ref[:, at] = d_in.astype(bf16)
            if layer == 1:
                for k in range(4):
                    gb_ref[...] += d_in[:, tile_of(k)]

    for layer in range(2):
        for side in range(2):
            start = (2 * layer + side) * HID
            out_ref[start : start + HID, :] = dot_nt(
                h_ref[layer], dx_ref[layer, side * HID : (side + 1) * HID, :]
            ).astype(bf16)
    out_ref[ROW_IN : ROW_IN + FEAT, :] = dot_nn(do_ref[...], feat_ref[...]).T.astype(bf16)
    out_ref[ROW_OUT : ROW_OUT + HSIZE, :] = jnp.zeros((HSIZE, HID), bf16)
    out_ref[ROW_OUT : ROW_OUT + HSIZE, 0:CLASSES] = dot_nt(pool_ref[...], dlog_ref[...]).astype(bf16)
    ones = jnp.ones((nodes, LANES), bf16)
    lane_wide = lax.broadcasted_iota(jnp.int32, (HID, LANES), 1)
    columns = jnp.where(lane_wide == 0, dot_nn(do_ref[...], ones), 0.0)
    for layer in range(2):
        da = da_ref[layer]
        row_head = lax.broadcasted_iota(jnp.int32, (HID, 16), 0) // HSIZE
        lane_head = lax.broadcasted_iota(jnp.int32, (HID, 16), 1)
        da = jnp.sum(jnp.where(row_head == lane_head, da, 0.0), axis=1, keepdims=True)
        columns = columns + jnp.where(lane_wide == 1 + layer, da, 0.0)
    columns = columns + jnp.where(lane_wide == 3, jnp.sum(gb_ref[...], axis=1, keepdims=True), 0.0)
    g_bias_out = dot_nn(dlog_ref[...], ones)
    g_bias_two = lax.dot_general(
        wo_ref[...].astype(f32), g_bias_out, (((1,), (0,)), ((), ())),
        precision=highest, preferred_element_type=f32,
    )
    loss = jnp.broadcast_to(jnp.sum(loss_ref[...], axis=1, keepdims=True), (8, LANES))
    loss_high = loss.astype(bf16).astype(f32)
    rest = HID - HSIZE - CLASSES - 16
    last = jnp.concatenate(
        [g_bias_two, g_bias_out, loss_high, loss - loss_high, jnp.zeros((rest, LANES), f32)], axis=0
    )
    columns = columns + jnp.where(lane_wide == 4, last, 0.0)
    out_ref[ROW_MISC : ROW_MISC + 16, :] = columns.T[0:16].astype(bf16)
    out_ref[ROW_MISC + 16 :, :] = jnp.zeros((ROWS - ROW_MISC - 16, HID), bf16)


def run_model(src, lab, msk, feat, w_in, w_gat, w_out, small_params, inv_count):
    nodes = feat.shape[0]
    blocks = nodes // LANES
    bias_in, attention, bias_one, bias_two, bias_out = split_small(small_params)
    flat = attention.reshape(2, HID)
    last = jnp.concatenate([bias_two, bias_out, jnp.zeros((HID - HSIZE - CLASSES,), f32)])
    count_col = jnp.full((HID,), inv_count, f32)
    col = jnp.stack([bias_in, bias_one, flat[0], flat[1], last, count_col, last, last], axis=1)
    head_row = jnp.arange(8, dtype=jnp.int32)[:, None]
    head_mask = (jnp.arange(HID, dtype=jnp.int32)[None, :] // HSIZE == head_row).astype(f32)
    high = flat.astype(bf16).astype(f32)
    both = jnp.concatenate([head_mask * high[:, None, :], head_mask * (flat - high)[:, None, :]], axis=1)
    am = both.astype(bf16)
    wgt = jnp.swapaxes(w_gat, -1, -2).reshape(2, 2 * HID, HID)
    wg = jnp.swapaxes(w_gat, 1, 2).reshape(2, HID, 2 * HID)
    scratch = [
        pltpu.VMEM((blocks, 2 * LANES, DEG * LANES), bf16),
        pltpu.VMEM((2, blocks, HID, SLOTS * LANES), bf16),
        pltpu.VMEM((2, blocks, 8, SLOTS * LANES), f32),
        pltpu.VMEM((2, HID, nodes), bf16),
        pltpu.VMEM((2, HID, nodes), f32),
        pltpu.VMEM((2 * HID, nodes), bf16),
        pltpu.VMEM((2, 2 * HID, nodes), bf16),
        pltpu.VMEM((HID, nodes), bf16),
        pltpu.VMEM((HSIZE, nodes), bf16),
        pltpu.VMEM((CLASSES, nodes), bf16),
        pltpu.VMEM((HID, SLOTS * LANES), bf16),
        pltpu.VMEM((HID, SLOTS * LANES), bf16),
        pltpu.VMEM((2, 2, HID, LANES), bf16),
        pltpu.VMEM((2, HID, 16), f32),
        pltpu.VMEM((HID, LANES), f32),
        pltpu.VMEM((1, 4 * LANES), f32),
    ]
    return pl.pallas_call(
        model_kernel,
        out_shape=jax.ShapeDtypeStruct((ROWS, HID), bf16),
        in_specs=[pl.BlockSpec(memory_space=pltpu.VMEM)] * 11,
        out_specs=pl.BlockSpec(memory_space=pltpu.VMEM),
        scratch_shapes=scratch,
        compiler_params=pltpu.CompilerParams(vmem_limit_bytes=56 * 1024 * 1024),
        name="model",
    )(src, lab, msk, feat, w_in.T, wgt, wg, w_out.T, w_out, col, am)


def precondition(gradient, weight_rows, stat_rows, stat_right, root_rows, root_right, start):
    count_rows = weight_rows.shape[-2]
    grad_rows = lax.dynamic_slice_in_dim(gradient, start, count_rows, gradient.ndim - 2)
    flipped = jnp.swapaxes(gradient, -1, -2)
    new_left = shampoo_decay * stat_rows + (1.0 - shampoo_decay) * jnp.matmul(
        grad_rows, flipped, precision=highest
    )
    new_right = shampoo_decay * stat_right + (1.0 - shampoo_decay) * jnp.matmul(
        flipped, gradient, precision=highest
    )
    update = jnp.matmul(
        root_rows, jnp.matmul(gradient, root_right, precision=highest), precision=highest
    )
    new_weight = weight_rows - shampoo_rate * (update + weight_decay * weight_rows)
    return (new_weight, new_left, new_right)


def adamw_step(parameter, gradient, moment_one, moment_two):
    moment_one = beta_one * moment_one + (1.0 - beta_one) * gradient
    moment_two = beta_two * moment_two + (1.0 - beta_two) * gradient * gradient
    corr_one = 1.0 - beta_one**STEPS
    corr_two = 1.0 - beta_two**STEPS
    update = moment_one / corr_one / (jnp.sqrt(moment_two / corr_two) + adam_eps)
    return (parameter - adam_rate * (update + adam_decay * parameter), moment_one, moment_two)


def average(old_value, new_value):
    return ema_keep * old_value + (1.0 - ema_keep) * new_value


def per_device(
    features,
    sources,
    send_index,
    labels,
    label_mask,
    w_in,
    w_gat,
    w_out,
    small_params,
    stat_l_in,
    stat_r_in,
    stat_l_gat,
    stat_r_gat,
    stat_l_out,
    stat_r_out,
    root_l_in,
    root_r_in,
    root_l_gat,
    root_r_gat,
    root_l_out,
    root_r_out,
    adam_first,
    adam_second,
    ema_in,
    ema_gat,
    ema_out,
    ema_small,
):
    dom_size = lax.axis_size("dom")
    all_size = dom_size * lax.axis_size("section")
    dom_id = lax.axis_index("dom")
    section_id = lax.axis_index("section")
    nodes = features.shape[1]
    half = send_index.shape[1] // 2
    rows_in, rows_gat, rows_out = (w_in.shape[0], w_gat.shape[2], w_out.shape[0])

    def of_micro(value):
        return lax.dynamic_index_in_dim(value, section_id, 0, keepdims=False)

    feat, src, send = (of_micro(features), of_micro(sources).T, of_micro(send_index))
    marks = jnp.stack([of_micro(labels), of_micro(label_mask)])
    down = [((i + 1) % dom_size, i) for i in range(dom_size)]
    feat_next = lax.ppermute(feat[:half], "dom", down)
    ints = jnp.concatenate([src[:, :half], marks[:, :half], send[None, :half]], axis=0)
    ints_next = lax.ppermute(ints, "dom", down)

    count = jnp.sum(label_mask)
    digits = jnp.stack([lax.div(count, 256), lax.rem(count, 256)]).astype(bf16)
    packed = jnp.concatenate(
        [
            w_in.astype(bf16),
            w_gat.astype(bf16).reshape(4 * rows_gat, HID),
            jnp.pad(w_out.astype(bf16), ((0, 0), (0, HID - CLASSES))),
            jnp.pad(digits[None, :], ((0, 0), (0, HID - 2))),
        ],
        axis=0,
    )
    whole = lax.all_gather(packed, "dom", axis=0, tiled=False)
    full_in = whole[:, :rows_in].reshape(FEAT, HID)
    cut = rows_in + 4 * rows_gat
    full_gat = whole[:, rows_in:cut].reshape(dom_size, 2, 2, rows_gat, HID)
    full_gat = full_gat.transpose(1, 2, 0, 3, 4).reshape(2, 2, HID, HID)
    full_out = whole[:, cut : cut + rows_out, :CLASSES].reshape(HSIZE, CLASSES)
    digits = jnp.sum(whole[:, cut + rows_out, :2].astype(f32), axis=0)
    label_count = digits[0] * 256.0 + digits[1]

    feat = jnp.concatenate([feat[half:], feat_next], axis=0)
    src = jnp.concatenate([src[:, half:], ints_next[:DEG]], axis=1)
    marks = jnp.concatenate([marks[:, half:], ints_next[DEG : DEG + 2]], axis=1)
    table = jnp.concatenate([send[half:] - (nodes - half), half + ints_next[DEG + 2]])
    edge = src[:, nodes - GRAPH :]
    spots = jnp.arange(2 * half, dtype=jnp.int32)[None, :, None] + nodes
    looked = jnp.sum(jnp.where(edge[:, None, :] == spots, table[None, :, None], 0), axis=1)
    edge = jnp.where(edge >= nodes, looked, (edge - half) % GRAPH)
    src = jnp.concatenate([(src[:, : nodes - GRAPH] - half) % GRAPH, edge], axis=1)
    lane = jnp.arange(nodes, dtype=jnp.int32)[None, :]
    src = src + (lane // GRAPH) % 2 * GRAPH

    partial = run_model(
        src, marks[0:1], marks[1:2], feat, full_in, full_gat, full_out, small_params, 1.0 / label_count
    )
    parts = lax.all_to_all(partial.reshape(all_size, -1, HID), ("section", "dom"), 0, 0)
    mine = jnp.sum(parts.astype(f32), axis=0)
    shared = jnp.broadcast_to(mine.astype(bf16)[None], (all_size,) + mine.shape)
    summed = lax.all_to_all(shared, ("section", "dom"), 0, 0).reshape(ROWS, HID).astype(f32)

    grad_gat = summed[:ROW_IN].reshape(2, 2, HID, HID)
    grad_in = summed[ROW_IN:ROW_OUT]
    grad_out = summed[ROW_OUT:ROW_MISC, :CLASSES]
    misc = summed[ROW_MISC : ROW_MISC + 8]
    grad_small = jnp.concatenate([misc[:4].reshape(-1), misc[4, : HSIZE + CLASSES]])
    spot = HSIZE + CLASSES
    mean_loss = misc[4, spot] + misc[4, spot + 8]
    grad_norm = jnp.sqrt(
        jnp.sum(grad_in * grad_in)
        + jnp.sum(grad_gat * grad_gat)
        + jnp.sum(grad_out * grad_out)
        + jnp.sum(grad_small * grad_small)
    )
    clip_scale = jnp.minimum(1.0, clip_norm / grad_norm)
    new_w_in, new_l_in, new_r_in = precondition(
        grad_in * clip_scale,
        w_in,
        stat_l_in,
        stat_r_in,
        root_l_in,
        root_r_in,
        dom_id * w_in.shape[0],
    )
    new_w_gat, new_l_gat, new_r_gat = precondition(
        grad_gat * clip_scale,
        w_gat,
        stat_l_gat,
        stat_r_gat,
        root_l_gat,
        root_r_gat,
        dom_id * w_gat.shape[2],
    )
    new_w_out, new_l_out, new_r_out = precondition(
        grad_out * clip_scale,
        w_out,
        stat_l_out,
        stat_r_out,
        root_l_out,
        root_r_out,
        dom_id * w_out.shape[0],
    )
    new_small, new_first, new_second = adamw_step(
        small_params, grad_small * clip_scale, adam_first, adam_second
    )
    return (
        new_w_in,
        new_w_gat,
        new_w_out,
        new_small,
        new_l_in,
        new_r_in,
        new_l_gat,
        new_r_gat,
        new_l_out,
        new_r_out,
        new_first,
        new_second,
        average(ema_in, new_w_in),
        average(ema_gat, new_w_gat),
        average(ema_out, new_w_out),
        average(ema_small, new_small),
        mean_loss,
        grad_norm,
    )


def solution(mesh):
    placed = (
        P(None, "dom", None),
        P(None, "dom", None),
        P(None, "dom"),
        P(None, "dom"),
        P(None, "dom"),
        P("dom", None),
        P(None, None, "dom", None),
        P("dom", None),
        P(),
        P("dom", None),
        P(),
        P(None, None, "dom", None),
        P(),
        P("dom", None),
        P(),
        P("dom", None),
        P(),
        P(None, None, "dom", None),
        P(),
        P("dom", None),
        P(),
        P(),
        P(),
        P("dom", None),
        P(None, None, "dom", None),
        P("dom", None),
        P(),
    )
    return jax.shard_map(
        per_device,
        mesh=mesh,
        in_specs=placed,
        out_specs=(
            P("dom", None),
            P(None, None, "dom", None),
            P("dom", None),
            P(),
            P("dom", None),
            P(),
            P(None, None, "dom", None),
            P(),
            P("dom", None),
            P(),
            P(),
            P(),
            P("dom", None),
            P(None, None, "dom", None),
            P("dom", None),
            P(),
            P(),
            P(),
        ),
        check_vma=False,
    )
```

```python
import jax
import jax.numpy as jnp
from jax import lax
from jax.experimental import pallas as pl
from jax.experimental.pallas import tpu as pltpu
from jax.sharding import PartitionSpec as P

FEAT = 128
HEADS = 4
HSIZE = 64
CLASSES = 40
STEPS = 5
HID = 256
SMALL = 1128


highest = lax.Precision.HIGHEST
leak_slope = 0.2
smooth = 0.1
clip_norm = 0.001
shampoo_rate = 0.3
shampoo_decay = 0.5
weight_decay = 0.0001
adam_rate = 0.1
beta_one = 0.9
beta_two = 0.999
adam_eps = 1e-08
adam_decay = 0.01
ema_keep = 0.9


def split_small(small_params):
    bias_in = small_params[0:HID]
    attention = small_params[HID : 3 * HID].reshape(2, HEADS, HSIZE)
    bias_one = small_params[3 * HID : 4 * HID]
    bias_two = small_params[4 * HID : 4 * HID + HSIZE]
    bias_out = small_params[4 * HID + HSIZE :]
    return (bias_in, attention, bias_one, bias_two, bias_out)


GRAPH = 64
LANES = 128
DEG = 8
SLOTS = DEG + 1
ROWS = 1280
GROUPS = 8
IN_G = FEAT // GROUPS
GAT_G = HID // GROUPS
OUT_G = HSIZE // GROUPS
TAIL_G = IN_G + 4 * GAT_G
PACK_G = TAIL_G + 2 * OUT_G
HALF = GRAPH // 2
ROW_IN = 4 * HID
ROW_OUT = ROW_IN + FEAT
ROW_MISC = ROW_OUT + HSIZE

bf16 = jnp.bfloat16
f32 = jnp.float32


def dot_nn(a, b):
    return lax.dot_general(a, b, (((1,), (0,)), ((), ())), preferred_element_type=f32)


def dot_nt(a, b):
    return lax.dot_general(a, b, (((1,), (1,)), ((), ())), preferred_element_type=f32)


def tile_of(k):
    return slice(k * LANES, (k + 1) * LANES)


def head_of(h):
    return slice(h * HSIZE, (h + 1) * HSIZE)


def row_of(ref, micro, width):
    picked = ref[0:1, 0:width]
    for other in range(1, ref.shape[0]):
        picked = jnp.where(micro == other, ref[other : other + 1, 0:width], picked)
    return picked


def pack_kernel(
    micro_ref,
    feat_ref,
    src_ref,
    lab_ref,
    msk_ref,
    send_ref,
    win_ref,
    wgat_ref,
    wout_ref,
    pack_ref,
    ints_ref,
    first_ref,
    tail_ref,
):
    micro = micro_ref[0]
    first_ref[...] = feat_ref[0]
    ints_ref[...] = jnp.zeros_like(ints_ref)
    shift = LANES - HALF
    ints_ref[0:DEG, :] = pltpu.roll(src_ref[0], shift, 1)
    ints_ref[DEG : DEG + 1, :] = pltpu.roll(row_of(lab_ref, micro, LANES), shift, 1)
    ints_ref[DEG + 1 : DEG + 2, :] = pltpu.roll(row_of(msk_ref, micro, LANES), shift, 1)
    send = row_of(send_ref, micro, 2 * HALF)
    ints_ref[DEG + 2 : DEG + 3, :] = jnp.concatenate([send, send], axis=1)
    if win_ref.shape[0] != IN_G:
        pack_ref[...] = jnp.zeros_like(pack_ref)
        return
    pack_ref[0:IN_G, :] = win_ref[...].astype(bf16)
    for layer in range(2):
        for side in range(2):
            start = IN_G + (2 * layer + side) * GAT_G
            pack_ref[start : start + GAT_G, :] = wgat_ref[layer, side].astype(bf16)
    tail_ref[...] = jnp.zeros_like(tail_ref)
    tail_ref[0:OUT_G, 0:CLASSES] = wout_ref[...]
    count = jnp.sum(jnp.sum(msk_ref[...].astype(f32), axis=1, keepdims=True), axis=0, keepdims=True)
    high = jnp.floor(count * (1.0 / 256.0))
    lane = lax.broadcasted_iota(jnp.int32, (1, HID), 1)
    low = jnp.where(lane == 1, count - 256.0 * high, 0.0)
    tail_ref[OUT_G : OUT_G + 1, :] = jnp.where(lane == 0, high, low)
    pack_ref[TAIL_G:PACK_G, :] = tail_ref[...].astype(bf16)


def vmem(count):
    return [pl.BlockSpec(memory_space=pltpu.VMEM)] * count


def pack_inputs(micro, features, src_all, labels, label_mask, send_index, w_in, w_gat, w_out):
    grid_spec = pltpu.PrefetchScalarGridSpec(
        num_scalar_prefetch=1,
        grid=(1,),
        in_specs=[
            pl.BlockSpec((1, HALF, FEAT), lambda i, m: (m[0], 0, 0)),
            pl.BlockSpec((1, DEG, LANES), lambda i, m: (m[0], 0, 0)),
        ]
        + vmem(6),
        out_specs=vmem(3),
        scratch_shapes=[pltpu.VMEM((2 * OUT_G, HID), f32)],
    )
    return pl.pallas_call(
        pack_kernel,
        grid_spec=grid_spec,
        out_shape=(
            jax.ShapeDtypeStruct((PACK_G, HID), bf16),
            jax.ShapeDtypeStruct((16, LANES), jnp.int32),
            jax.ShapeDtypeStruct((HALF, FEAT), bf16),
        ),
        compiler_params=pltpu.CompilerParams(vmem_limit_bytes=60 * 1024 * 1024),
        name="pack",
    )(micro, features, src_all, labels, label_mask, send_index, w_in, w_gat, w_out)


def gather_weights(packed, w_in, w_gat, w_out, label_mask):
    size = lax.axis_size("dom")
    if size == GROUPS:
        return lax.all_gather(packed, "dom", axis=0, tiled=False)
    rows_in, rows_gat, rows_out = (w_in.shape[0], w_gat.shape[2], w_out.shape[0])
    count = jnp.sum(label_mask)
    digits = jnp.stack([lax.div(count, 256), lax.rem(count, 256)]).astype(bf16)
    packed = jnp.concatenate(
        [
            w_in.astype(bf16),
            w_gat.astype(bf16).reshape(4 * rows_gat, HID),
            jnp.pad(w_out.astype(bf16), ((0, 0), (0, HID - CLASSES))),
            jnp.pad(digits[None, :], ((0, 0), (0, HID - 2))),
        ],
        axis=0,
    )
    whole = lax.all_gather(packed, "dom", axis=0, tiled=False)
    cut = rows_in + 4 * rows_gat
    part_in = whole[:, :rows_in].reshape(GROUPS, IN_G, HID)
    part_gat = whole[:, rows_in:cut].reshape(GROUPS, size // GROUPS, 4, rows_gat, HID)
    part_gat = part_gat.transpose(0, 2, 1, 3, 4).reshape(GROUPS, 4 * GAT_G, HID)
    part_out = whole[:, cut : cut + rows_out].reshape(GROUPS, OUT_G, HID)
    counts = whole[:, cut + rows_out].reshape(GROUPS, size // GROUPS, HID)
    counts = jnp.pad(counts, ((0, 0), (0, OUT_G - size // GROUPS), (0, 0)))
    return jnp.concatenate([part_in, part_gat, part_out, counts], axis=1)


def column_of(row):
    return jnp.broadcast_to(row.reshape(1, -1), (LANES, row.shape[0])).T


def model_kernel(
    micro_ref,
    feat_ref,
    src_ref,
    lab_ref,
    msk_ref,
    send_ref,
    whole_ref,
    ints_ref,
    next_ref,
    small_ref,
    out_ref,
    e_ref,
    t_ref,
    al_ref,
    att_ref,
    h_ref,
    slope_ref,
    xlr_ref,
    dx_ref,
    do_ref,
    pool_ref,
    dlog_ref,
    w_ref,
    sum_ref,
    a_ref,
    da_ref,
    gb_ref,
    loss_ref,
    node_ref,
    edge_ref,
    mark_ref,
    wi_ref,
    wgt_ref,
    wg_ref,
    wo_ref,
    wof_ref,
    am_ref,
):
    nodes = feat_ref.shape[1]
    blocks = nodes // LANES
    chunk = 4 * LANES
    chunks = nodes // chunk
    mixed = DEG * LANES
    micro = micro_ref[0]
    final = nodes - LANES

    node_ref[0 : nodes - HALF, :] = feat_ref[0, HALF:nodes, :]
    node_ref[nodes - HALF : nodes, :] = next_ref[...]
    lane_row = lax.broadcasted_iota(jnp.int32, (1, LANES), 1)
    kept = lane_row < LANES - HALF
    edge_ref[...] = pltpu.roll(src_ref[0], nodes - HALF, 1)
    edge_ref[:, final:nodes] = jnp.where(kept, edge_ref[:, final:nodes], ints_ref[0:DEG, :])
    for place, ref in enumerate((lab_ref, msk_ref)):
        mark_ref[place : place + 1, :] = pltpu.roll(row_of(ref, micro, nodes), nodes - HALF, 1)
        came = ints_ref[DEG + place : DEG + place + 1, :]
        mark_ref[place : place + 1, final:nodes] = jnp.where(kept, mark_ref[place : place + 1, final:nodes], came)
    send = row_of(send_ref, micro, 2 * HALF)
    send = jnp.concatenate([send, send], axis=1)
    arrived = pltpu.roll(ints_ref[DEG + 2 : DEG + 3, :], HALF, 1)
    table = jnp.where(
        lane_row < HALF, pltpu.roll(send, HALF, 1) - (nodes - HALF), arrived + HALF
    )
    spot_row = lax.broadcasted_iota(jnp.int32, (GRAPH, LANES), 0)
    spot_lane = lax.broadcasted_iota(jnp.int32, (GRAPH, LANES), 1)
    table = jnp.sum(jnp.where(spot_row == spot_lane, table.astype(f32), 0.0), axis=1, keepdims=True)
    looked = []
    for k in range(DEG):
        far = edge_ref[k : k + 1, final:nodes] - nodes == spot_row
        looked.append(jnp.sum(jnp.where(far, table, 0.0), axis=0, keepdims=True))
    looked = jnp.concatenate(looked, axis=0).astype(jnp.int32)
    raw = edge_ref[:, final:nodes]
    looked = jnp.where(raw >= nodes, looked, jnp.bitwise_and(raw - HALF, GRAPH - 1))
    local = jnp.bitwise_and(edge_ref[...] - HALF, GRAPH - 1)
    lane_all = lax.broadcasted_iota(jnp.int32, (DEG, nodes), 1)
    second = jnp.bitwise_and(lane_all, GRAPH)
    edge_ref[...] = local + second
    edge_ref[:, final:nodes] = looked + jnp.bitwise_and(
        lax.broadcasted_iota(jnp.int32, (DEG, LANES), 1), GRAPH
    )

    digits = jnp.zeros((OUT_G, HID), f32)
    for g in range(GROUPS):
        wi_ref[g * IN_G : (g + 1) * IN_G, :] = whole_ref[g, 0:IN_G, :]
        for layer in range(2):
            for side in range(2):
                start = IN_G + (2 * layer + side) * GAT_G
                wg_ref[layer, g * GAT_G : (g + 1) * GAT_G, side * HID : (side + 1) * HID] = whole_ref[
                    g, start : start + GAT_G, :
                ]
        tail = whole_ref[g, TAIL_G:PACK_G, :].astype(f32)
        wof_ref[g * OUT_G : (g + 1) * OUT_G, :] = tail[0:OUT_G]
        digits = digits + tail[OUT_G : 2 * OUT_G]
    for layer in range(2):
        for side in range(2):
            wgt_ref[layer, side * HID : (side + 1) * HID, :] = wg_ref[
                layer, :, side * HID : (side + 1) * HID
            ].T
    wi_t = wi_ref[...].T
    wo_ref[...] = wof_ref[:, 0:CLASSES].astype(bf16)
    wo_t = wof_ref[...].T[0:CLASSES].astype(bf16)
    digits = jnp.sum(digits, axis=0, keepdims=True)
    inv_count = 1.0 / (digits[:, 0:1] * 256.0 + digits[:, 1:2])

    row_id = lax.broadcasted_iota(jnp.int32, (LANES, LANES), 0)
    lane_id = lax.broadcasted_iota(jnp.int32, (LANES, LANES), 1)
    eye = jnp.where(row_id == lane_id, 1.0, 0.0).astype(bf16)
    head_row = lax.broadcasted_iota(jnp.int32, (16, HID), 0)
    head_col = lax.broadcasted_iota(jnp.int32, (16, HID), 1)
    head_mask = jnp.where(head_col // HSIZE == head_row, 1.0, 0.0)

    bias_in = column_of(small_ref[0:HID])[:, 0:1]
    bias_one = column_of(small_ref[3 * HID : 4 * HID])[:, 0:1]
    bias_two = column_of(small_ref[4 * HID : 4 * HID + HSIZE])[:, 0:1]
    bias_out = column_of(small_ref[4 * HID + HSIZE : SMALL])[:, 0:1]
    for layer in range(2):
        row = small_ref[(1 + layer) * HID : (2 + layer) * HID]
        a_ref[layer] = column_of(row)
        row = row.reshape(1, HID)
        high = row.astype(bf16).astype(f32)
        am_ref[layer] = jnp.concatenate([head_mask[0:8] * high, head_mask[0:8] * (row - high)], axis=0).astype(bf16)
    fold_row = lax.broadcasted_iota(jnp.int32, (16, HEADS * 16), 0)
    fold_col = lax.broadcasted_iota(jnp.int32, (16, HEADS * 16), 1)
    fold = jnp.where(fold_col // 16 == fold_row, 1.0, 0.0).astype(bf16)
    spots = lax.broadcasted_iota(jnp.int32, (GRAPH, LANES), 0).astype(f32).astype(bf16)
    spots = spots.reshape(4, 16, LANES)
    half_lane = lax.broadcasted_iota(jnp.int32, (16, LANES), 1)
    first_half = (half_lane < GRAPH).astype(f32).astype(bf16)[None] > 0
    own_spot = jnp.bitwise_and(half_lane, GRAPH - 1).astype(f32).astype(bf16)
    zero = jnp.zeros((4, 16, LANES), bf16)
    da_ref[...] = jnp.zeros_like(da_ref)
    gb_ref[...] = jnp.zeros_like(gb_ref)
    loss_ref[...] = jnp.zeros_like(loss_ref)

    def lanes_of(i, width):
        return pl.ds(pl.multiple_of(i * width, width), width)

    @pl.loop(0, chunks)
    def _(c):
        at = lanes_of(c, chunk)
        pre = dot_nt(wi_t, node_ref[at, :]) + bias_in
        grown = jnp.exp(jnp.minimum(pre, 0.0))
        h_ref[0, :, at] = jnp.where(pre > 0, pre, grown - 1.0).astype(bf16)
        slope_ref[0, :, at] = jnp.where(pre > 0, 1.0, grown)

    for layer in range(2):

        @pl.loop(0, chunks)
        def _(c):
            at = lanes_of(c, chunk)
            xlr_ref[layer, :, at] = dot_nn(wgt_ref[layer], h_ref[layer, :, at]).astype(bf16)

        @pl.loop(0, blocks, unroll=4)
        def _(i):
            at = lanes_of(i, LANES)
            if layer == 0:
                for k in range(DEG):
                    hit = row_id == edge_ref[k : k + 1, at]
                    e_ref[i, 0:LANES, tile_of(k)] = jnp.where(hit, 1.0, 0.0).astype(bf16)
                    e_ref[i, LANES : 2 * LANES, tile_of(k)] = eye
            left = xlr_ref[layer, 0:HID, at]
            right = xlr_ref[layer, HID : 2 * HID, at]
            both = jnp.concatenate([left, right], axis=1)
            t_ref[layer, i, :, 0:mixed] = dot_nn(both, e_ref[i]).astype(bf16)
            t_ref[layer, i, :, tile_of(DEG)] = left + right
            t = t_ref[layer, i]
            z = jnp.maximum(t, t * leak_slope)
            scores = dot_nn(am_ref[layer], z)
            grown = jnp.exp(scores[0:8] + scores[8:16])
            total = grown[:, tile_of(0)]
            for k in range(1, SLOTS):
                total = total + grown[:, tile_of(k)]
            inverse = 1.0 / total
            grids = [zero] * HEADS
            for k in range(SLOTS):
                alpha = grown[:, tile_of(k)] * inverse
                al_ref[layer, i, :, tile_of(k)] = alpha
                if k == DEG:
                    spot = own_spot
                else:
                    spot = jnp.bitwise_and(edge_ref[k : k + 1, at], GRAPH - 1).astype(f32)
                    spot = jnp.broadcast_to(spot, (16, LANES)).astype(bf16)
                hit = spots == spot[None]
                for h in range(HEADS):
                    part = jnp.broadcast_to(alpha[h : h + 1], (16, LANES)).astype(bf16)
                    grids[h] = grids[h] + jnp.where(hit, part[None], zero)
            pooled = None
            for h in range(HEADS):
                upper = jnp.where(first_half, grids[h], zero).reshape(GRAPH, LANES)
                lower = jnp.where(first_half, zero, grids[h]).reshape(GRAPH, LANES)
                grid = jnp.concatenate([upper, lower], axis=0)
                att_ref[layer, i, h] = grid
                total = dot_nn(left[head_of(h)], grid)
                if layer == 0:
                    pre = total + bias_one[head_of(h)]
                    grown_one = jnp.exp(jnp.minimum(pre, 0.0))
                    h_ref[1, head_of(h), at] = jnp.where(pre > 0, pre, grown_one - 1.0).astype(bf16)
                    slope_ref[1, head_of(h), at] = jnp.where(pre > 0, 1.0, grown_one)
                else:
                    rounded = total.astype(bf16).astype(f32)
                    pooled = rounded if pooled is None else pooled + rounded
            if layer == 1:
                pool_ref[:, at] = (pooled * (1.0 / HEADS) + bias_two).astype(bf16)

    @pl.loop(0, chunks)
    def _(c):
        at = lanes_of(c, chunk)
        logits = dot_nn(wo_t, pool_ref[:, at]) + bias_out
        shifted = logits - jnp.max(logits, axis=0, keepdims=True)
        log_prob = shifted - jnp.log(jnp.sum(jnp.exp(shifted), axis=0, keepdims=True))
        class_id = lax.broadcasted_iota(jnp.int32, (CLASSES, chunk), 0)
        onehot = jnp.where(class_id == mark_ref[0:1, at], 1.0, 0.0)
        share = mark_ref[1:2, at].astype(f32) * inv_count
        term = jnp.sum(((smooth - 1.0) * onehot - smooth / CLASSES) * log_prob, axis=0, keepdims=True)
        loss_ref[...] += term * share
        d_logits = (jnp.exp(log_prob) - (1.0 - smooth) * onehot - smooth / CLASSES) * share
        d_logits = d_logits.astype(bf16)
        dlog_ref[:, at] = d_logits
        d_pooled = (dot_nn(wo_ref[...], d_logits) * (1.0 / HEADS)).astype(bf16)
        for h in range(HEADS):
            do_ref[head_of(h), at] = d_pooled

    for layer in (1, 0):

        @pl.loop(0, blocks, unroll=4)
        def _(i):
            at = lanes_of(i, LANES)
            d_out = do_ref[:, at]
            for h in range(HEADS):
                d_head = d_out[head_of(h)].reshape(4, 16, LANES)
                for k in range(SLOTS):
                    product = t_ref[layer, i, head_of(h), tile_of(k)].reshape(4, 16, LANES) * d_head
                    sum_ref[h * 16 : (h + 1) * 16, tile_of(k)] = (product[0] + product[1]) + (product[2] + product[3])
            d_alpha = dot_nn(fold, sum_ref[...])[0:8]
            alpha = al_ref[layer, i]
            weighted = alpha * d_alpha
            total = weighted[:, tile_of(0)]
            for k in range(1, SLOTS):
                total = total + weighted[:, tile_of(k)]
            for k in range(SLOTS):
                d_score = weighted[:, tile_of(k)] - alpha[:, tile_of(k)] * total
                for h in range(HEADS):
                    one = jnp.broadcast_to(d_score[h : h + 1], (16, LANES))
                    two = (one * leak_slope).astype(bf16)[None]
                    one = one.astype(bf16)[None]
                    t = t_ref[layer, i, head_of(h), tile_of(k)].reshape(4, 16, LANES)
                    w_ref[head_of(h), tile_of(k)] = jnp.where(t > 0, one, two).reshape(HSIZE, LANES)
            spread = dot_nt(w_ref[:, 0:mixed], e_ref[i])
            own = w_ref[:, tile_of(DEG)].astype(f32)
            left_w = spread[:, 0:LANES] + own
            right_w = spread[:, LANES : 2 * LANES] + own
            left = xlr_ref[layer, 0:HID, at].astype(f32)
            right = xlr_ref[layer, HID : 2 * HID, at].astype(f32)
            da_ref[layer] += left * left_w + right * right_w
            wide = a_ref[layer]
            for h in range(HEADS):
                passed = dot_nt(d_out[head_of(h)], att_ref[layer, i, h])
                d_left = wide[head_of(h)] * left_w[head_of(h)] + passed
                dx_ref[layer, head_of(h), at] = d_left.astype(bf16)
            dx_ref[layer, HID : 2 * HID, at] = (wide * right_w).astype(bf16)

        @pl.loop(0, chunks)
        def _(c):
            at = lanes_of(c, chunk)
            d_in = dot_nn(wg_ref[layer], dx_ref[layer, :, at]).astype(bf16).astype(f32)
            d_in = d_in * slope_ref[layer, :, at]
            do_ref[:, at] = d_in.astype(bf16)
            if layer == 1:
                for k in range(4):
                    gb_ref[...] += d_in[:, tile_of(k)]

    for layer in range(2):
        for side in range(2):
            start = (2 * layer + side) * HID
            out_ref[start : start + HID, :] = dot_nt(
                h_ref[layer], dx_ref[layer, side * HID : (side + 1) * HID, :]
            ).astype(bf16)
    out_ref[ROW_IN : ROW_IN + FEAT, :] = dot_nn(do_ref[...], node_ref[...]).T.astype(bf16)
    out_ref[ROW_OUT : ROW_OUT + HSIZE, :] = jnp.zeros((HSIZE, HID), bf16)
    out_ref[ROW_OUT : ROW_OUT + HSIZE, 0:CLASSES] = dot_nt(pool_ref[...], dlog_ref[...]).astype(bf16)
    ones = jnp.ones((nodes, LANES), bf16)
    lane_wide = lax.broadcasted_iota(jnp.int32, (HID, LANES), 1)
    columns = jnp.where(lane_wide == 0, dot_nn(do_ref[...], ones), 0.0)
    for layer in range(2):
        da = jnp.sum(da_ref[layer], axis=1, keepdims=True)
        columns = columns + jnp.where(lane_wide == 1 + layer, da, 0.0)
    columns = columns + jnp.where(lane_wide == 3, jnp.sum(gb_ref[...], axis=1, keepdims=True), 0.0)
    g_bias_out = dot_nn(dlog_ref[...], ones)
    g_bias_two = lax.dot_general(
        wo_ref[...].astype(f32), g_bias_out, (((1,), (0,)), ((), ())),
        precision=highest, preferred_element_type=f32,
    )
    loss = jnp.broadcast_to(jnp.sum(loss_ref[...], axis=1, keepdims=True), (8, LANES))
    loss_high = loss.astype(bf16).astype(f32)
    rest = HID - HSIZE - CLASSES - 16
    last = jnp.concatenate(
        [g_bias_two, g_bias_out, loss_high, loss - loss_high, jnp.zeros((rest, LANES), f32)], axis=0
    )
    columns = columns + jnp.where(lane_wide == 4, last, 0.0)
    out_ref[ROW_MISC : ROW_MISC + 16, :] = columns.T[0:16].astype(bf16)
    out_ref[ROW_MISC + 16 :, :] = jnp.zeros((ROWS - ROW_MISC - 16, HID), bf16)


def run_model(micro, features, src_all, labels, label_mask, send_index, whole, ints, first, small_params):
    nodes = features.shape[1]
    blocks = nodes // LANES
    scratch = [
        pltpu.VMEM((blocks, 2 * LANES, DEG * LANES), bf16),
        pltpu.VMEM((2, blocks, HID, SLOTS * LANES), bf16),
        pltpu.VMEM((2, blocks, 8, SLOTS * LANES), f32),
        pltpu.VMEM((2, blocks, HEADS, LANES, LANES), bf16),
        pltpu.VMEM((2, HID, nodes), bf16),
        pltpu.VMEM((2, HID, nodes), f32),
        pltpu.VMEM((2, 2 * HID, nodes), bf16),
        pltpu.VMEM((2, 2 * HID, nodes), bf16),
        pltpu.VMEM((HID, nodes), bf16),
        pltpu.VMEM((HSIZE, nodes), bf16),
        pltpu.VMEM((CLASSES, nodes), bf16),
        pltpu.VMEM((HID, SLOTS * LANES), bf16),
        pltpu.VMEM((HEADS * 16, SLOTS * LANES), bf16),
        pltpu.VMEM((2, HID, LANES), f32),
        pltpu.VMEM((2, HID, LANES), f32),
        pltpu.VMEM((HID, LANES), f32),
        pltpu.VMEM((1, 4 * LANES), f32),
        pltpu.VMEM((nodes, FEAT), bf16),
        pltpu.VMEM((DEG, nodes), jnp.int32),
        pltpu.VMEM((8, nodes), jnp.int32),
        pltpu.VMEM((FEAT, HID), bf16),
        pltpu.VMEM((2, 2 * HID, HID), bf16),
        pltpu.VMEM((2, HID, 2 * HID), bf16),
        pltpu.VMEM((HSIZE, CLASSES), bf16),
        pltpu.VMEM((HSIZE, HID), f32),
        pltpu.VMEM((2, 16, HID), bf16),
    ]
    grid_spec = pltpu.PrefetchScalarGridSpec(
        num_scalar_prefetch=1,
        grid=(1,),
        in_specs=[
            pl.BlockSpec((1, nodes, FEAT), lambda i, m: (m[0], 0, 0)),
            pl.BlockSpec((1, DEG, nodes), lambda i, m: (m[0], 0, 0)),
        ]
        + vmem(7),
        out_specs=vmem(1)[0],
        scratch_shapes=scratch,
    )
    return pl.pallas_call(
        model_kernel,
        grid_spec=grid_spec,
        out_shape=jax.ShapeDtypeStruct((ROWS, HID), bf16),
        compiler_params=pltpu.CompilerParams(vmem_limit_bytes=60 * 1024 * 1024),
        name="model",
    )(micro, features, src_all, labels, label_mask, send_index, whole, ints, first, small_params)


def adamw_step(parameter, gradient, moment_one, moment_two):
    moment_one = beta_one * moment_one + (1.0 - beta_one) * gradient
    moment_two = beta_two * moment_two + (1.0 - beta_two) * gradient * gradient
    corr_one = 1.0 - beta_one**STEPS
    corr_two = 1.0 - beta_two**STEPS
    update = moment_one / corr_one / (jnp.sqrt(moment_two / corr_two) + adam_eps)
    return (parameter - adam_rate * (update + adam_decay * parameter), moment_one, moment_two)


def average(old_value, new_value):
    return ema_keep * old_value + (1.0 - ema_keep) * new_value


def dot_tn(a, b):
    return lax.dot_general(a, b, (((0,), (0,)), ((), ())), preferred_element_type=f32)


def halves(value):
    high = value.astype(bf16)
    return high, (value - high.astype(f32)).astype(bf16)


def wide_rows(total):
    return max(total, 16)


def own_rows(gradient, start, count):
    total = gradient.shape[0]
    row = lax.broadcasted_iota(jnp.int32, (wide_rows(count), total), 0) + start
    lane = lax.broadcasted_iota(jnp.int32, (wide_rows(count), total), 1)
    pick = jnp.where(row == lane, 1.0, 0.0).astype(bf16)
    return dot_nn(pick, gradient).astype(bf16)


def precondition(gradient, weight, stat_l, stat_r, root_l, root_r, ema, outs, scale, start):
    (new_w, new_l, new_r, new_ema) = outs
    count = weight.shape[0]
    square = (1.0 - shampoo_decay) * scale * scale
    mine = own_rows(gradient, start, count)
    new_l[...] = shampoo_decay * stat_l + square * dot_nt(mine, gradient)[0:count]
    new_r[...] = shampoo_decay * stat_r + square * dot_tn(gradient, gradient)
    high, low = halves(root_l)
    middle = dot_nn(high, gradient) + dot_nn(low, gradient)
    m_high, m_low = halves(middle * scale)
    r_high, r_low = halves(root_r)
    update = dot_nn(m_high, r_high) + dot_nn(m_low, r_high) + dot_nn(m_high, r_low)
    weight = weight - shampoo_rate * (update + weight_decay * weight)
    new_w[...] = weight
    new_ema[...] = average(ema, weight)


def update_kernel(
    dom_ref,
    sum_ref,
    w_in,
    w_gat,
    w_out,
    small,
    l_in,
    r_in,
    l_gat,
    r_gat,
    l_out,
    r_out,
    rl_in,
    rr_in,
    rl_gat,
    rr_gat,
    rl_out,
    rr_out,
    first,
    second,
    e_in,
    e_gat,
    e_out,
    e_small,
    n_w_in,
    n_w_gat,
    n_w_out,
    n_small,
    n_l_in,
    n_r_in,
    n_l_gat,
    n_r_gat,
    n_l_out,
    n_r_out,
    n_first,
    n_second,
    n_e_in,
    n_e_gat,
    n_e_out,
    n_e_small,
    loss_ref,
    norm_ref,
):
    dom = dom_ref[0]
    grads = sum_ref[0:ROW_MISC, :].astype(f32)
    squares = jnp.sum(grads * grads)
    misc = sum_ref[ROW_MISC : ROW_MISC + 8, :].astype(f32)
    row = lax.broadcasted_iota(jnp.int32, (8, HID), 0)
    lane = lax.broadcasted_iota(jnp.int32, (8, HID), 1)
    spot = HSIZE + CLASSES
    loss_ref[0] = jnp.sum(jnp.where((row == 4) & ((lane == spot) | (lane == spot + 8)), misc, 0.0))
    small_part = jnp.where((row < 4) | ((row == 4) & (lane < spot)), misc, 0.0)
    squares = squares + jnp.sum(small_part * small_part)
    norm = jnp.sqrt(jnp.broadcast_to(squares, (1, 1)))
    scale = jnp.minimum(1.0, clip_norm / norm)
    norm_ref[0] = jnp.sum(norm)
    for layer in range(2):
        for side in range(2):
            at = (layer, side)
            begin = (2 * layer + side) * HID
            precondition(
                sum_ref[begin : begin + HID, :],
                w_gat[at],
                l_gat[at],
                r_gat[at],
                rl_gat[at],
                rr_gat[at],
                e_gat[at],
                (n_w_gat.at[at], n_l_gat.at[at], n_r_gat.at[at], n_e_gat.at[at]),
                scale,
                dom * w_gat.shape[2],
            )
    precondition(
        sum_ref[ROW_IN:ROW_OUT, :],
        w_in[...],
        l_in[...],
        r_in[...],
        rl_in[...],
        rr_in[...],
        e_in[...],
        (n_w_in, n_l_in, n_r_in, n_e_in),
        scale,
        dom * w_in.shape[0],
    )
    precondition(
        sum_ref[ROW_OUT:ROW_MISC, 0:CLASSES],
        w_out[...],
        l_out[...],
        r_out[...],
        rl_out[...],
        rr_out[...],
        e_out[...],
        (n_w_out, n_l_out, n_r_out, n_e_out),
        scale,
        dom * w_out.shape[0],
    )
    for place in range(5):
        width = HID if place < 4 else spot
        at = pl.ds(place * HID, width)
        gradient = misc[place : place + 1, 0:width] * scale

        def line(ref):
            return ref[at].reshape(1, width)

        new_value, moment_one, moment_two = adamw_step(line(small), gradient, line(first), line(second))
        n_small[at] = new_value.reshape(width)
        n_first[at] = moment_one.reshape(width)
        n_second[at] = moment_two.reshape(width)
        n_e_small[at] = average(line(e_small), new_value).reshape(width)


def per_device(
    features,
    sources,
    send_index,
    labels,
    label_mask,
    w_in,
    w_gat,
    w_out,
    small_params,
    stat_l_in,
    stat_r_in,
    stat_l_gat,
    stat_r_gat,
    stat_l_out,
    stat_r_out,
    root_l_in,
    root_r_in,
    root_l_gat,
    root_r_gat,
    root_l_out,
    root_r_out,
    adam_first,
    adam_second,
    ema_in,
    ema_gat,
    ema_out,
    ema_small,
):
    all_size = lax.axis_size("dom") * lax.axis_size("section")
    dom_id = lax.axis_index("dom").astype(jnp.int32).reshape(1)
    micro = lax.axis_index("section").astype(jnp.int32).reshape(1)
    size = lax.axis_size("dom")
    src_all = jnp.swapaxes(sources, 1, 2)
    packed, ints, first_rows = pack_inputs(
        micro, features, src_all, labels, label_mask, send_index, w_in, w_gat, w_out
    )
    down = [((i + 1) % size, i) for i in range(size)]
    first_rows = lax.ppermute(first_rows, "dom", down)
    ints = lax.ppermute(ints, "dom", down)
    whole = gather_weights(packed, w_in, w_gat, w_out, label_mask)
    partial = run_model(
        micro, features, src_all, labels, label_mask, send_index, whole, ints, first_rows, small_params
    )
    parts = lax.all_to_all(partial.reshape(all_size, -1, HID), ("section", "dom"), 0, 0)
    mine = jnp.sum(parts.astype(f32), axis=0)
    shared = jnp.broadcast_to(mine.astype(bf16)[None], (all_size,) + mine.shape)
    summed = lax.all_to_all(shared, ("section", "dom"), 0, 0).reshape(ROWS, HID)
    state = (
        w_in,
        w_gat,
        w_out,
        small_params,
        stat_l_in,
        stat_r_in,
        stat_l_gat,
        stat_r_gat,
        stat_l_out,
        stat_r_out,
        root_l_in,
        root_r_in,
        root_l_gat,
        root_r_gat,
        root_l_out,
        root_r_out,
        adam_first,
        adam_second,
        ema_in,
        ema_gat,
        ema_out,
        ema_small,
    )
    like = state[:10] + (adam_first, adam_second, ema_in, ema_gat, ema_out, ema_small)
    results = pl.pallas_call(
        update_kernel,
        out_shape=[jax.ShapeDtypeStruct(v.shape, f32) for v in like] + [jax.ShapeDtypeStruct((1,), f32)] * 2,
        in_specs=[pl.BlockSpec(memory_space=pltpu.SMEM)] + vmem(23),
        out_specs=vmem(16) + [pl.BlockSpec(memory_space=pltpu.SMEM)] * 2,
        compiler_params=pltpu.CompilerParams(vmem_limit_bytes=60 * 1024 * 1024),
        name="update",
    )(dom_id, summed, *state)
    return tuple(results[:16]) + (results[16].reshape(()), results[17].reshape(()))


def solution(mesh):
    placed = (
        P(None, "dom", None),
        P(None, "dom", None),
        P(None, "dom"),
        P(None, "dom"),
        P(None, "dom"),
        P("dom", None),
        P(None, None, "dom", None),
        P("dom", None),
        P(),
        P("dom", None),
        P(),
        P(None, None, "dom", None),
        P(),
        P("dom", None),
        P(),
        P("dom", None),
        P(),
        P(None, None, "dom", None),
        P(),
        P("dom", None),
        P(),
        P(),
        P(),
        P("dom", None),
        P(None, None, "dom", None),
        P("dom", None),
        P(),
    )
    return jax.shard_map(
        per_device,
        mesh=mesh,
        in_specs=placed,
        out_specs=(
            P("dom", None),
            P(None, None, "dom", None),
            P("dom", None),
            P(),
            P("dom", None),
            P(),
            P(None, None, "dom", None),
            P(),
            P("dom", None),
            P(),
            P(),
            P(),
            P("dom", None),
            P(None, None, "dom", None),
            P("dom", None),
            P(),
            P(),
            P(),
        ),
        check_vma=False,
    )
```

```python
import jax
import jax.numpy as jnp
from jax import lax
from jax.experimental import pallas as pl
from jax.experimental.pallas import tpu as pltpu
from jax.sharding import PartitionSpec as P

FEAT = 128
HEADS = 4
HSIZE = 64
CLASSES = 40
STEPS = 5
HID = 256
SMALL = 1128


highest = lax.Precision.HIGHEST
leak_slope = 0.2
smooth = 0.1
clip_norm = 0.001
shampoo_rate = 0.3
shampoo_decay = 0.5
weight_decay = 0.0001
adam_rate = 0.1
beta_one = 0.9
beta_two = 0.999
adam_eps = 1e-08
adam_decay = 0.01
ema_keep = 0.9


def split_small(small_params):
    bias_in = small_params[0:HID]
    attention = small_params[HID : 3 * HID].reshape(2, HEADS, HSIZE)
    bias_one = small_params[3 * HID : 4 * HID]
    bias_two = small_params[4 * HID : 4 * HID + HSIZE]
    bias_out = small_params[4 * HID + HSIZE :]
    return (bias_in, attention, bias_one, bias_two, bias_out)


GRAPH = 64
LANES = 128
DEG = 8
SLOTS = DEG + 1
WAYS = 4
ROWS = 1280
GROUPS = 8
IN_G = FEAT // GROUPS
GAT_G = HID // GROUPS
OUT_G = HSIZE // GROUPS
TAIL_G = IN_G + 4 * GAT_G
PACK_G = TAIL_G + 2 * OUT_G
HALO_G = PACK_G + 32
PIECE = ROWS // 8
HALF = GRAPH // 2
ROW_IN = 4 * HID
ROW_OUT = ROW_IN + FEAT
ROW_MISC = ROW_OUT + HSIZE

bf16 = jnp.bfloat16
f32 = jnp.float32


def dot_nn(a, b):
    return lax.dot_general(a, b, (((1,), (0,)), ((), ())), preferred_element_type=f32)


def dot_nt(a, b):
    return lax.dot_general(a, b, (((1,), (1,)), ((), ())), preferred_element_type=f32)


def tile_of(k):
    return slice(k * LANES, (k + 1) * LANES)


def head_of(h):
    return slice(h * HSIZE, (h + 1) * HSIZE)


def row_of(ref, micro, width):
    picked = ref[0:1, 0:width]
    for other in range(1, ref.shape[0]):
        picked = jnp.where(micro == other, ref[other : other + 1, 0:width], picked)
    return picked


def pack_kernel(
    place_ref,
    feat_ref,
    src_ref,
    lab_ref,
    msk_ref,
    send_ref,
    win_ref,
    wgat_ref,
    wout_ref,
    pack_ref,
    tail_ref,
    ints_ref,
):
    micro = place_ref[0]
    nodes = lab_ref.shape[1]
    pack_ref[PACK_G : PACK_G + 16, 0:FEAT] = feat_ref[0, 0:16]
    pack_ref[PACK_G : PACK_G + 16, FEAT : 2 * FEAT] = feat_ref[0, 16:32]
    shift = LANES - HALF
    ints_ref[...] = jnp.zeros_like(ints_ref)
    far = src_ref[0]
    far = jnp.where(far >= nodes, far - nodes + GRAPH, far)
    ints_ref[0:DEG, 0:LANES] = pltpu.roll(far, shift, 1).astype(f32)
    ints_ref[DEG : DEG + 1, 0:LANES] = pltpu.roll(row_of(lab_ref, micro, LANES), shift, 1).astype(f32)
    ints_ref[DEG + 1 : DEG + 2, 0:LANES] = pltpu.roll(row_of(msk_ref, micro, LANES), shift, 1).astype(f32)
    send = row_of(send_ref, micro, 2 * HALF)
    ints_ref[DEG + 2 : DEG + 3, 0:LANES] = jnp.concatenate([send, send], axis=1).astype(f32)
    pack_ref[PACK_G + 16 : HALO_G, :] = ints_ref[...].astype(bf16)
    if win_ref.shape[0] != IN_G:
        pack_ref[0:PACK_G, :] = jnp.zeros((PACK_G, HID), bf16)
        return
    pack_ref[0:IN_G, :] = win_ref[...].astype(bf16)
    for layer in range(2):
        for side in range(2):
            start = IN_G + (2 * layer + side) * GAT_G
            pack_ref[start : start + GAT_G, :] = wgat_ref[layer, side].astype(bf16)
    tail_ref[...] = jnp.zeros_like(tail_ref)
    tail_ref[0:OUT_G, 0:CLASSES] = wout_ref[...]
    count = jnp.sum(jnp.sum(msk_ref[...].astype(f32), axis=1, keepdims=True), axis=0, keepdims=True)
    high = jnp.floor(count * (1.0 / 256.0))
    lane = lax.broadcasted_iota(jnp.int32, (1, HID), 1)
    low = jnp.where(lane == 1, count - 256.0 * high, 0.0)
    tail_ref[OUT_G : OUT_G + 1, :] = jnp.where(lane == 0, high, low)
    pack_ref[TAIL_G:PACK_G, :] = tail_ref[...].astype(bf16)


def vmem(count):
    return [pl.BlockSpec(memory_space=pltpu.VMEM)] * count


def pack_inputs(place, features, src_all, labels, label_mask, send_index, w_in, w_gat, w_out):
    grid_spec = pltpu.PrefetchScalarGridSpec(
        num_scalar_prefetch=1,
        grid=(1,),
        in_specs=[
            pl.BlockSpec((1, HALF, FEAT), lambda i, m: (m[0], 0, 0)),
            pl.BlockSpec((1, DEG, LANES), lambda i, m: (m[0], 0, 0)),
        ]
        + vmem(6),
        out_specs=vmem(1)[0],
        scratch_shapes=[pltpu.VMEM((2 * OUT_G, HID), f32), pltpu.VMEM((16, HID), f32)],
    )
    return pl.pallas_call(
        pack_kernel,
        grid_spec=grid_spec,
        out_shape=jax.ShapeDtypeStruct((HALO_G, HID), bf16),
        compiler_params=pltpu.CompilerParams(vmem_limit_bytes=60 * 1024 * 1024),
        name="pack",
    )(place, features, src_all, labels, label_mask, send_index, w_in, w_gat, w_out)


def crossed(value, axis, mask):
    return lax.ppermute(value, axis, [(i, i ^ mask) for i in range(lax.axis_size(axis))])


def gather_weights(packed, w_in, w_gat, w_out, label_mask):
    size = lax.axis_size("dom")
    if size == GROUPS:
        near = [packed] + [crossed(packed, "dom", 2 * j) for j in range(1, 4)]
        return near + [crossed(piece, "dom", 1) for piece in near], lax.axis_index("dom")
    halo = lax.ppermute(packed[PACK_G:], "dom", [((i + 1) % size, i) for i in range(size)])
    halo = jnp.broadcast_to(halo[None], (GROUPS,) + halo.shape)
    rows_in, rows_gat, rows_out = (w_in.shape[0], w_gat.shape[2], w_out.shape[0])
    count = jnp.sum(label_mask)
    digits = jnp.stack([lax.div(count, 256), lax.rem(count, 256)]).astype(bf16)
    packed = jnp.concatenate(
        [
            w_in.astype(bf16),
            w_gat.astype(bf16).reshape(4 * rows_gat, HID),
            jnp.pad(w_out.astype(bf16), ((0, 0), (0, HID - CLASSES))),
            jnp.pad(digits[None, :], ((0, 0), (0, HID - 2))),
        ],
        axis=0,
    )
    whole = lax.all_gather(packed, "dom", axis=0, tiled=False)
    cut = rows_in + 4 * rows_gat
    part_in = whole[:, :rows_in].reshape(GROUPS, IN_G, HID)
    part_gat = whole[:, rows_in:cut].reshape(GROUPS, size // GROUPS, 4, rows_gat, HID)
    part_gat = part_gat.transpose(0, 2, 1, 3, 4).reshape(GROUPS, 4 * GAT_G, HID)
    part_out = whole[:, cut : cut + rows_out].reshape(GROUPS, OUT_G, HID)
    counts = whole[:, cut + rows_out].reshape(GROUPS, size // GROUPS, HID)
    counts = jnp.pad(counts, ((0, 0), (0, OUT_G - size // GROUPS), (0, 0)))
    whole = jnp.concatenate([part_in, part_gat, part_out, counts, halo], axis=1)
    return [whole[g] for g in (0, 2, 4, 6, 1, 3, 5, 7)], 0


def column_of(row):
    return jnp.broadcast_to(row.reshape(1, -1), (LANES, row.shape[0])).T


def model_kernel(
    place_ref,
    feat_ref,
    src_ref,
    lab_ref,
    msk_ref,
    send_ref,
    piece_0,
    piece_1,
    piece_2,
    piece_3,
    piece_4,
    piece_5,
    piece_6,
    piece_7,
    small_ref,
    keep_ref,
    send_out_ref,
    e_ref,
    t_ref,
    al_ref,
    att_ref,
    h_ref,
    slope_ref,
    xlr_ref,
    dx_ref,
    do_ref,
    pool_ref,
    dlog_ref,
    w_ref,
    sum_ref,
    a_ref,
    da_ref,
    gb_ref,
    loss_ref,
    node_ref,
    edge_ref,
    mark_ref,
    wi_ref,
    wgt_ref,
    wg_ref,
    wo_ref,
    wof_ref,
    am_ref,
    out_ref,
    eye_ref,
    halo_ref,
):
    nodes = feat_ref.shape[1]
    blocks = nodes // LANES
    chunk = 4 * LANES
    chunks = nodes // chunk
    mixed = DEG * LANES
    micro = place_ref[0]
    after = jnp.bitwise_and(place_ref[2] + 1, GROUPS - 1)
    final = nodes - LANES

    digits = jnp.zeros((OUT_G, HID), f32)
    pieces = (piece_0, piece_1, piece_2, piece_3, piece_4, piece_5, piece_6, piece_7)
    for j, piece in enumerate(pieces):
        group = jnp.bitwise_xor(place_ref[2], 2 * (j & 3) + (j >> 2))

        def rows_of(width):
            return pl.ds(pl.multiple_of(group * width, width), width)

        wi_ref[rows_of(IN_G), :] = piece[0:IN_G, :]
        for layer in range(2):
            for side in range(2):
                start = IN_G + (2 * layer + side) * GAT_G
                wg_ref[layer, rows_of(GAT_G), side * HID : (side + 1) * HID] = piece[start : start + GAT_G, :]
        tail = piece[TAIL_G:PACK_G, :].astype(f32)
        wof_ref[rows_of(OUT_G), :] = tail[0:OUT_G]
        digits = digits + tail[OUT_G : 2 * OUT_G]
        halo_ref[group] = piece[PACK_G:HALO_G, :]

    node_ref[0 : nodes - HALF, :] = feat_ref[0, HALF:nodes, :]
    node_ref[nodes - HALF : nodes - 16, :] = halo_ref[after, 0:16, 0:FEAT]
    node_ref[nodes - 16 : nodes, :] = halo_ref[after, 0:16, FEAT : 2 * FEAT]
    ints = halo_ref[after, 16:32, 0:LANES].astype(f32).astype(jnp.int32)
    lane_row = lax.broadcasted_iota(jnp.int32, (1, LANES), 1)
    kept = lane_row < LANES - HALF
    edge_ref[...] = pltpu.roll(src_ref[0], nodes - HALF, 1)
    edge_ref[:, final:nodes] = jnp.where(
        kept,
        edge_ref[:, final:nodes],
        jnp.where(ints[0:DEG] >= GRAPH, ints[0:DEG] + (nodes - GRAPH), ints[0:DEG]),
    )
    for place, ref in enumerate((lab_ref, msk_ref)):
        mark_ref[place : place + 1, :] = pltpu.roll(row_of(ref, micro, nodes), nodes - HALF, 1)
        came = ints[DEG + place : DEG + place + 1]
        mark_ref[place : place + 1, final:nodes] = jnp.where(kept, mark_ref[place : place + 1, final:nodes], came)
    send = row_of(send_ref, micro, 2 * HALF)
    send = jnp.concatenate([send, send], axis=1)
    arrived = pltpu.roll(ints[DEG + 2 : DEG + 3], HALF, 1)
    table = jnp.where(
        lane_row < HALF, pltpu.roll(send, HALF, 1) - (nodes - HALF), arrived + HALF
    )
    spot_row = lax.broadcasted_iota(jnp.int32, (GRAPH, LANES), 0)
    spot_lane = lax.broadcasted_iota(jnp.int32, (GRAPH, LANES), 1)
    table = jnp.sum(jnp.where(spot_row == spot_lane, table.astype(f32), 0.0), axis=1, keepdims=True)
    looked = []
    for k in range(DEG):
        far = edge_ref[k : k + 1, final:nodes] - nodes == spot_row
        looked.append(jnp.sum(jnp.where(far, table, 0.0), axis=0, keepdims=True))
    looked = jnp.concatenate(looked, axis=0).astype(jnp.int32)
    raw = edge_ref[:, final:nodes]
    looked = jnp.where(raw >= nodes, looked, jnp.bitwise_and(raw - HALF, GRAPH - 1))
    local = jnp.bitwise_and(edge_ref[...] - HALF, GRAPH - 1)
    lane_all = lax.broadcasted_iota(jnp.int32, (DEG, nodes), 1)
    second = jnp.bitwise_and(lane_all, GRAPH)
    edge_ref[...] = local + second
    edge_ref[:, final:nodes] = looked + jnp.bitwise_and(
        lax.broadcasted_iota(jnp.int32, (DEG, LANES), 1), GRAPH
    )

    for layer in range(2):
        for side in range(2):
            wgt_ref[layer, side * HID : (side + 1) * HID, :] = wg_ref[
                layer, :, side * HID : (side + 1) * HID
            ].T
    wi_t = wi_ref[...].T
    wo_ref[...] = wof_ref[:, 0:CLASSES].astype(bf16)
    wo_t = wof_ref[...].T[0:CLASSES].astype(bf16)
    digits = jnp.sum(digits, axis=0, keepdims=True)
    inv_count = 1.0 / (digits[:, 0:1] * 256.0 + digits[:, 1:2])

    row_id = lax.broadcasted_iota(jnp.int32, (LANES, LANES), 0)
    lane_id = lax.broadcasted_iota(jnp.int32, (LANES, LANES), 1)
    eye = jnp.where(row_id == lane_id, 1.0, 0.0).astype(bf16)
    head_row = lax.broadcasted_iota(jnp.int32, (16, HID), 0)
    head_col = lax.broadcasted_iota(jnp.int32, (16, HID), 1)
    head_mask = jnp.where(head_col // HSIZE == head_row, 1.0, 0.0)

    bias_in = column_of(small_ref[0:HID])[:, 0:1]
    bias_one = column_of(small_ref[3 * HID : 4 * HID])[:, 0:1]
    bias_two = column_of(small_ref[4 * HID : 4 * HID + HSIZE])[:, 0:1]
    bias_out = column_of(small_ref[4 * HID + HSIZE : SMALL])[:, 0:1]
    for layer in range(2):
        row = small_ref[(1 + layer) * HID : (2 + layer) * HID]
        a_ref[layer] = column_of(row)
        row = row.reshape(1, HID)
        high = row.astype(bf16).astype(f32)
        am_ref[layer] = jnp.concatenate([head_mask[0:8] * high, head_mask[0:8] * (row - high)], axis=0).astype(bf16)
    fold_row = lax.broadcasted_iota(jnp.int32, (16, HEADS * 16), 0)
    fold_col = lax.broadcasted_iota(jnp.int32, (16, HEADS * 16), 1)
    fold = jnp.where(fold_col // 16 == fold_row, 1.0, 0.0).astype(bf16)
    spots = lax.broadcasted_iota(jnp.int32, (GRAPH, LANES), 0).astype(f32).astype(bf16)
    spots = spots.reshape(4, 16, LANES)
    half_lane = lax.broadcasted_iota(jnp.int32, (16, LANES), 1)
    first_half = (half_lane < GRAPH).astype(f32).astype(bf16)[None] > 0
    own_spot = jnp.bitwise_and(half_lane, GRAPH - 1).astype(f32).astype(bf16)
    zero = jnp.zeros((4, 16, LANES), bf16)
    da_ref[...] = jnp.zeros_like(da_ref)
    gb_ref[...] = jnp.zeros_like(gb_ref)
    loss_ref[...] = jnp.zeros_like(loss_ref)

    def lanes_of(i, width):
        return pl.ds(pl.multiple_of(i * width, width), width)

    @pl.loop(0, chunks, unroll=4)
    def _(c):
        at = lanes_of(c, chunk)
        pre = dot_nt(wi_t, node_ref[at, :]) + bias_in
        grown = jnp.exp(jnp.minimum(pre, 0.0))
        h_ref[0, :, at] = jnp.where(pre > 0, pre, grown - 1.0).astype(bf16)
        slope_ref[0, :, at] = jnp.where(pre > 0, 1.0, grown)

    wide_spots = lax.broadcasted_iota(jnp.int32, (LANES, LANES), 0).astype(f32).astype(bf16)
    wide_spots = wide_spots.reshape(8, 16, LANES)
    for k in range(DEG):
        eye_ref[:, tile_of(k)] = eye

    @pl.loop(0, blocks)
    def _(i):
        at = lanes_of(i, LANES)
        for k in range(DEG):
            spot = jnp.broadcast_to(edge_ref[k : k + 1, at].astype(f32), (16, LANES)).astype(bf16)
            hit = wide_spots == spot[None]
            hit = jnp.where(hit, jnp.ones((8, 16, LANES), bf16), jnp.zeros((8, 16, LANES), bf16))
            e_ref[i, :, tile_of(k)] = hit.reshape(LANES, LANES)

    for layer in range(2):

        @pl.loop(0, chunks, unroll=4)
        def _(c):
            at = lanes_of(c, chunk)
            xlr_ref[layer, :, at] = dot_nn(wgt_ref[layer], h_ref[layer, :, at]).astype(bf16)

        @pl.loop(0, blocks // WAYS)
        def _(step):
            ids = [step * WAYS + u for u in range(WAYS)]
            ats = [lanes_of(i, LANES) for i in ids]
            ways = range(WAYS)
            left = [xlr_ref[layer, 0:HID, ats[u]] for u in ways]
            grown = []
            for u in ways:
                right = xlr_ref[layer, HID : 2 * HID, ats[u]]
                mixed_rows = dot_nn(left[u], e_ref[ids[u]]).astype(bf16)
                mixed_rows = mixed_rows + jnp.concatenate([right] * DEG, axis=1)
                own = left[u] + right
                t_ref[layer, ids[u], :, 0:mixed] = mixed_rows
                t_ref[layer, ids[u], :, tile_of(DEG)] = own
                t = jnp.concatenate([mixed_rows, own], axis=1)
                z = jnp.maximum(t, t * leak_slope)
                scores = dot_nn(am_ref[layer], z)
                grown.append(jnp.exp(scores[0:8] + scores[8:16]))
            grids_all = []
            for u in ways:
                total = grown[u][:, tile_of(0)]
                for k in range(1, SLOTS):
                    total = total + grown[u][:, tile_of(k)]
                inverse = 1.0 / total
                grids = [zero] * HEADS
                for k in range(SLOTS):
                    alpha = grown[u][:, tile_of(k)] * inverse
                    al_ref[layer, ids[u], :, tile_of(k)] = alpha
                    if k == DEG:
                        spot = own_spot
                    else:
                        spot = jnp.bitwise_and(edge_ref[k : k + 1, ats[u]], GRAPH - 1).astype(f32)
                        spot = jnp.broadcast_to(spot, (16, LANES)).astype(bf16)
                    hit = spots == spot[None]
                    for h in range(HEADS):
                        part = jnp.broadcast_to(alpha[h : h + 1], (16, LANES)).astype(bf16)
                        grids[h] = grids[h] + jnp.where(hit, part[None], zero)
                grids_all.append(grids)
            for u in ways:
                pooled = None
                for h in range(HEADS):
                    upper = jnp.where(first_half, grids_all[u][h], zero).reshape(GRAPH, LANES)
                    lower = jnp.where(first_half, zero, grids_all[u][h]).reshape(GRAPH, LANES)
                    grid = jnp.concatenate([upper, lower], axis=0)
                    att_ref[layer, ids[u], h] = grid
                    total = dot_nn(left[u][head_of(h)], grid)
                    if layer == 0:
                        pre = total + bias_one[head_of(h)]
                        grown_one = jnp.exp(jnp.minimum(pre, 0.0))
                        h_ref[1, head_of(h), ats[u]] = jnp.where(pre > 0, pre, grown_one - 1.0).astype(bf16)
                        slope_ref[1, head_of(h), ats[u]] = jnp.where(pre > 0, 1.0, grown_one)
                    else:
                        rounded = total.astype(bf16).astype(f32)
                        pooled = rounded if pooled is None else pooled + rounded
                if layer == 1:
                    pool_ref[:, ats[u]] = (pooled * (1.0 / HEADS) + bias_two).astype(bf16)

    @pl.loop(0, chunks, unroll=4)
    def _(c):
        at = lanes_of(c, chunk)
        logits = dot_nn(wo_t, pool_ref[:, at]) + bias_out
        shifted = logits - jnp.max(logits, axis=0, keepdims=True)
        log_prob = shifted - jnp.log(jnp.sum(jnp.exp(shifted), axis=0, keepdims=True))
        class_id = lax.broadcasted_iota(jnp.int32, (CLASSES, chunk), 0)
        onehot = jnp.where(class_id == mark_ref[0:1, at], 1.0, 0.0)
        share = mark_ref[1:2, at].astype(f32) * inv_count
        term = jnp.sum(((smooth - 1.0) * onehot - smooth / CLASSES) * log_prob, axis=0, keepdims=True)
        loss_ref[...] += term * share
        d_logits = (jnp.exp(log_prob) - (1.0 - smooth) * onehot - smooth / CLASSES) * share
        d_logits = d_logits.astype(bf16)
        dlog_ref[:, at] = d_logits
        d_pooled = (dot_nn(wo_ref[...], d_logits) * (1.0 / HEADS)).astype(bf16)
        for h in range(HEADS):
            do_ref[head_of(h), at] = d_pooled

    for layer in (1, 0):

        @pl.loop(0, blocks // WAYS)
        def _(step):
            ids = [step * WAYS + u for u in range(WAYS)]
            ats = [lanes_of(i, LANES) for i in ids]
            ways = range(WAYS)
            d_out = [do_ref[:, ats[u]] for u in ways]
            d_alpha = []
            for u in ways:
                for h in range(HEADS):
                    d_head = d_out[u][head_of(h)].reshape(4, 16, LANES)
                    for k in range(SLOTS):
                        t = t_ref[layer, ids[u], head_of(h), tile_of(k)].reshape(4, 16, LANES)
                        product = t * d_head
                        sum_ref[u, h * 16 : (h + 1) * 16, tile_of(k)] = (product[0] + product[1]) + (
                            product[2] + product[3]
                        )
                d_alpha.append(dot_nn(fold, sum_ref[u])[0:8])
            for u in ways:
                alpha = al_ref[layer, ids[u]]
                weighted = alpha * d_alpha[u]
                total = weighted[:, tile_of(0)]
                for k in range(1, SLOTS):
                    total = total + weighted[:, tile_of(k)]
                for k in range(SLOTS):
                    d_score = weighted[:, tile_of(k)] - alpha[:, tile_of(k)] * total
                    for h in range(HEADS):
                        one = jnp.broadcast_to(d_score[h : h + 1], (16, LANES))
                        two = (one * leak_slope).astype(bf16)[None]
                        one = one.astype(bf16)[None]
                        t = t_ref[layer, ids[u], head_of(h), tile_of(k)].reshape(4, 16, LANES)
                        w_ref[u, head_of(h), tile_of(k)] = jnp.where(t > 0, one, two).reshape(HSIZE, LANES)
            for u in ways:
                together = jnp.concatenate([e_ref[ids[u]], eye_ref[...]], axis=0)
                spread = dot_nt(w_ref[u, :, 0:mixed], together)
                own = w_ref[u, :, tile_of(DEG)].astype(f32)
                left_w = spread[:, 0:LANES] + own
                right_w = spread[:, LANES : 2 * LANES] + own
                left = xlr_ref[layer, 0:HID, ats[u]].astype(f32)
                right = xlr_ref[layer, HID : 2 * HID, ats[u]].astype(f32)
                da_ref[layer] += left * left_w + right * right_w
                wide = a_ref[layer]
                for h in range(HEADS):
                    passed = dot_nt(d_out[u][head_of(h)], att_ref[layer, ids[u], h])
                    d_left = wide[head_of(h)] * left_w[head_of(h)] + passed
                    dx_ref[layer, head_of(h), ats[u]] = d_left.astype(bf16)
                dx_ref[layer, HID : 2 * HID, ats[u]] = (wide * right_w).astype(bf16)

        @pl.loop(0, chunks, unroll=4)
        def _(c):
            at = lanes_of(c, chunk)
            d_in = dot_nn(wg_ref[layer], dx_ref[layer, :, at]).astype(bf16).astype(f32)
            d_in = d_in * slope_ref[layer, :, at]
            do_ref[:, at] = d_in.astype(bf16)
            if layer == 1:
                for k in range(4):
                    gb_ref[...] += d_in[:, tile_of(k)]

    for layer in range(2):
        for side in range(2):
            start = (2 * layer + side) * HID
            out_ref[start : start + HID, :] = dot_nt(
                h_ref[layer], dx_ref[layer, side * HID : (side + 1) * HID, :]
            ).astype(bf16)
    out_ref[ROW_IN : ROW_IN + FEAT, :] = dot_nn(do_ref[...], node_ref[...]).T.astype(bf16)
    out_ref[ROW_OUT : ROW_OUT + HSIZE, :] = jnp.zeros((HSIZE, HID), bf16)
    out_ref[ROW_OUT : ROW_OUT + HSIZE, 0:CLASSES] = dot_nt(pool_ref[...], dlog_ref[...]).astype(bf16)
    ones = jnp.ones((nodes, LANES), bf16)
    lane_wide = lax.broadcasted_iota(jnp.int32, (HID, LANES), 1)
    columns = jnp.where(lane_wide == 0, dot_nn(do_ref[...], ones), 0.0)
    for layer in range(2):
        da = jnp.sum(da_ref[layer], axis=1, keepdims=True)
        columns = columns + jnp.where(lane_wide == 1 + layer, da, 0.0)
    columns = columns + jnp.where(lane_wide == 3, jnp.sum(gb_ref[...], axis=1, keepdims=True), 0.0)
    g_bias_out = dot_nn(dlog_ref[...], ones)
    g_bias_two = lax.dot_general(
        wo_ref[...].astype(f32), g_bias_out, (((1,), (0,)), ((), ())),
        precision=highest, preferred_element_type=f32,
    )
    loss = jnp.broadcast_to(jnp.sum(loss_ref[...], axis=1, keepdims=True), (8, LANES))
    loss_high = loss.astype(bf16).astype(f32)
    rest = HID - HSIZE - CLASSES - 16
    last = jnp.concatenate(
        [g_bias_two, g_bias_out, loss_high, loss - loss_high, jnp.zeros((rest, LANES), f32)], axis=0
    )
    columns = columns + jnp.where(lane_wide == 4, last, 0.0)
    out_ref[ROW_MISC : ROW_MISC + 16, :] = columns.T[0:16].astype(bf16)
    out_ref[ROW_MISC + 16 :, :] = jnp.zeros((ROWS - ROW_MISC - 16, HID), bf16)
    core = jnp.bitwise_and(place_ref[1], 1)
    width = ROWS // 2
    keep_ref[...] = out_ref[pl.ds(pl.multiple_of(core * width, width), width), :]
    send_out_ref[...] = out_ref[pl.ds(pl.multiple_of((1 - core) * width, width), width), :]


def run_model(place, features, src_all, labels, label_mask, send_index, pieces, small_params):
    nodes = features.shape[1]
    blocks = nodes // LANES
    scratch = [
        pltpu.VMEM((blocks, LANES, DEG * LANES), bf16),
        pltpu.VMEM((2, blocks, HID, SLOTS * LANES), bf16),
        pltpu.VMEM((2, blocks, 8, SLOTS * LANES), f32),
        pltpu.VMEM((2, blocks, HEADS, LANES, LANES), bf16),
        pltpu.VMEM((2, HID, nodes), bf16),
        pltpu.VMEM((2, HID, nodes), f32),
        pltpu.VMEM((2, 2 * HID, nodes), bf16),
        pltpu.VMEM((2, 2 * HID, nodes), bf16),
        pltpu.VMEM((HID, nodes), bf16),
        pltpu.VMEM((HSIZE, nodes), bf16),
        pltpu.VMEM((CLASSES, nodes), bf16),
        pltpu.VMEM((WAYS, HID, SLOTS * LANES), bf16),
        pltpu.VMEM((WAYS, HEADS * 16, SLOTS * LANES), bf16),
        pltpu.VMEM((2, HID, LANES), f32),
        pltpu.VMEM((2, HID, LANES), f32),
        pltpu.VMEM((HID, LANES), f32),
        pltpu.VMEM((1, 4 * LANES), f32),
        pltpu.VMEM((nodes, FEAT), bf16),
        pltpu.VMEM((DEG, nodes), jnp.int32),
        pltpu.VMEM((8, nodes), jnp.int32),
        pltpu.VMEM((FEAT, HID), bf16),
        pltpu.VMEM((2, 2 * HID, HID), bf16),
        pltpu.VMEM((2, HID, 2 * HID), bf16),
        pltpu.VMEM((HSIZE, CLASSES), bf16),
        pltpu.VMEM((HSIZE, HID), f32),
        pltpu.VMEM((2, 16, HID), bf16),
        pltpu.VMEM((ROWS, HID), bf16),
        pltpu.VMEM((LANES, DEG * LANES), bf16),
        pltpu.VMEM((GROUPS, HALO_G - PACK_G, HID), bf16),
    ]
    grid_spec = pltpu.PrefetchScalarGridSpec(
        num_scalar_prefetch=1,
        grid=(1,),
        in_specs=[
            pl.BlockSpec((1, nodes, FEAT), lambda i, m: (m[0], 0, 0)),
            pl.BlockSpec((1, DEG, nodes), lambda i, m: (m[0], 0, 0)),
        ]
        + vmem(12),
        out_specs=vmem(2),
        scratch_shapes=scratch,
    )
    return pl.pallas_call(
        model_kernel,
        grid_spec=grid_spec,
        out_shape=[jax.ShapeDtypeStruct((ROWS // 2, HID), bf16)] * 2,
        compiler_params=pltpu.CompilerParams(vmem_limit_bytes=54 * 1024 * 1024),
        name="model",
    )(place, features, src_all, labels, label_mask, send_index, *pieces, small_params)


def settled(total, is_last):
    base = ROW_MISC % PIECE
    block = total[base : base + 8]
    row = lax.broadcasted_iota(jnp.int32, (8, HID), 0)
    lane = lax.broadcasted_iota(jnp.int32, (8, HID), 1)
    spot = HSIZE + CLASSES
    joined = block + pltpu.roll(block, HID - 8, 1)
    high = joined.astype(bf16).astype(f32)
    low = pltpu.roll(joined - high, 8, 1)
    here = (row == 4) & (lane >= spot) & (lane < spot + 16) & (is_last == 1)
    block = jnp.where(here, jnp.where(lane < spot + 8, high, low), block)
    return jnp.concatenate([total[:base], block, total[base + 8 :]], axis=0).astype(bf16)


def last_piece(core, section):
    return jnp.where((core == 1) & (section == 3), 1, 0)


def split_kernel(place_ref, keep_ref, got_ref, *out_refs):
    section = place_ref[0]
    core = jnp.bitwise_and(place_ref[1], 1)
    for j, out_ref in enumerate(out_refs):
        part = jnp.bitwise_xor(section, j)
        at = pl.ds(pl.multiple_of(part * PIECE, PIECE), PIECE)
        total = keep_ref[at, :].astype(f32) + got_ref[at, :].astype(f32)
        out_ref[...] = settled(total, last_piece(core, part))


def join_kernel(place_ref, own_ref, one_ref, two_ref, three_ref, out_ref):
    pair = own_ref[...].astype(f32) + one_ref[...].astype(f32)
    other = two_ref[...].astype(f32) + three_ref[...].astype(f32)
    core = jnp.bitwise_and(place_ref[1], 1)
    out_ref[...] = settled(pair + other, last_piece(core, place_ref[0]))


def small_call(kernel, name, place, count, operands):
    shape = jax.ShapeDtypeStruct((PIECE, HID), bf16)
    return pl.pallas_call(
        kernel,
        out_shape=[shape] * count if count > 1 else shape,
        in_specs=[pl.BlockSpec(memory_space=pltpu.SMEM)] + vmem(len(operands)),
        out_specs=vmem(count) if count > 1 else vmem(1)[0],
        compiler_params=pltpu.CompilerParams(vmem_limit_bytes=8 * 1024 * 1024),
        name=name,
    )(place, *operands)


def sum_gradients(place, keep, send):
    if lax.axis_size("dom") == 8 and lax.axis_size("section") == 4:
        got = crossed(send, "dom", 1)
        parts = small_call(split_kernel, "split", place, 4, (keep, got))
        came = [crossed(parts[j], "section", j) for j in range(1, 4)]
        mine = small_call(join_kernel, "join", place, 1, (parts[0], *came))
        came = [crossed(mine, "dom", 2 * j) for j in range(1, 4)]
        mine = small_call(join_kernel, "join", place, 1, (mine, *came))
        near = [mine] + [crossed(mine, "section", j) for j in range(1, 4)]
        return near + [crossed(piece, "dom", 1) for piece in near], place
    all_size = lax.axis_size("dom") * lax.axis_size("section")
    swap = jnp.bitwise_and(place[1], 1) == 1
    partial = jnp.concatenate([jnp.where(swap, send, keep), jnp.where(swap, keep, send)], axis=0)
    parts = lax.all_to_all(partial.reshape(all_size, -1, HID), ("section", "dom"), 0, 0)
    mine = jnp.sum(parts.astype(f32), axis=0)
    shared = jnp.broadcast_to(mine.astype(bf16)[None], (all_size,) + mine.shape)
    summed = lax.all_to_all(shared, ("section", "dom"), 0, 0).reshape(8, PIECE, HID)
    return [summed[j] for j in range(8)], place * jnp.array([0, 2, 0], jnp.int32)


def adamw_step(parameter, gradient, moment_one, moment_two):
    moment_one = beta_one * moment_one + (1.0 - beta_one) * gradient
    moment_two = beta_two * moment_two + (1.0 - beta_two) * gradient * gradient
    corr_one = 1.0 - beta_one**STEPS
    corr_two = 1.0 - beta_two**STEPS
    update = moment_one / corr_one / (jnp.sqrt(moment_two / corr_two) + adam_eps)
    return (parameter - adam_rate * (update + adam_decay * parameter), moment_one, moment_two)


def average(old_value, new_value):
    return ema_keep * old_value + (1.0 - ema_keep) * new_value


def dot_tn(a, b):
    return lax.dot_general(a, b, (((0,), (0,)), ((), ())), preferred_element_type=f32)


def halves(value):
    high = value.astype(bf16)
    return high, (value - high.astype(f32)).astype(bf16)


def wide_rows(total):
    return max(total, 16)


def own_rows(gradient, start, count):
    total = gradient.shape[0]
    row = lax.broadcasted_iota(jnp.int32, (wide_rows(count), total), 0) + start
    lane = lax.broadcasted_iota(jnp.int32, (wide_rows(count), total), 1)
    pick = jnp.where(row == lane, 1.0, 0.0).astype(bf16)
    return dot_nn(pick, gradient).astype(bf16)


def precondition(gradient, weight, stat_l, stat_r, root_l, root_r, ema, outs, scale, start):
    (new_w, new_l, new_r, new_ema) = outs
    count = weight.shape[0]
    square = (1.0 - shampoo_decay) * scale * scale
    mine = own_rows(gradient, start, count)
    new_l[...] = shampoo_decay * stat_l + square * dot_nt(mine, gradient)[0:count]
    new_r[...] = shampoo_decay * stat_r + square * dot_tn(gradient, gradient)
    high, low = halves(root_l)
    middle = dot_nn(high, gradient) + dot_nn(low, gradient)
    m_high, m_low = halves(middle * scale)
    r_high, r_low = halves(root_r)
    update = dot_nn(m_high, r_high) + dot_nn(m_low, r_high) + dot_nn(m_high, r_low)
    weight = weight - shampoo_rate * (update + weight_decay * weight)
    new_w[...] = weight
    new_ema[...] = average(ema, weight)


def update_kernel(
    dom_ref,
    place_ref,
    piece_0,
    piece_1,
    piece_2,
    piece_3,
    piece_4,
    piece_5,
    piece_6,
    piece_7,
    w_in,
    w_gat,
    w_out,
    small,
    l_in,
    r_in,
    l_gat,
    r_gat,
    l_out,
    r_out,
    rl_in,
    rr_in,
    rl_gat,
    rr_gat,
    rl_out,
    rr_out,
    first,
    second,
    e_in,
    e_gat,
    e_out,
    e_small,
    n_w_in,
    n_w_gat,
    n_w_out,
    n_small,
    n_l_in,
    n_r_in,
    n_l_gat,
    n_r_gat,
    n_l_out,
    n_r_out,
    n_first,
    n_second,
    n_e_in,
    n_e_gat,
    n_e_out,
    n_e_small,
    loss_ref,
    norm_ref,
    sum_ref,
):
    dom = dom_ref[0]
    core = jnp.bitwise_and(place_ref[1], 1)
    pieces = (piece_0, piece_1, piece_2, piece_3, piece_4, piece_5, piece_6, piece_7)
    for j, piece in enumerate(pieces):
        spot = jnp.bitwise_xor(core, j >> 2) * 4 + jnp.bitwise_xor(place_ref[0], j & 3)
        sum_ref[pl.ds(pl.multiple_of(spot * PIECE, PIECE), PIECE), :] = piece[...]
    grads = sum_ref[0:ROW_MISC, :].astype(f32)
    squares = jnp.sum(grads * grads)
    misc = sum_ref[ROW_MISC : ROW_MISC + 8, :].astype(f32)
    row = lax.broadcasted_iota(jnp.int32, (8, HID), 0)
    lane = lax.broadcasted_iota(jnp.int32, (8, HID), 1)
    spot = HSIZE + CLASSES
    loss_ref[0] = jnp.sum(jnp.where((row == 4) & ((lane == spot) | (lane == spot + 8)), misc, 0.0))
    small_part = jnp.where((row < 4) | ((row == 4) & (lane < spot)), misc, 0.0)
    squares = squares + jnp.sum(small_part * small_part)
    norm = jnp.sqrt(jnp.broadcast_to(squares, (1, 1)))
    scale = jnp.minimum(1.0, clip_norm / norm)
    norm_ref[0] = jnp.sum(norm)
    for layer in range(2):
        for side in range(2):
            at = (layer, side)
            begin = (2 * layer + side) * HID
            precondition(
                sum_ref[begin : begin + HID, :],
                w_gat[at],
                l_gat[at],
                r_gat[at],
                rl_gat[at],
                rr_gat[at],
                e_gat[at],
                (n_w_gat.at[at], n_l_gat.at[at], n_r_gat.at[at], n_e_gat.at[at]),
                scale,
                dom * w_gat.shape[2],
            )
    precondition(
        sum_ref[ROW_IN:ROW_OUT, :],
        w_in[...],
        l_in[...],
        r_in[...],
        rl_in[...],
        rr_in[...],
        e_in[...],
        (n_w_in, n_l_in, n_r_in, n_e_in),
        scale,
        dom * w_in.shape[0],
    )
    precondition(
        sum_ref[ROW_OUT:ROW_MISC, 0:CLASSES],
        w_out[...],
        l_out[...],
        r_out[...],
        rl_out[...],
        rr_out[...],
        e_out[...],
        (n_w_out, n_l_out, n_r_out, n_e_out),
        scale,
        dom * w_out.shape[0],
    )
    for place in range(5):
        width = HID if place < 4 else spot
        at = pl.ds(place * HID, width)
        gradient = misc[place : place + 1, 0:width] * scale

        def line(ref):
            return ref[at].reshape(1, width)

        new_value, moment_one, moment_two = adamw_step(line(small), gradient, line(first), line(second))
        n_small[at] = new_value.reshape(width)
        n_first[at] = moment_one.reshape(width)
        n_second[at] = moment_two.reshape(width)
        n_e_small[at] = average(line(e_small), new_value).reshape(width)


def per_device(
    features,
    sources,
    send_index,
    labels,
    label_mask,
    w_in,
    w_gat,
    w_out,
    small_params,
    stat_l_in,
    stat_r_in,
    stat_l_gat,
    stat_r_gat,
    stat_l_out,
    stat_r_out,
    root_l_in,
    root_r_in,
    root_l_gat,
    root_r_gat,
    root_l_out,
    root_r_out,
    adam_first,
    adam_second,
    ema_in,
    ema_gat,
    ema_out,
    ema_small,
):
    dom_id = lax.axis_index("dom").astype(jnp.int32).reshape(1)
    section_id = lax.axis_index("section")
    place = jnp.stack([section_id, lax.axis_index("dom"), lax.axis_index("dom")]).astype(jnp.int32)
    src_all = jnp.swapaxes(sources, 1, 2)
    packed = pack_inputs(place, features, src_all, labels, label_mask, send_index, w_in, w_gat, w_out)
    pieces, spot = gather_weights(packed, w_in, w_gat, w_out, label_mask)
    place = jnp.stack([section_id, lax.axis_index("dom"), spot]).astype(jnp.int32)
    keep, send = run_model(
        place, features, src_all, labels, label_mask, send_index, pieces, small_params
    )
    pieces, spot = sum_gradients(place, keep, send)
    state = (
        w_in,
        w_gat,
        w_out,
        small_params,
        stat_l_in,
        stat_r_in,
        stat_l_gat,
        stat_r_gat,
        stat_l_out,
        stat_r_out,
        root_l_in,
        root_r_in,
        root_l_gat,
        root_r_gat,
        root_l_out,
        root_r_out,
        adam_first,
        adam_second,
        ema_in,
        ema_gat,
        ema_out,
        ema_small,
    )
    like = state[:10] + (adam_first, adam_second, ema_in, ema_gat, ema_out, ema_small)
    results = pl.pallas_call(
        update_kernel,
        out_shape=[jax.ShapeDtypeStruct(v.shape, f32) for v in like] + [jax.ShapeDtypeStruct((1,), f32)] * 2,
        in_specs=[pl.BlockSpec(memory_space=pltpu.SMEM)] * 2 + vmem(30),
        out_specs=vmem(16) + [pl.BlockSpec(memory_space=pltpu.SMEM)] * 2,
        scratch_shapes=[pltpu.VMEM((ROWS, HID), bf16)],
        compiler_params=pltpu.CompilerParams(vmem_limit_bytes=16 * 1024 * 1024),
        name="update",
    )(dom_id, spot, *pieces, *state)
    return tuple(results[:16]) + (results[16].reshape(()), results[17].reshape(()))


def solution(mesh):
    placed = (
        P(None, "dom", None),
        P(None, "dom", None),
        P(None, "dom"),
        P(None, "dom"),
        P(None, "dom"),
        P("dom", None),
        P(None, None, "dom", None),
        P("dom", None),
        P(),
        P("dom", None),
        P(),
        P(None, None, "dom", None),
        P(),
        P("dom", None),
        P(),
        P("dom", None),
        P(),
        P(None, None, "dom", None),
        P(),
        P("dom", None),
        P(),
        P(),
        P(),
        P("dom", None),
        P(None, None, "dom", None),
        P("dom", None),
        P(),
    )
    return jax.shard_map(
        per_device,
        mesh=mesh,
        in_specs=placed,
        out_specs=(
            P("dom", None),
            P(None, None, "dom", None),
            P("dom", None),
            P(),
            P("dom", None),
            P(),
            P(None, None, "dom", None),
            P(),
            P("dom", None),
            P(),
            P(),
            P(),
            P("dom", None),
            P(None, None, "dom", None),
            P("dom", None),
            P(),
            P(),
            P(),
        ),
        check_vma=False,
    )
```

```python
import jax
import jax.numpy as jnp
from jax import lax
from jax.experimental import pallas as pl
from jax.experimental.pallas import tpu as pltpu
from jax.sharding import PartitionSpec as P

FEAT = 128
HEADS = 4
HSIZE = 64
CLASSES = 40
STEPS = 5
HID = 256
SMALL = 1128


highest = lax.Precision.HIGHEST
leak_slope = 0.2
smooth = 0.1
clip_norm = 0.001
shampoo_rate = 0.3
shampoo_decay = 0.5
weight_decay = 0.0001
adam_rate = 0.1
beta_one = 0.9
beta_two = 0.999
adam_eps = 1e-08
adam_decay = 0.01
ema_keep = 0.9


def split_small(small_params):
    bias_in = small_params[0:HID]
    attention = small_params[HID : 3 * HID].reshape(2, HEADS, HSIZE)
    bias_one = small_params[3 * HID : 4 * HID]
    bias_two = small_params[4 * HID : 4 * HID + HSIZE]
    bias_out = small_params[4 * HID + HSIZE :]
    return (bias_in, attention, bias_one, bias_two, bias_out)


GRAPH = 64
LANES = 128
DEG = 8
SLOTS = DEG + 1
WAYS = 4
ROWS = 1280
GROUPS = 8
IN_G = FEAT // GROUPS
GAT_G = HID // GROUPS
OUT_G = HSIZE // GROUPS
TAIL_G = IN_G + 4 * GAT_G
PACK_G = TAIL_G + 2 * OUT_G
HALO_G = PACK_G + 16
CODES = slice(HID - LANES, HID)
PIECE = ROWS // 8
HALF = GRAPH // 2
ROW_IN = 4 * HID
ROW_OUT = ROW_IN + FEAT
ROW_MISC = ROW_OUT + HSIZE

bf16 = jnp.bfloat16
f32 = jnp.float32


def dot_nn(a, b):
    return lax.dot_general(a, b, (((1,), (0,)), ((), ())), preferred_element_type=f32)


def dot_nt(a, b):
    return lax.dot_general(a, b, (((1,), (1,)), ((), ())), preferred_element_type=f32)


def tile_of(k):
    return slice(k * LANES, (k + 1) * LANES)


def head_of(h):
    return slice(h * HSIZE, (h + 1) * HSIZE)


def row_of(ref, micro, width):
    picked = ref[0:1, 0:width]
    for other in range(1, ref.shape[0]):
        picked = jnp.where(micro == other, ref[other : other + 1, 0:width], picked)
    return picked


def pack_kernel(
    section_ref,
    feat_ref,
    src_ref,
    lab_ref,
    msk_ref,
    send_ref,
    win_ref,
    wgat_ref,
    wout_ref,
    pack_ref,
    tail_ref,
):
    micro = section_ref[0]
    nodes = lab_ref.shape[1]
    pack_ref[PACK_G:HALO_G, 0:FEAT] = feat_ref[0, 0:16]
    pack_ref[PACK_G:HALO_G, FEAT : 2 * FEAT] = feat_ref[0, 16:32]
    shift = LANES - HALF
    tail_ref[...] = jnp.zeros_like(tail_ref)
    far = src_ref[0]
    far = jnp.where(far >= nodes, far - nodes + GRAPH, far)
    tail_ref[0:DEG, CODES] = pltpu.roll(far, shift, 1).astype(f32)
    tail_ref[DEG : DEG + 1, CODES] = pltpu.roll(row_of(lab_ref, micro, LANES), shift, 1).astype(f32)
    tail_ref[DEG + 1 : DEG + 2, CODES] = pltpu.roll(row_of(msk_ref, micro, LANES), shift, 1).astype(f32)
    send = row_of(send_ref, micro, 2 * HALF)
    tail_ref[DEG + 2 : DEG + 3, CODES] = jnp.concatenate([send, send], axis=1).astype(f32)
    if win_ref.shape[0] != IN_G:
        pack_ref[0:TAIL_G, :] = jnp.zeros((TAIL_G, HID), bf16)
        pack_ref[TAIL_G:PACK_G, :] = tail_ref[...].astype(bf16)
        return
    pack_ref[0:IN_G, :] = win_ref[...].astype(bf16)
    for layer in range(2):
        for side in range(2):
            start = IN_G + (2 * layer + side) * GAT_G
            pack_ref[start : start + GAT_G, :] = wgat_ref[layer, side].astype(bf16)
    tail_ref[0:OUT_G, 0:CLASSES] = wout_ref[...]
    count = jnp.sum(jnp.sum(msk_ref[...].astype(f32), axis=1, keepdims=True), axis=0, keepdims=True)
    high = jnp.floor(count * (1.0 / 256.0))
    lane = lax.broadcasted_iota(jnp.int32, (1, LANES), 1)
    low = jnp.where(lane == 1, count - 256.0 * high, 0.0)
    tail_ref[OUT_G : OUT_G + 1, 0:LANES] = jnp.where(lane == 0, high, low)
    pack_ref[TAIL_G:PACK_G, :] = tail_ref[...].astype(bf16)


def vmem(count):
    return [pl.BlockSpec(memory_space=pltpu.VMEM)] * count


def pack_inputs(section_id, features, src_all, labels, label_mask, send_index, w_in, w_gat, w_out):
    grid_spec = pltpu.PrefetchScalarGridSpec(
        num_scalar_prefetch=1,
        grid=(1,),
        in_specs=[
            pl.BlockSpec((1, HALF, FEAT), lambda i, m: (m[0], 0, 0)),
            pl.BlockSpec((1, DEG, LANES), lambda i, m: (m[0], 0, 0)),
        ]
        + vmem(6),
        out_specs=vmem(1)[0],
        scratch_shapes=[pltpu.VMEM((2 * OUT_G, HID), f32)],
    )
    return pl.pallas_call(
        pack_kernel,
        grid_spec=grid_spec,
        out_shape=jax.ShapeDtypeStruct((HALO_G, HID), bf16),
        compiler_params=pltpu.CompilerParams(vmem_limit_bytes=60 * 1024 * 1024),
        name="pack",
    )(section_id, features, src_all, labels, label_mask, send_index, w_in, w_gat, w_out)


def crossed(value, axis, mask):
    return lax.ppermute(value, axis, [(i, i ^ mask) for i in range(lax.axis_size(axis))])


def gather_weights(dom_id, packed, w_in, w_gat, w_out, label_mask):
    size = lax.axis_size("dom")
    if size == GROUPS:
        near = [packed] + [crossed(packed, "dom", 2 * j) for j in range(1, 4)]
        return near + [crossed(piece, "dom", 1) for piece in near], dom_id
    halo = lax.ppermute(packed[TAIL_G:], "dom", [((i + 1) % size, i) for i in range(size)])
    halo = jnp.broadcast_to(halo[None], (GROUPS,) + halo.shape)
    rows_in, rows_gat, rows_out = (w_in.shape[0], w_gat.shape[2], w_out.shape[0])
    count = jnp.sum(label_mask)
    digits = jnp.stack([lax.div(count, 256), lax.rem(count, 256)]).astype(bf16)
    packed = jnp.concatenate(
        [
            w_in.astype(bf16),
            w_gat.astype(bf16).reshape(4 * rows_gat, HID),
            jnp.pad(w_out.astype(bf16), ((0, 0), (0, HID - CLASSES))),
            jnp.pad(digits[None, :], ((0, 0), (0, HID - 2))),
        ],
        axis=0,
    )
    whole = lax.all_gather(packed, "dom", axis=0, tiled=False)
    cut = rows_in + 4 * rows_gat
    part_in = whole[:, :rows_in].reshape(GROUPS, IN_G, HID)
    part_gat = whole[:, rows_in:cut].reshape(GROUPS, size // GROUPS, 4, rows_gat, HID)
    part_gat = part_gat.transpose(0, 2, 1, 3, 4).reshape(GROUPS, 4 * GAT_G, HID)
    part_out = whole[:, cut : cut + rows_out].reshape(GROUPS, OUT_G, HID)
    counts = whole[:, cut + rows_out].reshape(GROUPS, size // GROUPS, HID)
    counts = jnp.pad(counts, ((0, 0), (0, OUT_G - size // GROUPS), (0, 0)))
    tail = jnp.concatenate([part_out, counts], axis=1)
    tail = jnp.concatenate([tail[:, :, :LANES], halo[:, : 2 * OUT_G, LANES:]], axis=2)
    whole = jnp.concatenate([part_in, part_gat, tail, halo[:, 2 * OUT_G :]], axis=1)
    return [whole[g] for g in (0, 2, 4, 6, 1, 3, 5, 7)], dom_id * 0


def column_of(row):
    return jnp.broadcast_to(row.reshape(1, -1), (LANES, row.shape[0])).T


def model_kernel(
    section_ref,
    dom_ref,
    spot_ref,
    feat_ref,
    src_ref,
    lab_ref,
    msk_ref,
    send_ref,
    piece_0,
    piece_1,
    piece_2,
    piece_3,
    piece_4,
    piece_5,
    piece_6,
    piece_7,
    small_ref,
    keep_ref,
    send_out_ref,
    e_ref,
    t_ref,
    al_ref,
    att_ref,
    h_ref,
    slope_ref,
    both_ref,
    do_ref,
    pool_ref,
    dlog_ref,
    w_ref,
    sum_ref,
    a_ref,
    da_ref,
    gb_ref,
    loss_ref,
    node_ref,
    edge_ref,
    mark_ref,
    wi_ref,
    wgt_ref,
    wg_ref,
    wo_ref,
    wof_ref,
    am_ref,
    out_ref,
    eye_ref,
    halo_ref,
):
    nodes = feat_ref.shape[1]
    blocks = nodes // LANES
    chunk = 4 * LANES
    chunks = nodes // chunk
    mixed = DEG * LANES
    micro = section_ref[0]
    after = jnp.bitwise_and(spot_ref[0] + 1, GROUPS - 1)
    final = nodes - LANES

    digits = jnp.zeros((OUT_G, LANES), f32)
    pieces = (piece_0, piece_1, piece_2, piece_3, piece_4, piece_5, piece_6, piece_7)
    for j, piece in enumerate(pieces):
        group = jnp.bitwise_xor(spot_ref[0], 2 * (j & 3) + (j >> 2))

        def rows_of(width):
            return pl.ds(pl.multiple_of(group * width, width), width)

        wi_ref[rows_of(IN_G), :] = piece[0:IN_G, :]
        for layer in range(2):
            for side in range(2):
                start = IN_G + (2 * layer + side) * GAT_G
                wg_ref[layer, rows_of(GAT_G), side * HID : (side + 1) * HID] = piece[start : start + GAT_G, :]
        tail = piece[TAIL_G:PACK_G, :].astype(f32)
        wof_ref[rows_of(OUT_G), :] = tail[0:OUT_G, 0:LANES]
        digits = digits + tail[OUT_G : 2 * OUT_G, 0:LANES]
        halo_ref[group] = piece[TAIL_G:HALO_G, :]

    node_ref[0 : nodes - HALF, :] = feat_ref[0, HALF:nodes, :]
    node_ref[nodes - HALF : nodes - 16, :] = halo_ref[after, 16:32, 0:FEAT]
    node_ref[nodes - 16 : nodes, :] = halo_ref[after, 16:32, FEAT : 2 * FEAT]
    ints = halo_ref[after, 0:16, CODES].astype(f32).astype(jnp.int32)
    lane_row = lax.broadcasted_iota(jnp.int32, (1, LANES), 1)
    kept = lane_row < LANES - HALF
    edge_ref[...] = pltpu.roll(src_ref[0], nodes - HALF, 1)
    edge_ref[:, final:nodes] = jnp.where(
        kept,
        edge_ref[:, final:nodes],
        jnp.where(ints[0:DEG] >= GRAPH, ints[0:DEG] + (nodes - GRAPH), ints[0:DEG]),
    )
    for place, ref in enumerate((lab_ref, msk_ref)):
        mark_ref[place : place + 1, :] = pltpu.roll(row_of(ref, micro, nodes), nodes - HALF, 1)
        came = ints[DEG + place : DEG + place + 1]
        mark_ref[place : place + 1, final:nodes] = jnp.where(kept, mark_ref[place : place + 1, final:nodes], came)
    send = row_of(send_ref, micro, 2 * HALF)
    send = jnp.concatenate([send, send], axis=1)
    arrived = pltpu.roll(ints[DEG + 2 : DEG + 3], HALF, 1)
    table = jnp.where(
        lane_row < HALF, pltpu.roll(send, HALF, 1) - (nodes - HALF), arrived + HALF
    )
    spot_row = lax.broadcasted_iota(jnp.int32, (GRAPH, LANES), 0)
    spot_lane = lax.broadcasted_iota(jnp.int32, (GRAPH, LANES), 1)
    table = jnp.sum(jnp.where(spot_row == spot_lane, table.astype(f32), 0.0), axis=1, keepdims=True)
    looked = []
    for k in range(DEG):
        far = edge_ref[k : k + 1, final:nodes] - nodes == spot_row
        looked.append(jnp.sum(jnp.where(far, table, 0.0), axis=0, keepdims=True))
    looked = jnp.concatenate(looked, axis=0).astype(jnp.int32)
    raw = edge_ref[:, final:nodes]
    looked = jnp.where(raw >= nodes, looked, jnp.bitwise_and(raw - HALF, GRAPH - 1))
    local = jnp.bitwise_and(edge_ref[...] - HALF, GRAPH - 1)
    lane_all = lax.broadcasted_iota(jnp.int32, (DEG, nodes), 1)
    second = jnp.bitwise_and(lane_all, GRAPH)
    edge_ref[...] = local + second
    edge_ref[:, final:nodes] = looked + jnp.bitwise_and(
        lax.broadcasted_iota(jnp.int32, (DEG, LANES), 1), GRAPH
    )

    for layer in range(2):
        for side in range(2):
            wgt_ref[layer, side * HID : (side + 1) * HID, :] = wg_ref[
                layer, :, side * HID : (side + 1) * HID
            ].T
    wi_t = wi_ref[...].T
    wo_ref[...] = wof_ref[:, 0:CLASSES].astype(bf16)
    wo_t = wof_ref[...].T[0:CLASSES].astype(bf16)
    digits = jnp.sum(digits, axis=0, keepdims=True)
    inv_count = 1.0 / (digits[:, 0:1] * 256.0 + digits[:, 1:2])

    row_id = lax.broadcasted_iota(jnp.int32, (LANES, LANES), 0)
    lane_id = lax.broadcasted_iota(jnp.int32, (LANES, LANES), 1)
    eye = jnp.where(row_id == lane_id, 1.0, 0.0).astype(bf16)
    head_row = lax.broadcasted_iota(jnp.int32, (16, HID), 0)
    head_col = lax.broadcasted_iota(jnp.int32, (16, HID), 1)
    head_mask = jnp.where(head_col // HSIZE == head_row, 1.0, 0.0)

    bias_in = column_of(small_ref[0:HID])[:, 0:1]
    bias_one = column_of(small_ref[3 * HID : 4 * HID])[:, 0:1]
    bias_two = column_of(small_ref[4 * HID : 4 * HID + HSIZE])[:, 0:1]
    bias_out = column_of(small_ref[4 * HID + HSIZE : SMALL])[:, 0:1]
    for layer in range(2):
        row = small_ref[(1 + layer) * HID : (2 + layer) * HID]
        a_ref[layer] = column_of(row)
        row = row.reshape(1, HID)
        high = row.astype(bf16).astype(f32)
        am_ref[layer] = jnp.concatenate([head_mask[0:8] * high, head_mask[0:8] * (row - high)], axis=0).astype(bf16)
    fold_row = lax.broadcasted_iota(jnp.int32, (16, HEADS * 16), 0)
    fold_col = lax.broadcasted_iota(jnp.int32, (16, HEADS * 16), 1)
    fold = jnp.where(fold_col // 16 == fold_row, 1.0, 0.0).astype(bf16)
    spots = lax.broadcasted_iota(jnp.int32, (GRAPH, LANES), 0).astype(f32).astype(bf16)
    spots = spots.reshape(4, 16, LANES)
    half_lane = lax.broadcasted_iota(jnp.int32, (16, LANES), 1)
    first_half = (half_lane < GRAPH).astype(f32).astype(bf16)[None] > 0
    own_spot = jnp.bitwise_and(half_lane, GRAPH - 1).astype(f32).astype(bf16)
    zero = jnp.zeros((4, 16, LANES), bf16)
    da_ref[...] = jnp.zeros_like(da_ref)
    gb_ref[...] = jnp.zeros_like(gb_ref)
    loss_ref[...] = jnp.zeros_like(loss_ref)

    def lanes_of(i, width):
        return pl.ds(pl.multiple_of(i * width, width), width)

    @pl.loop(0, chunks, unroll=4)
    def _(c):
        at = lanes_of(c, chunk)
        pre = dot_nt(wi_t, node_ref[at, :]) + bias_in
        grown = jnp.exp(jnp.minimum(pre, 0.0))
        h_ref[0, :, at] = jnp.where(pre > 0, pre, grown - 1.0).astype(bf16)
        slope_ref[0, :, at] = jnp.where(pre > 0, 1.0, grown)

    wide_spots = lax.broadcasted_iota(jnp.int32, (LANES, LANES), 0).astype(f32).astype(bf16)
    wide_spots = wide_spots.reshape(8, 16, LANES)
    for k in range(DEG):
        eye_ref[:, tile_of(k)] = eye

    @pl.loop(0, blocks)
    def _(i):
        at = lanes_of(i, LANES)
        for k in range(DEG):
            spot = jnp.broadcast_to(edge_ref[k : k + 1, at].astype(f32), (16, LANES)).astype(bf16)
            hit = wide_spots == spot[None]
            hit = jnp.where(hit, jnp.ones((8, 16, LANES), bf16), jnp.zeros((8, 16, LANES), bf16))
            e_ref[i, :, tile_of(k)] = hit.reshape(LANES, LANES)

    for layer in range(2):

        @pl.loop(0, chunks, unroll=4)
        def _(c):
            at = lanes_of(c, chunk)
            both_ref[layer, :, at] = dot_nn(wgt_ref[layer], h_ref[layer, :, at]).astype(bf16)

        @pl.loop(0, blocks // WAYS)
        def _(step):
            ids = [step * WAYS + u for u in range(WAYS)]
            ats = [lanes_of(i, LANES) for i in ids]
            ways = range(WAYS)
            left = [both_ref[layer, 0:HID, ats[u]] for u in ways]
            grown = []
            for u in ways:
                right = both_ref[layer, HID : 2 * HID, ats[u]]
                left_f = left[u].astype(f32)
                mixed_rows = jnp.concatenate([jnp.take_along_axis(left_f, jnp.broadcast_to(edge_ref[k : k + 1, ats[u]], (HID, LANES)), axis=1, mode='promise_in_bounds').astype(bf16) for k in range(DEG)],axis=1)
                mixed_rows = mixed_rows + jnp.concatenate([right] * DEG, axis=1)
                own = left[u] + right
                t_ref[layer, ids[u], :, 0:mixed] = mixed_rows
                t_ref[layer, ids[u], :, tile_of(DEG)] = own
                t = jnp.concatenate([mixed_rows, own], axis=1)
                z = jnp.maximum(t, t * leak_slope)
                scores = dot_nn(am_ref[layer], z)
                grown.append(jnp.exp(scores[0:8] + scores[8:16]))
            grids_all = []
            for u in ways:
                total = grown[u][:, tile_of(0)]
                for k in range(1, SLOTS):
                    total = total + grown[u][:, tile_of(k)]
                inverse = 1.0 / total
                grids = [zero] * HEADS
                for k in range(SLOTS):
                    alpha = grown[u][:, tile_of(k)] * inverse
                    al_ref[layer, ids[u], :, tile_of(k)] = alpha
                    if k == DEG:
                        spot = own_spot
                    else:
                        spot = jnp.bitwise_and(edge_ref[k : k + 1, ats[u]], GRAPH - 1).astype(f32)
                        spot = jnp.broadcast_to(spot, (16, LANES)).astype(bf16)
                    hit = spots == spot[None]
                    for h in range(HEADS):
                        part = jnp.broadcast_to(alpha[h : h + 1], (16, LANES)).astype(bf16)
                        grids[h] = grids[h] + jnp.where(hit, part[None], zero)
                grids_all.append(grids)
            for u in ways:
                pooled = None
                for h in range(HEADS):
                    upper = jnp.where(first_half, grids_all[u][h], zero).reshape(GRAPH, LANES)
                    lower = jnp.where(first_half, zero, grids_all[u][h]).reshape(GRAPH, LANES)
                    grid = jnp.concatenate([upper, lower], axis=0)
                    att_ref[layer, ids[u], h] = grid
                    total = dot_nn(left[u][head_of(h)], grid)
                    if layer == 0:
                        pre = total + bias_one[head_of(h)]
                        grown_one = jnp.exp(jnp.minimum(pre, 0.0))
                        h_ref[1, head_of(h), ats[u]] = jnp.where(pre > 0, pre, grown_one - 1.0).astype(bf16)
                        slope_ref[1, head_of(h), ats[u]] = jnp.where(pre > 0, 1.0, grown_one)
                    else:
                        rounded = total.astype(bf16).astype(f32)
                        pooled = rounded if pooled is None else pooled + rounded
                if layer == 1:
                    pool_ref[:, ats[u]] = (pooled * (1.0 / HEADS) + bias_two).astype(bf16)

    @pl.loop(0, chunks, unroll=4)
    def _(c):
        at = lanes_of(c, chunk)
        logits = dot_nn(wo_t, pool_ref[:, at]) + bias_out
        shifted = logits - jnp.max(logits, axis=0, keepdims=True)
        log_prob = shifted - jnp.log(jnp.sum(jnp.exp(shifted), axis=0, keepdims=True))
        class_id = lax.broadcasted_iota(jnp.int32, (CLASSES, chunk), 0)
        onehot = jnp.where(class_id == mark_ref[0:1, at], 1.0, 0.0)
        share = mark_ref[1:2, at].astype(f32) * inv_count
        term = jnp.sum(((smooth - 1.0) * onehot - smooth / CLASSES) * log_prob, axis=0, keepdims=True)
        loss_ref[...] += term * share
        d_logits = (jnp.exp(log_prob) - (1.0 - smooth) * onehot - smooth / CLASSES) * share
        d_logits = d_logits.astype(bf16)
        dlog_ref[:, at] = d_logits
        d_pooled = (dot_nn(wo_ref[...], d_logits) * (1.0 / HEADS)).astype(bf16)
        for h in range(HEADS):
            do_ref[head_of(h), at] = d_pooled

    for layer in (1, 0):

        @pl.loop(0, blocks // WAYS)
        def _(step):
            ids = [step * WAYS + u for u in range(WAYS)]
            ats = [lanes_of(i, LANES) for i in ids]
            ways = range(WAYS)
            d_out = [do_ref[:, ats[u]] for u in ways]
            d_alpha = []
            for u in ways:
                for h in range(HEADS):
                    d_head = d_out[u][head_of(h)].reshape(4, 16, LANES)
                    for k in range(SLOTS):
                        t = t_ref[layer, ids[u], head_of(h), tile_of(k)].reshape(4, 16, LANES)
                        product = t * d_head
                        sum_ref[u, h * 16 : (h + 1) * 16, tile_of(k)] = (product[0] + product[1]) + (
                            product[2] + product[3]
                        )
                d_alpha.append(dot_nn(fold, sum_ref[u])[0:8])
            for u in ways:
                alpha = al_ref[layer, ids[u]]
                weighted = alpha * d_alpha[u]
                total = weighted[:, tile_of(0)]
                for k in range(1, SLOTS):
                    total = total + weighted[:, tile_of(k)]
                for k in range(SLOTS):
                    d_score = weighted[:, tile_of(k)] - alpha[:, tile_of(k)] * total
                    for h in range(HEADS):
                        one = jnp.broadcast_to(d_score[h : h + 1], (16, LANES))
                        two = (one * leak_slope).astype(bf16)[None]
                        one = one.astype(bf16)[None]
                        t = t_ref[layer, ids[u], head_of(h), tile_of(k)].reshape(4, 16, LANES)
                        w_ref[u, head_of(h), tile_of(k)] = jnp.where(t > 0, one, two).reshape(HSIZE, LANES)
            for u in ways:
                together = jnp.concatenate([e_ref[ids[u]], eye_ref[...]], axis=0)
                spread = dot_nt(w_ref[u, :, 0:mixed], together)
                own = w_ref[u, :, tile_of(DEG)].astype(f32)
                left_w = spread[:, 0:LANES] + own
                right_w = spread[:, LANES : 2 * LANES] + own
                left = both_ref[layer, 0:HID, ats[u]].astype(f32)
                right = both_ref[layer, HID : 2 * HID, ats[u]].astype(f32)
                da_ref[layer] += left * left_w + right * right_w
                wide = a_ref[layer]
                for h in range(HEADS):
                    passed = dot_nt(d_out[u][head_of(h)], att_ref[layer, ids[u], h])
                    d_left = wide[head_of(h)] * left_w[head_of(h)] + passed
                    both_ref[1 + layer, head_of(h), ats[u]] = d_left.astype(bf16)
                both_ref[1 + layer, HID : 2 * HID, ats[u]] = (wide * right_w).astype(bf16)

        @pl.loop(0, chunks, unroll=4)
        def _(c):
            at = lanes_of(c, chunk)
            d_in = dot_nn(wg_ref[layer], both_ref[1 + layer, :, at]).astype(bf16).astype(f32)
            d_in = d_in * slope_ref[layer, :, at]
            do_ref[:, at] = d_in.astype(bf16)
            if layer == 1:
                for k in range(4):
                    gb_ref[...] += d_in[:, tile_of(k)]

    for layer in range(2):
        for side in range(2):
            start = (2 * layer + side) * HID
            out_ref[start : start + HID, :] = dot_nt(
                h_ref[layer], both_ref[1 + layer, side * HID : (side + 1) * HID, :]
            ).astype(bf16)
    out_ref[ROW_IN : ROW_IN + FEAT, :] = dot_nn(do_ref[...], node_ref[...]).T.astype(bf16)
    out_ref[ROW_OUT : ROW_OUT + HSIZE, :] = jnp.zeros((HSIZE, HID), bf16)
    out_ref[ROW_OUT : ROW_OUT + HSIZE, 0:CLASSES] = dot_nt(pool_ref[...], dlog_ref[...]).astype(bf16)
    ones = jnp.ones((nodes, LANES), bf16)
    lane_wide = lax.broadcasted_iota(jnp.int32, (HID, LANES), 1)
    columns = jnp.where(lane_wide == 0, dot_nn(do_ref[...], ones), 0.0)
    for layer in range(2):
        da = jnp.sum(da_ref[layer], axis=1, keepdims=True)
        columns = columns + jnp.where(lane_wide == 1 + layer, da, 0.0)
    columns = columns + jnp.where(lane_wide == 3, jnp.sum(gb_ref[...], axis=1, keepdims=True), 0.0)
    g_bias_out = dot_nn(dlog_ref[...], ones)
    g_bias_two = lax.dot_general(
        wo_ref[...].astype(f32), g_bias_out, (((1,), (0,)), ((), ())),
        precision=highest, preferred_element_type=f32,
    )
    loss = jnp.broadcast_to(jnp.sum(loss_ref[...], axis=1, keepdims=True), (8, LANES))
    loss_high = loss.astype(bf16).astype(f32)
    rest = HID - HSIZE - CLASSES - 16
    last = jnp.concatenate(
        [g_bias_two, g_bias_out, loss_high, loss - loss_high, jnp.zeros((rest, LANES), f32)], axis=0
    )
    columns = columns + jnp.where(lane_wide == 4, last, 0.0)
    out_ref[ROW_MISC : ROW_MISC + 16, :] = columns.T[0:16].astype(bf16)
    out_ref[ROW_MISC + 16 :, :] = jnp.zeros((ROWS - ROW_MISC - 16, HID), bf16)
    core = jnp.bitwise_and(dom_ref[0], 1)
    width = ROWS // 2
    keep_ref[...] = out_ref[pl.ds(pl.multiple_of(core * width, width), width), :]
    send_out_ref[...] = out_ref[pl.ds(pl.multiple_of((1 - core) * width, width), width), :]


def run_model(section_id, dom_id, spot, features, src_all, labels, label_mask, send_index, pieces, small_params):
    nodes = features.shape[1]
    blocks = nodes // LANES
    scratch = [
        pltpu.VMEM((blocks, LANES, DEG * LANES), bf16),
        pltpu.VMEM((2, blocks, HID, SLOTS * LANES), bf16),
        pltpu.VMEM((2, blocks, 8, SLOTS * LANES), f32),
        pltpu.VMEM((2, blocks, HEADS, LANES, LANES), bf16),
        pltpu.VMEM((2, HID, nodes), bf16),
        pltpu.VMEM((2, HID, nodes), f32),
        pltpu.VMEM((3, 2 * HID, nodes), bf16),
        pltpu.VMEM((HID, nodes), bf16),
        pltpu.VMEM((HSIZE, nodes), bf16),
        pltpu.VMEM((CLASSES, nodes), bf16),
        pltpu.VMEM((WAYS, HID, SLOTS * LANES), bf16),
        pltpu.VMEM((WAYS, HEADS * 16, SLOTS * LANES), bf16),
        pltpu.VMEM((2, HID, LANES), f32),
        pltpu.VMEM((2, HID, LANES), f32),
        pltpu.VMEM((HID, LANES), f32),
        pltpu.VMEM((1, 4 * LANES), f32),
        pltpu.VMEM((nodes, FEAT), bf16),
        pltpu.VMEM((DEG, nodes), jnp.int32),
        pltpu.VMEM((8, nodes), jnp.int32),
        pltpu.VMEM((FEAT, HID), bf16),
        pltpu.VMEM((2, 2 * HID, HID), bf16),
        pltpu.VMEM((2, HID, 2 * HID), bf16),
        pltpu.VMEM((HSIZE, CLASSES), bf16),
        pltpu.VMEM((HSIZE, LANES), f32),
        pltpu.VMEM((2, 16, HID), bf16),
        pltpu.VMEM((ROWS, HID), bf16),
        pltpu.VMEM((LANES, DEG * LANES), bf16),
        pltpu.VMEM((GROUPS, 32, HID), bf16),
    ]
    grid_spec = pltpu.PrefetchScalarGridSpec(
        num_scalar_prefetch=3,
        grid=(1,),
        in_specs=[
            pl.BlockSpec((1, nodes, FEAT), lambda i, m, d, p: (m[0], 0, 0)),
            pl.BlockSpec((1, DEG, nodes), lambda i, m, d, p: (m[0], 0, 0)),
        ]
        + vmem(12),
        out_specs=vmem(2),
        scratch_shapes=scratch,
    )
    return pl.pallas_call(
        model_kernel,
        grid_spec=grid_spec,
        out_shape=[jax.ShapeDtypeStruct((ROWS // 2, HID), bf16)] * 2,
        compiler_params=pltpu.CompilerParams(vmem_limit_bytes=50 * 1024 * 1024),
        name="model",
    )(section_id, dom_id, spot, features, src_all, labels, label_mask, send_index, *pieces, small_params)


def settled(total, is_last):
    base = ROW_MISC % PIECE
    block = total[base : base + 8]
    row = lax.broadcasted_iota(jnp.int32, (8, HID), 0)
    lane = lax.broadcasted_iota(jnp.int32, (8, HID), 1)
    spot = HSIZE + CLASSES
    joined = block + pltpu.roll(block, HID - 8, 1)
    high = joined.astype(bf16).astype(f32)
    low = pltpu.roll(joined - high, 8, 1)
    here = (row == 4) & (lane >= spot) & (lane < spot + 16) & (is_last == 1)
    block = jnp.where(here, jnp.where(lane < spot + 8, high, low), block)
    return jnp.concatenate([total[:base], block, total[base + 8 :]], axis=0).astype(bf16)


def last_piece(core, section):
    return jnp.where((core == 1) & (section == 3), 1, 0)


def split_kernel(section_ref, dom_ref, keep_ref, got_ref, *out_refs):
    section = section_ref[0]
    core = jnp.bitwise_and(dom_ref[0], 1)
    for j, out_ref in enumerate(out_refs):
        part = jnp.bitwise_xor(section, j)
        at = pl.ds(pl.multiple_of(part * PIECE, PIECE), PIECE)
        total = keep_ref[at, :].astype(f32) + got_ref[at, :].astype(f32)
        out_ref[...] = settled(total, last_piece(core, part))


def join_kernel(section_ref, dom_ref, own_ref, one_ref, two_ref, three_ref, out_ref):
    pair = own_ref[...].astype(f32) + one_ref[...].astype(f32)
    other = two_ref[...].astype(f32) + three_ref[...].astype(f32)
    core = jnp.bitwise_and(dom_ref[0], 1)
    out_ref[...] = settled(pair + other, last_piece(core, section_ref[0]))


def small_call(kernel, name, ids, count, operands):
    shape = jax.ShapeDtypeStruct((PIECE, HID), bf16)
    return pl.pallas_call(
        kernel,
        out_shape=[shape] * count if count > 1 else shape,
        in_specs=[pl.BlockSpec(memory_space=pltpu.SMEM)] * 2 + vmem(len(operands)),
        out_specs=vmem(count) if count > 1 else vmem(1)[0],
        compiler_params=pltpu.CompilerParams(vmem_limit_bytes=8 * 1024 * 1024),
        name=name,
    )(*ids, *operands)


def sum_gradients(ids, keep, send):
    if lax.axis_size("dom") == 8 and lax.axis_size("section") == 4:
        got = crossed(send, "dom", 1)
        parts = small_call(split_kernel, "split", ids, 4, (keep, got))
        came = [crossed(parts[j], "section", j) for j in range(1, 4)]
        mine = small_call(join_kernel, "join", ids, 1, (parts[0], *came))
        came = [crossed(mine, "dom", 2 * j) for j in range(1, 4)]
        mine = small_call(join_kernel, "join", ids, 1, (mine, *came))
        near = [mine] + [crossed(mine, "section", j) for j in range(1, 4)]
        return near + [crossed(piece, "dom", 1) for piece in near], ids
    all_size = lax.axis_size("dom") * lax.axis_size("section")
    swap = jnp.bitwise_and(ids[1][0], 1) == 1
    partial = jnp.concatenate([jnp.where(swap, send, keep), jnp.where(swap, keep, send)], axis=0)
    parts = lax.all_to_all(partial.reshape(all_size, -1, HID), ("section", "dom"), 0, 0)
    mine = jnp.sum(parts.astype(f32), axis=0)
    shared = jnp.broadcast_to(mine.astype(bf16)[None], (all_size,) + mine.shape)
    summed = lax.all_to_all(shared, ("section", "dom"), 0, 0).reshape(8, PIECE, HID)
    return [summed[j] for j in range(8)], (ids[0] * 0, ids[1] * 0)


def adamw_step(parameter, gradient, moment_one, moment_two):
    moment_one = beta_one * moment_one + (1.0 - beta_one) * gradient
    moment_two = beta_two * moment_two + (1.0 - beta_two) * gradient * gradient
    corr_one = 1.0 - beta_one**STEPS
    corr_two = 1.0 - beta_two**STEPS
    update = moment_one / corr_one / (jnp.sqrt(moment_two / corr_two) + adam_eps)
    return (parameter - adam_rate * (update + adam_decay * parameter), moment_one, moment_two)


def average(old_value, new_value):
    return ema_keep * old_value + (1.0 - ema_keep) * new_value


def dot_tn(a, b):
    return lax.dot_general(a, b, (((0,), (0,)), ((), ())), preferred_element_type=f32)


def halves(value):
    high = value.astype(bf16)
    return high, (value - high.astype(f32)).astype(bf16)


def wide_rows(total):
    return max(total, 16)


def own_rows(gradient, start, count):
    total = gradient.shape[0]
    row = lax.broadcasted_iota(jnp.int32, (wide_rows(count), total), 0) + start
    lane = lax.broadcasted_iota(jnp.int32, (wide_rows(count), total), 1)
    pick = jnp.where(row == lane, 1.0, 0.0).astype(bf16)
    return dot_nn(pick, gradient).astype(bf16)


def precondition(gradient, weight, stat_l, stat_r, root_l, root_r, ema, outs, scale, start):
    (new_w, new_l, new_r, new_ema) = outs
    count = weight.shape[0]
    square = (1.0 - shampoo_decay) * scale * scale
    mine = own_rows(gradient, start, count)
    new_l[...] = shampoo_decay * stat_l + square * dot_nt(mine, gradient)[0:count]
    new_r[...] = shampoo_decay * stat_r + square * dot_tn(gradient, gradient)
    high, low = halves(root_l)
    middle = dot_nn(high, gradient) + dot_nn(low, gradient)
    m_high, m_low = halves(middle * scale)
    r_high, r_low = halves(root_r)
    update = dot_nn(m_high, r_high) + dot_nn(m_low, r_high) + dot_nn(m_high, r_low)
    weight = weight - shampoo_rate * (update + weight_decay * weight)
    new_w[...] = weight
    new_ema[...] = average(ema, weight)


def update_kernel(
    dom_ref,
    section_ref,
    spot_ref,
    piece_0,
    piece_1,
    piece_2,
    piece_3,
    piece_4,
    piece_5,
    piece_6,
    piece_7,
    w_in,
    w_gat,
    w_out,
    small,
    l_in,
    r_in,
    l_gat,
    r_gat,
    l_out,
    r_out,
    rl_in,
    rr_in,
    rl_gat,
    rr_gat,
    rl_out,
    rr_out,
    first,
    second,
    e_in,
    e_gat,
    e_out,
    e_small,
    n_w_in,
    n_w_gat,
    n_w_out,
    n_small,
    n_l_in,
    n_r_in,
    n_l_gat,
    n_r_gat,
    n_l_out,
    n_r_out,
    n_first,
    n_second,
    n_e_in,
    n_e_gat,
    n_e_out,
    n_e_small,
    loss_ref,
    norm_ref,
    sum_ref,
):
    dom = dom_ref[0]
    core = jnp.bitwise_and(spot_ref[0], 1)
    pieces = (piece_0, piece_1, piece_2, piece_3, piece_4, piece_5, piece_6, piece_7)
    for j, piece in enumerate(pieces):
        spot = jnp.bitwise_xor(core, j >> 2) * 4 + jnp.bitwise_xor(section_ref[0], j & 3)
        sum_ref[pl.ds(pl.multiple_of(spot * PIECE, PIECE), PIECE), :] = piece[...]
    grads = sum_ref[0:ROW_MISC, :].astype(f32)
    squares = jnp.sum(grads * grads)
    misc = sum_ref[ROW_MISC : ROW_MISC + 8, :].astype(f32)
    row = lax.broadcasted_iota(jnp.int32, (8, HID), 0)
    lane = lax.broadcasted_iota(jnp.int32, (8, HID), 1)
    spot = HSIZE + CLASSES
    loss_ref[0] = jnp.sum(jnp.where((row == 4) & ((lane == spot) | (lane == spot + 8)), misc, 0.0))
    small_part = jnp.where((row < 4) | ((row == 4) & (lane < spot)), misc, 0.0)
    squares = squares + jnp.sum(small_part * small_part)
    norm = jnp.sqrt(jnp.broadcast_to(squares, (1, 1)))
    scale = jnp.minimum(1.0, clip_norm / norm)
    norm_ref[0] = jnp.sum(norm)
    for layer in range(2):
        for side in range(2):
            at = (layer, side)
            begin = (2 * layer + side) * HID
            precondition(
                sum_ref[begin : begin + HID, :],
                w_gat[at],
                l_gat[at],
                r_gat[at],
                rl_gat[at],
                rr_gat[at],
                e_gat[at],
                (n_w_gat.at[at], n_l_gat.at[at], n_r_gat.at[at], n_e_gat.at[at]),
                scale,
                dom * w_gat.shape[2],
            )
    precondition(
        sum_ref[ROW_IN:ROW_OUT, :],
        w_in[...],
        l_in[...],
        r_in[...],
        rl_in[...],
        rr_in[...],
        e_in[...],
        (n_w_in, n_l_in, n_r_in, n_e_in),
        scale,
        dom * w_in.shape[0],
    )
    precondition(
        sum_ref[ROW_OUT:ROW_MISC, 0:CLASSES],
        w_out[...],
        l_out[...],
        r_out[...],
        rl_out[...],
        rr_out[...],
        e_out[...],
        (n_w_out, n_l_out, n_r_out, n_e_out),
        scale,
        dom * w_out.shape[0],
    )
    for place in range(5):
        width = HID if place < 4 else spot
        at = pl.ds(place * HID, width)
        gradient = misc[place : place + 1, 0:width] * scale

        def line(ref):
            return ref[at].reshape(1, width)

        new_value, moment_one, moment_two = adamw_step(line(small), gradient, line(first), line(second))
        n_small[at] = new_value.reshape(width)
        n_first[at] = moment_one.reshape(width)
        n_second[at] = moment_two.reshape(width)
        n_e_small[at] = average(line(e_small), new_value).reshape(width)


def per_device(
    features,
    sources,
    send_index,
    labels,
    label_mask,
    w_in,
    w_gat,
    w_out,
    small_params,
    stat_l_in,
    stat_r_in,
    stat_l_gat,
    stat_r_gat,
    stat_l_out,
    stat_r_out,
    root_l_in,
    root_r_in,
    root_l_gat,
    root_r_gat,
    root_l_out,
    root_r_out,
    adam_first,
    adam_second,
    ema_in,
    ema_gat,
    ema_out,
    ema_small,
):
    dom_id = lax.axis_index("dom").astype(jnp.int32).reshape(1)
    section_id = lax.axis_index("section").astype(jnp.int32).reshape(1)
    src_all = jnp.swapaxes(sources, 1, 2)
    packed = pack_inputs(section_id, features, src_all, labels, label_mask, send_index, w_in, w_gat, w_out)
    pieces, spot = gather_weights(dom_id, packed, w_in, w_gat, w_out, label_mask)
    keep, send = run_model(
        section_id, dom_id, spot, features, src_all, labels, label_mask, send_index, pieces, small_params
    )
    pieces, spots = sum_gradients((section_id, dom_id), keep, send)
    state = (
        w_in,
        w_gat,
        w_out,
        small_params,
        stat_l_in,
        stat_r_in,
        stat_l_gat,
        stat_r_gat,
        stat_l_out,
        stat_r_out,
        root_l_in,
        root_r_in,
        root_l_gat,
        root_r_gat,
        root_l_out,
        root_r_out,
        adam_first,
        adam_second,
        ema_in,
        ema_gat,
        ema_out,
        ema_small,
    )
    like = state[:10] + (adam_first, adam_second, ema_in, ema_gat, ema_out, ema_small)
    results = pl.pallas_call(
        update_kernel,
        out_shape=[jax.ShapeDtypeStruct(v.shape, f32) for v in like] + [jax.ShapeDtypeStruct((1,), f32)] * 2,
        in_specs=[pl.BlockSpec(memory_space=pltpu.SMEM)] * 3 + vmem(30),
        out_specs=vmem(16) + [pl.BlockSpec(memory_space=pltpu.SMEM)] * 2,
        scratch_shapes=[pltpu.VMEM((ROWS, HID), bf16)],
        compiler_params=pltpu.CompilerParams(vmem_limit_bytes=16 * 1024 * 1024),
        name="update",
    )(dom_id, *spots, *pieces, *state)
    return tuple(results[:16]) + (results[16].reshape(()), results[17].reshape(()))


def solution(mesh):
    placed = (
        P(None, "dom", None),
        P(None, "dom", None),
        P(None, "dom"),
        P(None, "dom"),
        P(None, "dom"),
        P("dom", None),
        P(None, None, "dom", None),
        P("dom", None),
        P(),
        P("dom", None),
        P(),
        P(None, None, "dom", None),
        P(),
        P("dom", None),
        P(),
        P("dom", None),
        P(),
        P(None, None, "dom", None),
        P(),
        P("dom", None),
        P(),
        P(),
        P(),
        P("dom", None),
        P(None, None, "dom", None),
        P("dom", None),
        P(),
    )
    return jax.shard_map(
        per_device,
        mesh=mesh,
        in_specs=placed,
        out_specs=(
            P("dom", None),
            P(None, None, "dom", None),
            P("dom", None),
            P(),
            P("dom", None),
            P(),
            P(None, None, "dom", None),
            P(),
            P("dom", None),
            P(),
            P(),
            P(),
            P("dom", None),
            P(None, None, "dom", None),
            P("dom", None),
            P(),
            P(),
            P(),
        ),
        check_vma=False,
    )
```

```python
import jax
import jax.numpy as jnp
from jax import lax
from jax.experimental import pallas as pl
from jax.experimental.pallas import tpu as pltpu
from jax.sharding import PartitionSpec as P

FEAT = 128
HEADS = 4
HSIZE = 64
CLASSES = 40
STEPS = 5
HID = 256
SMALL = 1128


highest = lax.Precision.HIGHEST
leak_slope = 0.2
smooth = 0.1
clip_norm = 0.001
shampoo_rate = 0.3
shampoo_decay = 0.5
weight_decay = 0.0001
adam_rate = 0.1
beta_one = 0.9
beta_two = 0.999
adam_eps = 1e-08
adam_decay = 0.01
ema_keep = 0.9


def split_small(small_params):
    bias_in = small_params[0:HID]
    attention = small_params[HID : 3 * HID].reshape(2, HEADS, HSIZE)
    bias_one = small_params[3 * HID : 4 * HID]
    bias_two = small_params[4 * HID : 4 * HID + HSIZE]
    bias_out = small_params[4 * HID + HSIZE :]
    return (bias_in, attention, bias_one, bias_two, bias_out)


GRAPH = 64
LANES = 128
DEG = 8
SLOTS = DEG + 1
WAYS = 4
ROWS = 1280
GROUPS = 8
IN_G = FEAT // GROUPS
GAT_G = HID // GROUPS
OUT_G = HSIZE // GROUPS
TAIL_G = IN_G + 4 * GAT_G
PACK_G = TAIL_G + 2 * OUT_G
HALO_G = PACK_G + 16
CODES = slice(HID - LANES, HID)
PIECE = ROWS // 8
HALF = GRAPH // 2
ROW_IN = 4 * HID
ROW_OUT = ROW_IN + FEAT
ROW_MISC = ROW_OUT + HSIZE

bf16 = jnp.bfloat16
f32 = jnp.float32


def dot_nn(a, b):
    return lax.dot_general(a, b, (((1,), (0,)), ((), ())), preferred_element_type=f32)


def dot_nt(a, b):
    return lax.dot_general(a, b, (((1,), (1,)), ((), ())), preferred_element_type=f32)


def tile_of(k):
    return slice(k * LANES, (k + 1) * LANES)


def head_of(h):
    return slice(h * HSIZE, (h + 1) * HSIZE)


def row_of(ref, micro, width):
    picked = ref[0:1, 0:width]
    for other in range(1, ref.shape[0]):
        picked = jnp.where(micro == other, ref[other : other + 1, 0:width], picked)
    return picked


def pack_kernel(
    section_ref,
    feat_ref,
    src_ref,
    lab_ref,
    msk_ref,
    send_ref,
    win_ref,
    wgat_ref,
    wout_ref,
    pack_ref,
    tail_ref,
):
    micro = section_ref[0]
    nodes = lab_ref.shape[1]
    pack_ref[PACK_G:HALO_G, 0:FEAT] = feat_ref[0, 0:16]
    pack_ref[PACK_G:HALO_G, FEAT : 2 * FEAT] = feat_ref[0, 16:32]
    shift = LANES - HALF
    tail_ref[...] = jnp.zeros_like(tail_ref)
    far = src_ref[0]
    far = jnp.where(far >= nodes, far - nodes + GRAPH, far)
    tail_ref[0:DEG, CODES] = pltpu.roll(far, shift, 1).astype(f32)
    tail_ref[DEG : DEG + 1, CODES] = pltpu.roll(row_of(lab_ref, micro, LANES), shift, 1).astype(f32)
    tail_ref[DEG + 1 : DEG + 2, CODES] = pltpu.roll(row_of(msk_ref, micro, LANES), shift, 1).astype(f32)
    send = row_of(send_ref, micro, 2 * HALF)
    tail_ref[DEG + 2 : DEG + 3, CODES] = jnp.concatenate([send, send], axis=1).astype(f32)
    if win_ref.shape[0] != IN_G:
        pack_ref[0:TAIL_G, :] = jnp.zeros((TAIL_G, HID), bf16)
        pack_ref[TAIL_G:PACK_G, :] = tail_ref[...].astype(bf16)
        return
    pack_ref[0:IN_G, :] = win_ref[...].astype(bf16)
    for layer in range(2):
        for side in range(2):
            start = IN_G + (2 * layer + side) * GAT_G
            pack_ref[start : start + GAT_G, :] = wgat_ref[layer, side].astype(bf16)
    tail_ref[0:OUT_G, 0:CLASSES] = wout_ref[...]
    count = jnp.sum(jnp.sum(msk_ref[...].astype(f32), axis=1, keepdims=True), axis=0, keepdims=True)
    high = jnp.floor(count * (1.0 / 256.0))
    lane = lax.broadcasted_iota(jnp.int32, (1, LANES), 1)
    low = jnp.where(lane == 1, count - 256.0 * high, 0.0)
    tail_ref[OUT_G : OUT_G + 1, 0:LANES] = jnp.where(lane == 0, high, low)
    pack_ref[TAIL_G:PACK_G, :] = tail_ref[...].astype(bf16)


def vmem(count):
    return [pl.BlockSpec(memory_space=pltpu.VMEM)] * count


def pack_inputs(section_id, features, src_all, labels, label_mask, send_index, w_in, w_gat, w_out):
    grid_spec = pltpu.PrefetchScalarGridSpec(
        num_scalar_prefetch=1,
        grid=(1,),
        in_specs=[
            pl.BlockSpec((1, HALF, FEAT), lambda i, m: (m[0], 0, 0)),
            pl.BlockSpec((1, DEG, LANES), lambda i, m: (m[0], 0, 0)),
        ]
        + vmem(6),
        out_specs=vmem(1)[0],
        scratch_shapes=[pltpu.VMEM((2 * OUT_G, HID), f32)],
    )
    return pl.pallas_call(
        pack_kernel,
        grid_spec=grid_spec,
        out_shape=jax.ShapeDtypeStruct((HALO_G, HID), bf16),
        compiler_params=pltpu.CompilerParams(vmem_limit_bytes=58 * 1024 * 1024),
        name="pack",
    )(section_id, features, src_all, labels, label_mask, send_index, w_in, w_gat, w_out)


def crossed(value, axis, mask):
    return lax.ppermute(value, axis, [(i, i ^ mask) for i in range(lax.axis_size(axis))])


def gather_weights(dom_id, packed, w_in, w_gat, w_out, label_mask):
    size = lax.axis_size("dom")
    if size == GROUPS:
        near = [packed] + [crossed(packed, "dom", 2 * j) for j in range(1, 4)]
        return near + [crossed(piece, "dom", 1) for piece in near], dom_id
    halo = lax.ppermute(packed[TAIL_G:], "dom", [((i + 1) % size, i) for i in range(size)])
    halo = jnp.broadcast_to(halo[None], (GROUPS,) + halo.shape)
    rows_in, rows_gat, rows_out = (w_in.shape[0], w_gat.shape[2], w_out.shape[0])
    count = jnp.sum(label_mask)
    digits = jnp.stack([lax.div(count, 256), lax.rem(count, 256)]).astype(bf16)
    packed = jnp.concatenate(
        [
            w_in.astype(bf16),
            w_gat.astype(bf16).reshape(4 * rows_gat, HID),
            jnp.pad(w_out.astype(bf16), ((0, 0), (0, HID - CLASSES))),
            jnp.pad(digits[None, :], ((0, 0), (0, HID - 2))),
        ],
        axis=0,
    )
    whole = lax.all_gather(packed, "dom", axis=0, tiled=False)
    cut = rows_in + 4 * rows_gat
    part_in = whole[:, :rows_in].reshape(GROUPS, IN_G, HID)
    part_gat = whole[:, rows_in:cut].reshape(GROUPS, size // GROUPS, 4, rows_gat, HID)
    part_gat = part_gat.transpose(0, 2, 1, 3, 4).reshape(GROUPS, 4 * GAT_G, HID)
    part_out = whole[:, cut : cut + rows_out].reshape(GROUPS, OUT_G, HID)
    counts = whole[:, cut + rows_out].reshape(GROUPS, size // GROUPS, HID)
    counts = jnp.pad(counts, ((0, 0), (0, OUT_G - size // GROUPS), (0, 0)))
    tail = jnp.concatenate([part_out, counts], axis=1)
    tail = jnp.concatenate([tail[:, :, :LANES], halo[:, : 2 * OUT_G, LANES:]], axis=2)
    whole = jnp.concatenate([part_in, part_gat, tail, halo[:, 2 * OUT_G :]], axis=1)
    return [whole[g] for g in (0, 2, 4, 6, 1, 3, 5, 7)], dom_id * 0


def column_of(row):
    return jnp.broadcast_to(row.reshape(1, -1), (LANES, row.shape[0])).T


def model_kernel(
    section_ref,
    dom_ref,
    spot_ref,
    feat_ref,
    src_ref,
    lab_ref,
    msk_ref,
    send_ref,
    piece_0,
    piece_1,
    piece_2,
    piece_3,
    piece_4,
    piece_5,
    piece_6,
    piece_7,
    small_ref,
    keep_ref,
    send_out_ref,
    e_ref,
    t_ref,
    al_ref,
    att_ref,
    h_ref,
    slope_ref,
    both_ref,
    do_ref,
    pool_ref,
    dlog_ref,
    w_ref,
    sum_ref,
    a_ref,
    da_ref,
    gb_ref,
    loss_ref,
    node_ref,
    edge_ref,
    mark_ref,
    wi_ref,
    wgt_ref,
    wg_ref,
    wo_ref,
    wof_ref,
    am_ref,
    out_ref,
    eye_ref,
    halo_ref,
):
    nodes = feat_ref.shape[1]
    blocks = nodes // LANES
    chunk = 4 * LANES
    chunks = nodes // chunk
    mixed = DEG * LANES
    micro = section_ref[0]
    after = jnp.bitwise_and(spot_ref[0] + 1, GROUPS - 1)
    final = nodes - LANES

    digits = jnp.zeros((OUT_G, LANES), f32)
    pieces = (piece_0, piece_1, piece_2, piece_3, piece_4, piece_5, piece_6, piece_7)
    for j, piece in enumerate(pieces):
        group = jnp.bitwise_xor(spot_ref[0], 2 * (j & 3) + (j >> 2))

        def rows_of(width):
            return pl.ds(pl.multiple_of(group * width, width), width)

        wi_ref[rows_of(IN_G), :] = piece[0:IN_G, :]
        for layer in range(2):
            for side in range(2):
                start = IN_G + (2 * layer + side) * GAT_G
                wg_ref[layer, rows_of(GAT_G), side * HID : (side + 1) * HID] = piece[start : start + GAT_G, :]
        tail = piece[TAIL_G:PACK_G, :].astype(f32)
        wof_ref[rows_of(OUT_G), :] = tail[0:OUT_G, 0:LANES]
        digits = digits + tail[OUT_G : 2 * OUT_G, 0:LANES]
        halo_ref[group] = piece[TAIL_G:HALO_G, :]

    node_ref[0 : nodes - HALF, :] = feat_ref[0, HALF:nodes, :]
    node_ref[nodes - HALF : nodes - 16, :] = halo_ref[after, 16:32, 0:FEAT]
    node_ref[nodes - 16 : nodes, :] = halo_ref[after, 16:32, FEAT : 2 * FEAT]
    ints = halo_ref[after, 0:16, CODES].astype(f32).astype(jnp.int32)
    lane_row = lax.broadcasted_iota(jnp.int32, (1, LANES), 1)
    kept = lane_row < LANES - HALF
    edge_ref[...] = pltpu.roll(src_ref[0], nodes - HALF, 1)
    edge_ref[:, final:nodes] = jnp.where(
        kept,
        edge_ref[:, final:nodes],
        jnp.where(ints[0:DEG] >= GRAPH, ints[0:DEG] + (nodes - GRAPH), ints[0:DEG]),
    )
    for place, ref in enumerate((lab_ref, msk_ref)):
        mark_ref[place : place + 1, :] = pltpu.roll(row_of(ref, micro, nodes), nodes - HALF, 1)
        came = ints[DEG + place : DEG + place + 1]
        mark_ref[place : place + 1, final:nodes] = jnp.where(kept, mark_ref[place : place + 1, final:nodes], came)
    send = row_of(send_ref, micro, 2 * HALF)
    send = jnp.concatenate([send, send], axis=1)
    arrived = pltpu.roll(ints[DEG + 2 : DEG + 3], HALF, 1)
    table = jnp.where(
        lane_row < HALF, pltpu.roll(send, HALF, 1) - (nodes - HALF), arrived + HALF
    )
    spot_row = lax.broadcasted_iota(jnp.int32, (GRAPH, LANES), 0)
    spot_lane = lax.broadcasted_iota(jnp.int32, (GRAPH, LANES), 1)
    table = jnp.sum(jnp.where(spot_row == spot_lane, table.astype(f32), 0.0), axis=1, keepdims=True)
    looked = []
    for k in range(DEG):
        far = edge_ref[k : k + 1, final:nodes] - nodes == spot_row
        looked.append(jnp.sum(jnp.where(far, table, 0.0), axis=0, keepdims=True))
    looked = jnp.concatenate(looked, axis=0).astype(jnp.int32)
    raw = edge_ref[:, final:nodes]
    looked = jnp.where(raw >= nodes, looked, jnp.bitwise_and(raw - HALF, GRAPH - 1))
    local = jnp.bitwise_and(edge_ref[...] - HALF, GRAPH - 1)
    lane_all = lax.broadcasted_iota(jnp.int32, (DEG, nodes), 1)
    second = jnp.bitwise_and(lane_all, GRAPH)
    edge_ref[...] = local + second
    edge_ref[:, final:nodes] = looked + jnp.bitwise_and(
        lax.broadcasted_iota(jnp.int32, (DEG, LANES), 1), GRAPH
    )

    for layer in range(2):
        for side in range(2):
            wgt_ref[layer, side * HID : (side + 1) * HID, :] = wg_ref[
                layer, :, side * HID : (side + 1) * HID
            ].T
    wi_t = wi_ref[...].T
    wo_ref[...] = wof_ref[:, 0:CLASSES].astype(bf16)
    wo_t = wof_ref[...].T[0:CLASSES].astype(bf16)
    digits = jnp.sum(digits, axis=0, keepdims=True)
    inv_count = 1.0 / (digits[:, 0:1] * 256.0 + digits[:, 1:2])

    row_id = lax.broadcasted_iota(jnp.int32, (LANES, LANES), 0)
    lane_id = lax.broadcasted_iota(jnp.int32, (LANES, LANES), 1)
    eye = jnp.where(row_id == lane_id, 1.0, 0.0).astype(bf16)
    head_row = lax.broadcasted_iota(jnp.int32, (16, HID), 0)
    head_col = lax.broadcasted_iota(jnp.int32, (16, HID), 1)
    head_mask = jnp.where(head_col // HSIZE == head_row, 1.0, 0.0)

    bias_in = column_of(small_ref[0:HID])[:, 0:1]
    bias_one = column_of(small_ref[3 * HID : 4 * HID])[:, 0:1]
    bias_two = column_of(small_ref[4 * HID : 4 * HID + HSIZE])[:, 0:1]
    bias_out = column_of(small_ref[4 * HID + HSIZE : SMALL])[:, 0:1]
    for layer in range(2):
        row = small_ref[(1 + layer) * HID : (2 + layer) * HID]
        a_ref[layer] = column_of(row)
        row = row.reshape(1, HID)
        high = row.astype(bf16).astype(f32)
        am_ref[layer] = jnp.concatenate([head_mask[0:8] * high, head_mask[0:8] * (row - high)], axis=0).astype(bf16)
    fold_row = lax.broadcasted_iota(jnp.int32, (16, HEADS * 16), 0)
    fold_col = lax.broadcasted_iota(jnp.int32, (16, HEADS * 16), 1)
    fold = jnp.where(fold_col // 16 == fold_row, 1.0, 0.0).astype(bf16)
    spots = lax.broadcasted_iota(jnp.int32, (GRAPH, LANES), 0).astype(f32).astype(bf16)
    spots = spots.reshape(4, 16, LANES)
    half_lane = lax.broadcasted_iota(jnp.int32, (16, LANES), 1)
    first_half = (half_lane < GRAPH).astype(f32).astype(bf16)[None] > 0
    own_spot = jnp.bitwise_and(half_lane, GRAPH - 1).astype(f32).astype(bf16)
    zero = jnp.zeros((4, 16, LANES), bf16)
    da_ref[...] = jnp.zeros_like(da_ref)
    gb_ref[...] = jnp.zeros_like(gb_ref)
    loss_ref[...] = jnp.zeros_like(loss_ref)

    def lanes_of(i, width):
        return pl.ds(pl.multiple_of(i * width, width), width)

    @pl.loop(0, chunks, unroll=4)
    def _(c):
        at = lanes_of(c, chunk)
        pre = dot_nt(wi_t, node_ref[at, :]) + bias_in
        grown = jnp.exp(jnp.minimum(pre, 0.0))
        h_ref[0, :, at] = (jnp.maximum(pre, 0.0) + (grown - 1.0)).astype(bf16)
        slope_ref[0, :, at] = grown

    wide_spots = lax.broadcasted_iota(jnp.int32, (LANES, LANES), 0).astype(f32).astype(bf16)
    wide_spots = wide_spots.reshape(8, 16, LANES)
    for k in range(DEG):
        eye_ref[:, tile_of(k)] = eye

    @pl.loop(0, blocks)
    def _(i):
        at = lanes_of(i, LANES)
        for k in range(DEG):
            spot = jnp.broadcast_to(edge_ref[k : k + 1, at].astype(f32), (16, LANES)).astype(bf16)
            hit = wide_spots == spot[None]
            hit = jnp.where(hit, jnp.ones((8, 16, LANES), bf16), jnp.zeros((8, 16, LANES), bf16))
            e_ref[i, :, tile_of(k)] = hit.reshape(LANES, LANES)

    for layer in range(2):

        @pl.loop(0, chunks, unroll=4)
        def _(c):
            at = lanes_of(c, chunk)
            both_ref[layer, :, at] = dot_nn(wgt_ref[layer], h_ref[layer, :, at]).astype(bf16)

        @pl.loop(0, blocks // WAYS)
        def _(step):
            ids = [step * WAYS + u for u in range(WAYS)]
            ats = [lanes_of(i, LANES) for i in ids]
            ways = range(WAYS)
            left = [both_ref[layer, 0:HID, ats[u]] for u in ways]
            grown = []
            for u in ways:
                right = both_ref[layer, HID : 2 * HID, ats[u]]
                left_f = left[u].astype(f32)
                mixed_rows = [dot_nn(left[u], e_ref[ids[u], :, 0 : 2 * LANES]).astype(bf16)]
                for k in range(2, DEG):
                    index = jnp.broadcast_to(edge_ref[k : k + 1, ats[u]], (HID, LANES))
                    picked = jnp.take_along_axis(left_f, index, axis=1, mode="promise_in_bounds")
                    mixed_rows.append(picked.astype(bf16))
                mixed_rows = jnp.concatenate(mixed_rows, axis=1)
                mixed_rows = mixed_rows + jnp.concatenate([right] * DEG, axis=1)
                own = left[u] + right
                t_ref[layer, ids[u], :, 0:mixed] = mixed_rows
                t_ref[layer, ids[u], :, tile_of(DEG)] = own
                t = jnp.concatenate([mixed_rows, own], axis=1)
                z = jnp.maximum(t, t * leak_slope)
                scores = dot_nn(am_ref[layer], z)
                grown.append(jnp.exp(scores[0:8] + scores[8:16]))
            grids_all = []
            for u in ways:
                total = grown[u][:, tile_of(0)]
                for k in range(1, SLOTS):
                    total = total + grown[u][:, tile_of(k)]
                inverse = 1.0 / total
                grids = [zero] * HEADS
                for k in range(SLOTS):
                    alpha = grown[u][:, tile_of(k)] * inverse
                    al_ref[layer, ids[u], :, tile_of(k)] = alpha
                    if k == DEG:
                        spot = own_spot
                    else:
                        spot = jnp.bitwise_and(edge_ref[k : k + 1, ats[u]], GRAPH - 1).astype(f32)
                        spot = jnp.broadcast_to(spot, (16, LANES)).astype(bf16)
                    hit = spots == spot[None]
                    for h in range(HEADS):
                        part = jnp.broadcast_to(alpha[h : h + 1], (16, LANES)).astype(bf16)
                        grids[h] = grids[h] + jnp.where(hit, part[None], zero)
                grids_all.append(grids)
            for u in ways:
                pooled = None
                for h in range(HEADS):
                    upper = jnp.where(first_half, grids_all[u][h], zero).reshape(GRAPH, LANES)
                    lower = jnp.where(first_half, zero, grids_all[u][h]).reshape(GRAPH, LANES)
                    grid = jnp.concatenate([upper, lower], axis=0)
                    att_ref[layer, ids[u], h] = grid
                    total = dot_nn(left[u][head_of(h)], grid)
                    if layer == 0:
                        pre = total + bias_one[head_of(h)]
                        grown_one = jnp.exp(jnp.minimum(pre, 0.0))
                        h_ref[1, head_of(h), ats[u]] = (jnp.maximum(pre, 0.0) + (grown_one - 1.0)).astype(bf16)
                        slope_ref[1, head_of(h), ats[u]] = grown_one
                    else:
                        rounded = total.astype(bf16).astype(f32)
                        pooled = rounded if pooled is None else pooled + rounded
                if layer == 1:
                    pool_ref[:, ats[u]] = (pooled * (1.0 / HEADS) + bias_two).astype(bf16)

    @pl.loop(0, chunks, unroll=4)
    def _(c):
        at = lanes_of(c, chunk)
        logits = dot_nn(wo_t, pool_ref[:, at]) + bias_out
        shifted = logits - jnp.max(logits, axis=0, keepdims=True)
        log_prob = shifted - jnp.log(jnp.sum(jnp.exp(shifted), axis=0, keepdims=True))
        class_id = lax.broadcasted_iota(jnp.int32, (CLASSES, chunk), 0)
        onehot = jnp.where(class_id == mark_ref[0:1, at], 1.0, 0.0)
        share = mark_ref[1:2, at].astype(f32) * inv_count
        term = jnp.sum(((smooth - 1.0) * onehot - smooth / CLASSES) * log_prob, axis=0, keepdims=True)
        loss_ref[...] += term * share
        d_logits = (jnp.exp(log_prob) - (1.0 - smooth) * onehot - smooth / CLASSES) * share
        d_logits = d_logits.astype(bf16)
        dlog_ref[:, at] = d_logits
        d_pooled = (dot_nn(wo_ref[...], d_logits) * (1.0 / HEADS)).astype(bf16)
        for h in range(HEADS):
            do_ref[head_of(h), at] = d_pooled

    for layer in (1, 0):

        @pl.loop(0, blocks // WAYS)
        def _(step):
            ids = [step * WAYS + u for u in range(WAYS)]
            ats = [lanes_of(i, LANES) for i in ids]
            ways = range(WAYS)
            d_out = [do_ref[:, ats[u]] for u in ways]
            d_alpha = []
            for u in ways:
                for h in range(HEADS):
                    d_head = d_out[u][head_of(h)].reshape(4, 16, LANES)
                    for k in range(SLOTS):
                        t = t_ref[layer, ids[u], head_of(h), tile_of(k)].reshape(4, 16, LANES)
                        product = t * d_head
                        sum_ref[u, h * 16 : (h + 1) * 16, tile_of(k)] = (product[0] + product[1]) + (
                            product[2] + product[3]
                        )
                d_alpha.append(dot_nn(fold, sum_ref[u])[0:8])
            for u in ways:
                alpha = al_ref[layer, ids[u]]
                weighted = alpha * d_alpha[u]
                total = weighted[:, tile_of(0)]
                for k in range(1, SLOTS):
                    total = total + weighted[:, tile_of(k)]
                for k in range(SLOTS):
                    d_score = weighted[:, tile_of(k)] - alpha[:, tile_of(k)] * total
                    for h in range(HEADS):
                        one = jnp.broadcast_to(d_score[h : h + 1], (16, LANES))
                        two = (one * leak_slope).astype(bf16)[None]
                        one = one.astype(bf16)[None]
                        t = t_ref[layer, ids[u], head_of(h), tile_of(k)].reshape(4, 16, LANES)
                        w_ref[u, head_of(h), tile_of(k)] = jnp.where(t > 0, one, two).reshape(HSIZE, LANES)
            for u in ways:
                together = jnp.concatenate([e_ref[ids[u]], eye_ref[...]], axis=0)
                spread = dot_nt(w_ref[u, :, 0:mixed], together)
                own = w_ref[u, :, tile_of(DEG)].astype(f32)
                left_w = spread[:, 0:LANES] + own
                right_w = spread[:, LANES : 2 * LANES] + own
                left = both_ref[layer, 0:HID, ats[u]].astype(f32)
                right = both_ref[layer, HID : 2 * HID, ats[u]].astype(f32)
                da_ref[layer] += left * left_w + right * right_w
                wide = a_ref[layer]
                for h in range(HEADS):
                    passed = dot_nt(d_out[u][head_of(h)], att_ref[layer, ids[u], h])
                    d_left = wide[head_of(h)] * left_w[head_of(h)] + passed
                    both_ref[1 + layer, head_of(h), ats[u]] = d_left.astype(bf16)
                both_ref[1 + layer, HID : 2 * HID, ats[u]] = (wide * right_w).astype(bf16)

        @pl.loop(0, chunks, unroll=4)
        def _(c):
            at = lanes_of(c, chunk)
            d_in = dot_nn(wg_ref[layer], both_ref[1 + layer, :, at]).astype(bf16).astype(f32)
            d_in = d_in * slope_ref[layer, :, at]
            do_ref[:, at] = d_in.astype(bf16)
            if layer == 1:
                for k in range(4):
                    gb_ref[...] += d_in[:, tile_of(k)]

    for layer in range(2):
        for side in range(2):
            start = (2 * layer + side) * HID
            out_ref[start : start + HID, :] = dot_nt(
                h_ref[layer], both_ref[1 + layer, side * HID : (side + 1) * HID, :]
            ).astype(bf16)
    ones = jnp.ones((nodes, LANES), bf16)
    with_sums = dot_nn(do_ref[...], jnp.concatenate([node_ref[...], ones], axis=1))
    out_ref[ROW_IN : ROW_IN + FEAT, :] = with_sums[:, 0:FEAT].T.astype(bf16)
    out_ref[ROW_OUT : ROW_OUT + HSIZE, :] = jnp.zeros((HSIZE, HID), bf16)
    out_ref[ROW_OUT : ROW_OUT + HSIZE, 0:CLASSES] = dot_nt(pool_ref[...], dlog_ref[...]).astype(bf16)
    lane_wide = lax.broadcasted_iota(jnp.int32, (HID, LANES), 1)
    columns = jnp.where(lane_wide == 0, with_sums[:, FEAT:], 0.0)
    for layer in range(2):
        da = jnp.sum(da_ref[layer], axis=1, keepdims=True)
        columns = columns + jnp.where(lane_wide == 1 + layer, da, 0.0)
    columns = columns + jnp.where(lane_wide == 3, jnp.sum(gb_ref[...], axis=1, keepdims=True), 0.0)
    g_bias_out = dot_nn(dlog_ref[...], ones)
    g_bias_two = lax.dot_general(
        wo_ref[...].astype(f32), g_bias_out, (((1,), (0,)), ((), ())),
        precision=highest, preferred_element_type=f32,
    )
    loss = jnp.broadcast_to(jnp.sum(loss_ref[...], axis=1, keepdims=True), (8, LANES))
    loss_high = loss.astype(bf16).astype(f32)
    rest = HID - HSIZE - CLASSES - 16
    last = jnp.concatenate(
        [g_bias_two, g_bias_out, loss_high, loss - loss_high, jnp.zeros((rest, LANES), f32)], axis=0
    )
    columns = columns + jnp.where(lane_wide == 4, last, 0.0)
    out_ref[ROW_MISC : ROW_MISC + 16, :] = columns.T[0:16].astype(bf16)
    out_ref[ROW_MISC + 16 :, :] = jnp.zeros((ROWS - ROW_MISC - 16, HID), bf16)
    core = jnp.bitwise_and(dom_ref[0], 1)
    width = ROWS // 2
    keep_ref[...] = out_ref[pl.ds(pl.multiple_of(core * width, width), width), :]
    send_out_ref[...] = out_ref[pl.ds(pl.multiple_of((1 - core) * width, width), width), :]


def run_model(section_id, dom_id, spot, features, src_all, labels, label_mask, send_index, pieces, small_params):
    nodes = features.shape[1]
    blocks = nodes // LANES
    scratch = [
        pltpu.VMEM((blocks, LANES, DEG * LANES), bf16),
        pltpu.VMEM((2, blocks, HID, SLOTS * LANES), bf16),
        pltpu.VMEM((2, blocks, 8, SLOTS * LANES), f32),
        pltpu.VMEM((2, blocks, HEADS, LANES, LANES), bf16),
        pltpu.VMEM((2, HID, nodes), bf16),
        pltpu.VMEM((2, HID, nodes), f32),
        pltpu.VMEM((3, 2 * HID, nodes), bf16),
        pltpu.VMEM((HID, nodes), bf16),
        pltpu.VMEM((HSIZE, nodes), bf16),
        pltpu.VMEM((CLASSES, nodes), bf16),
        pltpu.VMEM((WAYS, HID, SLOTS * LANES), bf16),
        pltpu.VMEM((WAYS, HEADS * 16, SLOTS * LANES), bf16),
        pltpu.VMEM((2, HID, LANES), f32),
        pltpu.VMEM((2, HID, LANES), f32),
        pltpu.VMEM((HID, LANES), f32),
        pltpu.VMEM((1, 4 * LANES), f32),
        pltpu.VMEM((nodes, FEAT), bf16),
        pltpu.VMEM((DEG, nodes), jnp.int32),
        pltpu.VMEM((8, nodes), jnp.int32),
        pltpu.VMEM((FEAT, HID), bf16),
        pltpu.VMEM((2, 2 * HID, HID), bf16),
        pltpu.VMEM((2, HID, 2 * HID), bf16),
        pltpu.VMEM((HSIZE, CLASSES), bf16),
        pltpu.VMEM((HSIZE, LANES), f32),
        pltpu.VMEM((2, 16, HID), bf16),
        pltpu.VMEM((ROWS, HID), bf16),
        pltpu.VMEM((LANES, DEG * LANES), bf16),
        pltpu.VMEM((GROUPS, 32, HID), bf16),
    ]
    def body(*refs):
        pl.run_scoped(lambda *buffers: model_kernel(*refs, *buffers), *scratch)

    grid_spec = pltpu.PrefetchScalarGridSpec(
        num_scalar_prefetch=3,
        grid=(1,),
        in_specs=[
            pl.BlockSpec((1, nodes, FEAT), lambda i, m, d, p: (m[0], 0, 0)),
            pl.BlockSpec((1, DEG, nodes), lambda i, m, d, p: (m[0], 0, 0)),
        ]
        + vmem(12),
        out_specs=vmem(2),
    )
    return pl.pallas_call(
        body,
        grid_spec=grid_spec,
        out_shape=[jax.ShapeDtypeStruct((ROWS // 2, HID), bf16)] * 2,
        compiler_params=pltpu.CompilerParams(vmem_limit_bytes=50 * 1024 * 1024),
        name="model",
    )(section_id, dom_id, spot, features, src_all, labels, label_mask, send_index, *pieces, small_params)


def settled(total, is_last):
    base = ROW_MISC % PIECE
    block = total[base : base + 8]
    row = lax.broadcasted_iota(jnp.int32, (8, HID), 0)
    lane = lax.broadcasted_iota(jnp.int32, (8, HID), 1)
    spot = HSIZE + CLASSES
    joined = block + pltpu.roll(block, HID - 8, 1)
    high = joined.astype(bf16).astype(f32)
    low = pltpu.roll(joined - high, 8, 1)
    here = (row == 4) & (lane >= spot) & (lane < spot + 16) & (is_last == 1)
    block = jnp.where(here, jnp.where(lane < spot + 8, high, low), block)
    return jnp.concatenate([total[:base], block, total[base + 8 :]], axis=0).astype(bf16)


def last_piece(core, section):
    return jnp.where((core == 1) & (section == 3), 1, 0)


def split_kernel(section_ref, dom_ref, keep_ref, got_ref, *out_refs):
    section = section_ref[0]
    core = jnp.bitwise_and(dom_ref[0], 1)
    for j, out_ref in enumerate(out_refs):
        part = jnp.bitwise_xor(section, j)
        at = pl.ds(pl.multiple_of(part * PIECE, PIECE), PIECE)
        total = keep_ref[at, :].astype(f32) + got_ref[at, :].astype(f32)
        out_ref[...] = settled(total, last_piece(core, part))


def join_kernel(section_ref, dom_ref, own_ref, one_ref, two_ref, three_ref, out_ref):
    pair = own_ref[...].astype(f32) + one_ref[...].astype(f32)
    other = two_ref[...].astype(f32) + three_ref[...].astype(f32)
    core = jnp.bitwise_and(dom_ref[0], 1)
    out_ref[...] = settled(pair + other, last_piece(core, section_ref[0]))


def small_call(kernel, name, ids, count, operands):
    shape = jax.ShapeDtypeStruct((PIECE, HID), bf16)
    return pl.pallas_call(
        kernel,
        out_shape=[shape] * count if count > 1 else shape,
        in_specs=[pl.BlockSpec(memory_space=pltpu.SMEM)] * 2 + vmem(len(operands)),
        out_specs=vmem(count) if count > 1 else vmem(1)[0],
        compiler_params=pltpu.CompilerParams(vmem_limit_bytes=8 * 1024 * 1024),
        name=name,
    )(*ids, *operands)


def sum_gradients(ids, keep, send):
    if lax.axis_size("dom") == 8 and lax.axis_size("section") == 4:
        got = crossed(send, "dom", 1)
        parts = small_call(split_kernel, "split", ids, 4, (keep, got))
        came = [crossed(parts[j], "section", j) for j in range(1, 4)]
        mine = small_call(join_kernel, "join", ids, 1, (parts[0], *came))
        came = [crossed(mine, "dom", 2 * j) for j in range(1, 4)]
        mine = small_call(join_kernel, "join", ids, 1, (mine, *came))
        near = [mine] + [crossed(mine, "section", j) for j in range(1, 4)]
        return near + [crossed(piece, "dom", 1) for piece in near], ids
    all_size = lax.axis_size("dom") * lax.axis_size("section")
    swap = jnp.bitwise_and(ids[1][0], 1) == 1
    partial = jnp.concatenate([jnp.where(swap, send, keep), jnp.where(swap, keep, send)], axis=0)
    parts = lax.all_to_all(partial.reshape(all_size, -1, HID), ("section", "dom"), 0, 0)
    mine = jnp.sum(parts.astype(f32), axis=0)
    shared = jnp.broadcast_to(mine.astype(bf16)[None], (all_size,) + mine.shape)
    summed = lax.all_to_all(shared, ("section", "dom"), 0, 0).reshape(8, PIECE, HID)
    return [summed[j] for j in range(8)], (ids[0] * 0, ids[1] * 0)


def adamw_step(parameter, gradient, moment_one, moment_two):
    moment_one = beta_one * moment_one + (1.0 - beta_one) * gradient
    moment_two = beta_two * moment_two + (1.0 - beta_two) * gradient * gradient
    corr_one = 1.0 - beta_one**STEPS
    corr_two = 1.0 - beta_two**STEPS
    update = moment_one / corr_one / (jnp.sqrt(moment_two / corr_two) + adam_eps)
    return (parameter - adam_rate * (update + adam_decay * parameter), moment_one, moment_two)


def average(old_value, new_value):
    return ema_keep * old_value + (1.0 - ema_keep) * new_value


def dot_tn(a, b):
    return lax.dot_general(a, b, (((0,), (0,)), ((), ())), preferred_element_type=f32)


def halves(value):
    high = value.astype(bf16)
    return high, (value - high.astype(f32)).astype(bf16)


def wide_rows(total):
    return max(total, 16)


def own_rows(gradient, start, count):
    total = gradient.shape[0]
    row = lax.broadcasted_iota(jnp.int32, (wide_rows(count), total), 0) + start
    lane = lax.broadcasted_iota(jnp.int32, (wide_rows(count), total), 1)
    pick = jnp.where(row == lane, 1.0, 0.0).astype(bf16)
    return dot_nn(pick, gradient).astype(bf16)


def precondition(gradient, weight, stat_l, stat_r, root_l, root_r, ema, outs, scale, start):
    (new_w, new_l, new_r, new_ema) = outs
    count = weight.shape[0]
    square = (1.0 - shampoo_decay) * scale * scale
    mine = own_rows(gradient, start, count)
    new_l[...] = shampoo_decay * stat_l + square * dot_nt(mine, gradient)[0:count]
    new_r[...] = shampoo_decay * stat_r + square * dot_tn(gradient, gradient)
    high, low = halves(root_l)
    middle = dot_nn(high, gradient) + dot_nn(low, gradient)
    m_high, m_low = halves(middle * scale)
    r_high, r_low = halves(root_r)
    update = dot_nn(m_high, r_high) + dot_nn(m_low, r_high) + dot_nn(m_high, r_low)
    weight = weight - shampoo_rate * (update + weight_decay * weight)
    new_w[...] = weight
    new_ema[...] = average(ema, weight)


def update_kernel(
    dom_ref,
    section_ref,
    spot_ref,
    piece_0,
    piece_1,
    piece_2,
    piece_3,
    piece_4,
    piece_5,
    piece_6,
    piece_7,
    w_in,
    w_gat,
    w_out,
    small,
    l_in,
    r_in,
    l_gat,
    r_gat,
    l_out,
    r_out,
    rl_in,
    rr_in,
    rl_gat,
    rr_gat,
    rl_out,
    rr_out,
    first,
    second,
    e_in,
    e_gat,
    e_out,
    e_small,
    n_w_in,
    n_w_gat,
    n_w_out,
    n_small,
    n_l_in,
    n_r_in,
    n_l_gat,
    n_r_gat,
    n_l_out,
    n_r_out,
    n_first,
    n_second,
    n_e_in,
    n_e_gat,
    n_e_out,
    n_e_small,
    loss_ref,
    norm_ref,
    sum_ref,
):
    dom = dom_ref[0]
    core = jnp.bitwise_and(spot_ref[0], 1)
    pieces = (piece_0, piece_1, piece_2, piece_3, piece_4, piece_5, piece_6, piece_7)
    for j, piece in enumerate(pieces):
        spot = jnp.bitwise_xor(core, j >> 2) * 4 + jnp.bitwise_xor(section_ref[0], j & 3)
        sum_ref[pl.ds(pl.multiple_of(spot * PIECE, PIECE), PIECE), :] = piece[...]
    grads = sum_ref[0:ROW_MISC, :].astype(f32)
    squares = jnp.sum(grads * grads)
    misc = sum_ref[ROW_MISC : ROW_MISC + 8, :].astype(f32)
    row = lax.broadcasted_iota(jnp.int32, (8, HID), 0)
    lane = lax.broadcasted_iota(jnp.int32, (8, HID), 1)
    spot = HSIZE + CLASSES
    loss_ref[0] = jnp.sum(jnp.where((row == 4) & ((lane == spot) | (lane == spot + 8)), misc, 0.0))
    small_part = jnp.where((row < 4) | ((row == 4) & (lane < spot)), misc, 0.0)
    squares = squares + jnp.sum(small_part * small_part)
    norm = jnp.sqrt(jnp.broadcast_to(squares, (1, 1)))
    scale = jnp.minimum(1.0, clip_norm / norm)
    norm_ref[0] = jnp.sum(norm)
    for layer in range(2):
        for side in range(2):
            at = (layer, side)
            begin = (2 * layer + side) * HID
            precondition(
                sum_ref[begin : begin + HID, :],
                w_gat[at],
                l_gat[at],
                r_gat[at],
                rl_gat[at],
                rr_gat[at],
                e_gat[at],
                (n_w_gat.at[at], n_l_gat.at[at], n_r_gat.at[at], n_e_gat.at[at]),
                scale,
                dom * w_gat.shape[2],
            )
    precondition(
        sum_ref[ROW_IN:ROW_OUT, :],
        w_in[...],
        l_in[...],
        r_in[...],
        rl_in[...],
        rr_in[...],
        e_in[...],
        (n_w_in, n_l_in, n_r_in, n_e_in),
        scale,
        dom * w_in.shape[0],
    )
    precondition(
        sum_ref[ROW_OUT:ROW_MISC, 0:CLASSES],
        w_out[...],
        l_out[...],
        r_out[...],
        rl_out[...],
        rr_out[...],
        e_out[...],
        (n_w_out, n_l_out, n_r_out, n_e_out),
        scale,
        dom * w_out.shape[0],
    )
    for place in range(5):
        width = HID if place < 4 else spot
        at = pl.ds(place * HID, width)
        gradient = misc[place : place + 1, 0:width] * scale

        def line(ref):
            return ref[at].reshape(1, width)

        new_value, moment_one, moment_two = adamw_step(line(small), gradient, line(first), line(second))
        n_small[at] = new_value.reshape(width)
        n_first[at] = moment_one.reshape(width)
        n_second[at] = moment_two.reshape(width)
        n_e_small[at] = average(line(e_small), new_value).reshape(width)


def per_device(
    features,
    sources,
    send_index,
    labels,
    label_mask,
    w_in,
    w_gat,
    w_out,
    small_params,
    stat_l_in,
    stat_r_in,
    stat_l_gat,
    stat_r_gat,
    stat_l_out,
    stat_r_out,
    root_l_in,
    root_r_in,
    root_l_gat,
    root_r_gat,
    root_l_out,
    root_r_out,
    adam_first,
    adam_second,
    ema_in,
    ema_gat,
    ema_out,
    ema_small,
):
    dom_id = lax.axis_index("dom").astype(jnp.int32).reshape(1)
    section_id = lax.axis_index("section").astype(jnp.int32).reshape(1)
    src_all = jnp.swapaxes(sources, 1, 2)
    packed = pack_inputs(section_id, features, src_all, labels, label_mask, send_index, w_in, w_gat, w_out)
    pieces, spot = gather_weights(dom_id, packed, w_in, w_gat, w_out, label_mask)
    keep, send = run_model(
        section_id, dom_id, spot, features, src_all, labels, label_mask, send_index, pieces, small_params
    )
    pieces, spots = sum_gradients((section_id, dom_id), keep, send)
    state = (
        w_in,
        w_gat,
        w_out,
        small_params,
        stat_l_in,
        stat_r_in,
        stat_l_gat,
        stat_r_gat,
        stat_l_out,
        stat_r_out,
        root_l_in,
        root_r_in,
        root_l_gat,
        root_r_gat,
        root_l_out,
        root_r_out,
        adam_first,
        adam_second,
        ema_in,
        ema_gat,
        ema_out,
        ema_small,
    )
    like = state[:10] + (adam_first, adam_second, ema_in, ema_gat, ema_out, ema_small)
    results = pl.pallas_call(
        update_kernel,
        out_shape=[jax.ShapeDtypeStruct(v.shape, f32) for v in like] + [jax.ShapeDtypeStruct((1,), f32)] * 2,
        in_specs=[pl.BlockSpec(memory_space=pltpu.SMEM)] * 3 + vmem(30),
        out_specs=vmem(16) + [pl.BlockSpec(memory_space=pltpu.SMEM)] * 2,
        scratch_shapes=[pltpu.VMEM((ROWS, HID), bf16)],
        compiler_params=pltpu.CompilerParams(vmem_limit_bytes=16 * 1024 * 1024),
        name="update",
    )(dom_id, *spots, *pieces, *state)
    return tuple(results[:16]) + (results[16].reshape(()), results[17].reshape(()))


def solution(mesh):
    placed = (
        P(None, "dom", None),
        P(None, "dom", None),
        P(None, "dom"),
        P(None, "dom"),
        P(None, "dom"),
        P("dom", None),
        P(None, None, "dom", None),
        P("dom", None),
        P(),
        P("dom", None),
        P(),
        P(None, None, "dom", None),
        P(),
        P("dom", None),
        P(),
        P("dom", None),
        P(),
        P(None, None, "dom", None),
        P(),
        P("dom", None),
        P(),
        P(),
        P(),
        P("dom", None),
        P(None, None, "dom", None),
        P("dom", None),
        P(),
    )
    return jax.shard_map(
        per_device,
        mesh=mesh,
        in_specs=placed,
        out_specs=(
            P("dom", None),
            P(None, None, "dom", None),
            P("dom", None),
            P(),
            P("dom", None),
            P(),
            P(None, None, "dom", None),
            P(),
            P("dom", None),
            P(),
            P(),
            P(),
            P("dom", None),
            P(None, None, "dom", None),
            P("dom", None),
            P(),
            P(),
            P(),
        ),
        check_vma=False,
    )
```

```python
import jax
import jax.numpy as jnp
from jax import lax
from jax.experimental import pallas as pl
from jax.experimental.pallas import tpu as pltpu
from jax.sharding import PartitionSpec as P

FEAT = 128
HEADS = 4
HSIZE = 64
CLASSES = 40
STEPS = 5
HID = 256
SMALL = 1128


highest = lax.Precision.HIGHEST
leak_slope = 0.2
smooth = 0.1
clip_norm = 0.001
shampoo_rate = 0.3
shampoo_decay = 0.5
weight_decay = 0.0001
adam_rate = 0.1
beta_one = 0.9
beta_two = 0.999
adam_eps = 1e-08
adam_decay = 0.01
ema_keep = 0.9


def split_small(small_params):
    bias_in = small_params[0:HID]
    attention = small_params[HID : 3 * HID].reshape(2, HEADS, HSIZE)
    bias_one = small_params[3 * HID : 4 * HID]
    bias_two = small_params[4 * HID : 4 * HID + HSIZE]
    bias_out = small_params[4 * HID + HSIZE :]
    return (bias_in, attention, bias_one, bias_two, bias_out)


GRAPH = 64
LANES = 128
DEG = 8
SLOTS = DEG + 1
WAYS = 4
ROWS = 1280
GROUPS = 8
IN_G = FEAT // GROUPS
GAT_G = HID // GROUPS
OUT_G = HSIZE // GROUPS
TAIL_G = IN_G + 4 * GAT_G
PACK_G = TAIL_G + 2 * OUT_G
HALO_G = PACK_G + 16
CODES = slice(HID - LANES, HID)
PIECE = ROWS // 8
HALF = GRAPH // 2
ROW_IN = 4 * HID
ROW_OUT = ROW_IN + FEAT
ROW_MISC = ROW_OUT + HSIZE

bf16 = jnp.bfloat16
f32 = jnp.float32


def dot_nn(a, b):
    return lax.dot_general(a, b, (((1,), (0,)), ((), ())), preferred_element_type=f32)


def dot_nt(a, b):
    return lax.dot_general(a, b, (((1,), (1,)), ((), ())), preferred_element_type=f32)


def tile_of(k):
    return slice(k * LANES, (k + 1) * LANES)


def head_of(h):
    return slice(h * HSIZE, (h + 1) * HSIZE)


def row_of(ref, micro, width):
    picked = ref[0:1, 0:width]
    for other in range(1, ref.shape[0]):
        picked = jnp.where(micro == other, ref[other : other + 1, 0:width], picked)
    return picked


def pack_kernel(
    section_ref,
    feat_ref,
    src_ref,
    lab_ref,
    msk_ref,
    send_ref,
    win_ref,
    wgat_ref,
    wout_ref,
    pack_ref,
    tail_ref,
):
    micro = section_ref[0]
    nodes = lab_ref.shape[1]
    pack_ref[PACK_G:HALO_G, 0:FEAT] = feat_ref[0, 0:16]
    pack_ref[PACK_G:HALO_G, FEAT : 2 * FEAT] = feat_ref[0, 16:32]
    shift = LANES - HALF
    tail_ref[...] = jnp.zeros_like(tail_ref)
    far = src_ref[0]
    far = jnp.where(far >= nodes, far - nodes + GRAPH, far)
    tail_ref[0:DEG, CODES] = pltpu.roll(far, shift, 1).astype(f32)
    tail_ref[DEG : DEG + 1, CODES] = pltpu.roll(row_of(lab_ref, micro, LANES), shift, 1).astype(f32)
    tail_ref[DEG + 1 : DEG + 2, CODES] = pltpu.roll(row_of(msk_ref, micro, LANES), shift, 1).astype(f32)
    send = row_of(send_ref, micro, 2 * HALF)
    tail_ref[DEG + 2 : DEG + 3, CODES] = jnp.concatenate([send, send], axis=1).astype(f32)
    if win_ref.shape[0] != IN_G:
        pack_ref[0:TAIL_G, :] = jnp.zeros((TAIL_G, HID), bf16)
        pack_ref[TAIL_G:PACK_G, :] = tail_ref[...].astype(bf16)
        return
    pack_ref[0:IN_G, :] = win_ref[...].astype(bf16)
    for layer in range(2):
        for side in range(2):
            start = IN_G + (2 * layer + side) * GAT_G
            pack_ref[start : start + GAT_G, :] = wgat_ref[layer, side].astype(bf16)
    tail_ref[0:OUT_G, 0:CLASSES] = wout_ref[...]
    count = jnp.sum(jnp.sum(msk_ref[...].astype(f32), axis=1, keepdims=True), axis=0, keepdims=True)
    high = jnp.floor(count * (1.0 / 256.0))
    lane = lax.broadcasted_iota(jnp.int32, (1, LANES), 1)
    low = jnp.where(lane == 1, count - 256.0 * high, 0.0)
    tail_ref[OUT_G : OUT_G + 1, 0:LANES] = jnp.where(lane == 0, high, low)
    pack_ref[TAIL_G:PACK_G, :] = tail_ref[...].astype(bf16)


def vmem(count):
    return [pl.BlockSpec(memory_space=pltpu.VMEM)] * count


def pack_inputs(section_id, features, src_all, labels, label_mask, send_index, w_in, w_gat, w_out):
    grid_spec = pltpu.PrefetchScalarGridSpec(
        num_scalar_prefetch=1,
        grid=(1,),
        in_specs=[
            pl.BlockSpec((1, HALF, FEAT), lambda i, m: (m[0], 0, 0)),
            pl.BlockSpec((1, DEG, LANES), lambda i, m: (m[0], 0, 0)),
        ]
        + vmem(6),
        out_specs=vmem(1)[0],
        scratch_shapes=[pltpu.VMEM((2 * OUT_G, HID), f32)],
    )
    return pl.pallas_call(
        pack_kernel,
        grid_spec=grid_spec,
        out_shape=jax.ShapeDtypeStruct((HALO_G, HID), bf16),
        compiler_params=pltpu.CompilerParams(vmem_limit_bytes=58 * 1024 * 1024),
        name="pack",
    )(section_id, features, src_all, labels, label_mask, send_index, w_in, w_gat, w_out)


def crossed(value, axis, mask):
    return lax.ppermute(value, axis, [(i, i ^ mask) for i in range(lax.axis_size(axis))])


def gather_weights(dom_id, packed, w_in, w_gat, w_out, label_mask):
    size = lax.axis_size("dom")
    if size == GROUPS:
        near = [packed] + [crossed(packed, "dom", 2 * j) for j in range(1, 4)]
        return near + [crossed(piece, "dom", 1) for piece in near], dom_id
    halo = lax.ppermute(packed[TAIL_G:], "dom", [((i + 1) % size, i) for i in range(size)])
    halo = jnp.broadcast_to(halo[None], (GROUPS,) + halo.shape)
    rows_in, rows_gat, rows_out = (w_in.shape[0], w_gat.shape[2], w_out.shape[0])
    count = jnp.sum(label_mask)
    digits = jnp.stack([lax.div(count, 256), lax.rem(count, 256)]).astype(bf16)
    packed = jnp.concatenate(
        [
            w_in.astype(bf16),
            w_gat.astype(bf16).reshape(4 * rows_gat, HID),
            jnp.pad(w_out.astype(bf16), ((0, 0), (0, HID - CLASSES))),
            jnp.pad(digits[None, :], ((0, 0), (0, HID - 2))),
        ],
        axis=0,
    )
    whole = lax.all_gather(packed, "dom", axis=0, tiled=False)
    cut = rows_in + 4 * rows_gat
    part_in = whole[:, :rows_in].reshape(GROUPS, IN_G, HID)
    part_gat = whole[:, rows_in:cut].reshape(GROUPS, size // GROUPS, 4, rows_gat, HID)
    part_gat = part_gat.transpose(0, 2, 1, 3, 4).reshape(GROUPS, 4 * GAT_G, HID)
    part_out = whole[:, cut : cut + rows_out].reshape(GROUPS, OUT_G, HID)
    counts = whole[:, cut + rows_out].reshape(GROUPS, size // GROUPS, HID)
    counts = jnp.pad(counts, ((0, 0), (0, OUT_G - size // GROUPS), (0, 0)))
    tail = jnp.concatenate([part_out, counts], axis=1)
    tail = jnp.concatenate([tail[:, :, :LANES], halo[:, : 2 * OUT_G, LANES:]], axis=2)
    whole = jnp.concatenate([part_in, part_gat, tail, halo[:, 2 * OUT_G :]], axis=1)
    return [whole[g] for g in (0, 2, 4, 6, 1, 3, 5, 7)], dom_id * 0


def parted(rows):
    high = rows.astype(bf16).astype(f32)
    return jnp.concatenate([high, rows - high], axis=0)


def column_of(row):
    return jnp.broadcast_to(row.reshape(1, -1), (LANES, row.shape[0])).T


def model_kernel(
    section_ref,
    dom_ref,
    spot_ref,
    feat_ref,
    src_ref,
    lab_ref,
    msk_ref,
    send_ref,
    piece_refs,
    shard_refs,
    small_ref,
    keep_ref,
    send_out_ref,
    e_ref,
    t_ref,
    al_ref,
    att_ref,
    h_ref,
    slope_ref,
    both_ref,
    do_ref,
    pool_ref,
    dlog_ref,
    w_ref,
    sum_ref,
    a_ref,
    da_ref,
    gb_ref,
    loss_ref,
    node_ref,
    edge_ref,
    mark_ref,
    wi_ref,
    wgt_ref,
    wg_ref,
    wo_ref,
    wof_ref,
    am_ref,
    out_ref,
    eye_ref,
    halo_ref,
):
    nodes = feat_ref.shape[1]
    blocks = nodes // LANES
    chunk = 4 * LANES
    chunks = nodes // chunk
    mixed = DEG * LANES
    micro = section_ref[0]
    after = jnp.bitwise_and(spot_ref[0] + 1, GROUPS - 1)
    final = nodes - LANES

    digits = jnp.zeros((OUT_G, LANES), f32)
    own_count = jnp.zeros((1, 1), f32)
    first = GROUPS - len(piece_refs)
    if first == 1:
        (win_ref, wgat_ref, wout_ref) = shard_refs
        group = spot_ref[0]
        at_in = pl.ds(pl.multiple_of(group * IN_G, IN_G), IN_G)
        at_gat = pl.ds(pl.multiple_of(group * GAT_G, GAT_G), GAT_G)
        at_out = pl.ds(pl.multiple_of(group * OUT_G, OUT_G), OUT_G)
        wi_ref[at_in, :] = win_ref[...].astype(bf16)
        for layer in range(2):
            for side in range(2):
                wg_ref[layer, at_gat, side * HID : (side + 1) * HID] = wgat_ref[layer, side].astype(bf16)
        wof_ref[at_out, :] = jnp.zeros((OUT_G, LANES), f32)
        wof_ref[at_out, 0:CLASSES] = wout_ref[...]
        marked = jnp.sum(msk_ref[...].astype(f32), axis=1, keepdims=True)
        own_count = jnp.sum(marked, axis=0, keepdims=True)
    for j, piece in enumerate(piece_refs, first):
        group = jnp.bitwise_xor(spot_ref[0], 2 * (j & 3) + (j >> 2))

        def rows_of(width):
            return pl.ds(pl.multiple_of(group * width, width), width)

        wi_ref[rows_of(IN_G), :] = piece[0:IN_G, :]
        for layer in range(2):
            for side in range(2):
                start = IN_G + (2 * layer + side) * GAT_G
                wg_ref[layer, rows_of(GAT_G), side * HID : (side + 1) * HID] = piece[start : start + GAT_G, :]
        tail = piece[TAIL_G:PACK_G, :].astype(f32)
        wof_ref[rows_of(OUT_G), :] = tail[0:OUT_G, 0:LANES]
        digits = digits + tail[OUT_G : 2 * OUT_G, 0:LANES]
        halo_ref[group] = piece[TAIL_G:HALO_G, :]

    node_ref[0 : nodes - HALF, :] = feat_ref[0, HALF:nodes, :]
    node_ref[nodes - HALF : nodes - 16, :] = halo_ref[after, 16:32, 0:FEAT]
    node_ref[nodes - 16 : nodes, :] = halo_ref[after, 16:32, FEAT : 2 * FEAT]
    ints = halo_ref[after, 0:16, CODES].astype(f32).astype(jnp.int32)
    lane_row = lax.broadcasted_iota(jnp.int32, (1, LANES), 1)
    kept = lane_row < LANES - HALF
    edge_ref[...] = pltpu.roll(src_ref[0], nodes - HALF, 1)
    edge_ref[:, final:nodes] = jnp.where(
        kept,
        edge_ref[:, final:nodes],
        jnp.where(ints[0:DEG] >= GRAPH, ints[0:DEG] + (nodes - GRAPH), ints[0:DEG]),
    )
    for place, ref in enumerate((lab_ref, msk_ref)):
        mark_ref[place : place + 1, :] = pltpu.roll(row_of(ref, micro, nodes), nodes - HALF, 1)
        came = ints[DEG + place : DEG + place + 1]
        mark_ref[place : place + 1, final:nodes] = jnp.where(kept, mark_ref[place : place + 1, final:nodes], came)
    send = row_of(send_ref, micro, 2 * HALF)
    send = jnp.concatenate([send, send], axis=1)
    arrived = pltpu.roll(ints[DEG + 2 : DEG + 3], HALF, 1)
    table = jnp.where(
        lane_row < HALF, pltpu.roll(send, HALF, 1) - (nodes - HALF), arrived + HALF
    )
    spot_row = lax.broadcasted_iota(jnp.int32, (GRAPH, LANES), 0)
    spot_lane = lax.broadcasted_iota(jnp.int32, (GRAPH, LANES), 1)
    table = jnp.sum(jnp.where(spot_row == spot_lane, table.astype(f32), 0.0), axis=1, keepdims=True)
    looked = []
    for k in range(DEG):
        far = edge_ref[k : k + 1, final:nodes] - nodes == spot_row
        looked.append(jnp.sum(jnp.where(far, table, 0.0), axis=0, keepdims=True))
    looked = jnp.concatenate(looked, axis=0).astype(jnp.int32)
    raw = edge_ref[:, final:nodes]
    looked = jnp.where(raw >= nodes, looked, jnp.bitwise_and(raw - HALF, GRAPH - 1))
    local = jnp.bitwise_and(edge_ref[...] - HALF, GRAPH - 1)
    lane_all = lax.broadcasted_iota(jnp.int32, (DEG, nodes), 1)
    second = jnp.bitwise_and(lane_all, GRAPH)
    edge_ref[...] = local + second
    edge_ref[:, final:nodes] = looked + jnp.bitwise_and(
        lax.broadcasted_iota(jnp.int32, (DEG, LANES), 1), GRAPH
    )

    for layer in range(2):
        for side in range(2):
            wgt_ref[layer, side * HID : (side + 1) * HID, :] = wg_ref[
                layer, :, side * HID : (side + 1) * HID
            ].T
    wi_t = wi_ref[...].T
    wo_ref[...] = wof_ref[:, 0:CLASSES].astype(bf16)
    wo_t = wof_ref[...].T[0:CLASSES].astype(bf16)
    digits = jnp.sum(digits, axis=0, keepdims=True)
    inv_count = 1.0 / (digits[:, 0:1] * 256.0 + digits[:, 1:2] + own_count)

    row_id = lax.broadcasted_iota(jnp.int32, (LANES, LANES), 0)
    lane_id = lax.broadcasted_iota(jnp.int32, (LANES, LANES), 1)
    eye = jnp.where(row_id == lane_id, 1.0, 0.0).astype(bf16)
    head_row = lax.broadcasted_iota(jnp.int32, (16, HID), 0)
    head_col = lax.broadcasted_iota(jnp.int32, (16, HID), 1)
    head_mask = jnp.where(head_col // HSIZE == head_row, 1.0, 0.0)

    bias_in = column_of(small_ref[0:HID])[:, 0:1]
    bias_one = column_of(small_ref[3 * HID : 4 * HID])[:, 0:1]
    bias_two = column_of(small_ref[4 * HID : 4 * HID + HSIZE])[:, 0:1]
    bias_out = column_of(small_ref[4 * HID + HSIZE : SMALL])[:, 0:1]
    for layer in range(2):
        row = small_ref[(1 + layer) * HID : (2 + layer) * HID]
        a_ref[layer] = column_of(row)
        row = row.reshape(1, HID)
        high = row.astype(bf16).astype(f32)
        am_ref[layer] = jnp.concatenate([head_mask[0:8] * high, head_mask[0:8] * (row - high)], axis=0).astype(bf16)
    fold_row = lax.broadcasted_iota(jnp.int32, (16, HEADS * 16), 0)
    fold_col = lax.broadcasted_iota(jnp.int32, (16, HEADS * 16), 1)
    fold = jnp.where(fold_col // 16 == fold_row, 1.0, 0.0).astype(bf16)
    spots = lax.broadcasted_iota(jnp.int32, (GRAPH, LANES), 0).astype(f32).astype(bf16)
    spots = spots.reshape(4, 16, LANES)
    half_lane = lax.broadcasted_iota(jnp.int32, (16, LANES), 1)
    first_half = (half_lane < GRAPH).astype(f32).astype(bf16)[None] > 0
    own_spot = jnp.bitwise_and(half_lane, GRAPH - 1).astype(f32).astype(bf16)
    zero = jnp.zeros((4, 16, LANES), bf16)
    da_ref[...] = jnp.zeros_like(da_ref)
    gb_ref[...] = jnp.zeros_like(gb_ref)
    loss_ref[...] = jnp.zeros_like(loss_ref)

    def lanes_of(i, width):
        return pl.ds(pl.multiple_of(i * width, width), width)

    @pl.loop(0, chunks, unroll=4)
    def _(c):
        at = lanes_of(c, chunk)
        pre = dot_nt(wi_t, node_ref[at, :]) + bias_in
        grown = jnp.exp(jnp.minimum(pre, 0.0))
        h_ref[0, :, at] = (jnp.maximum(pre, 0.0) + (grown - 1.0)).astype(bf16)
        slope_ref[0, :, at] = grown

    wide_spots = lax.broadcasted_iota(jnp.int32, (LANES, LANES), 0).astype(f32).astype(bf16)
    wide_spots = wide_spots.reshape(8, 16, LANES)
    for k in range(DEG):
        eye_ref[:, tile_of(k)] = eye

    @pl.loop(0, blocks)
    def _(i):
        at = lanes_of(i, LANES)
        for k in range(DEG):
            spot = jnp.broadcast_to(edge_ref[k : k + 1, at].astype(f32), (16, LANES)).astype(bf16)
            hit = wide_spots == spot[None]
            hit = jnp.where(hit, jnp.ones((8, 16, LANES), bf16), jnp.zeros((8, 16, LANES), bf16))
            e_ref[i, :, tile_of(k)] = hit.reshape(LANES, LANES)

    for layer in range(2):

        @pl.loop(0, chunks, unroll=4)
        def _(c):
            at = lanes_of(c, chunk)
            both_ref[layer, :, at] = dot_nn(wgt_ref[layer], h_ref[layer, :, at]).astype(bf16)

        @pl.loop(0, blocks // WAYS)
        def _(step):
            ids = [step * WAYS + u for u in range(WAYS)]
            ats = [lanes_of(i, LANES) for i in ids]
            ways = range(WAYS)
            left = [both_ref[layer, 0:HID, ats[u]] for u in ways]
            grown = []
            for u in ways:
                right = both_ref[layer, HID : 2 * HID, ats[u]]
                left_f = left[u].astype(f32)
                mixed_rows = [dot_nn(left[u], e_ref[ids[u], :, 0 : 2 * LANES]).astype(bf16)]
                for k in range(2, DEG):
                    index = jnp.broadcast_to(edge_ref[k : k + 1, ats[u]], (HID, LANES))
                    picked = jnp.take_along_axis(left_f, index, axis=1, mode="promise_in_bounds")
                    mixed_rows.append(picked.astype(bf16))
                mixed_rows = jnp.concatenate(mixed_rows, axis=1)
                mixed_rows = mixed_rows + jnp.concatenate([right] * DEG, axis=1)
                own = left[u] + right
                t_ref[layer, ids[u], :, 0:mixed] = mixed_rows
                t_ref[layer, ids[u], :, tile_of(DEG)] = own
                t = jnp.concatenate([mixed_rows, own], axis=1)
                z = jnp.maximum(t, t * leak_slope)
                scores = dot_nn(am_ref[layer], z)
                grown.append(jnp.exp(scores[0:8] + scores[8:16]))
            grids_all = []
            for u in ways:
                total = grown[u][:, tile_of(0)]
                for k in range(1, SLOTS):
                    total = total + grown[u][:, tile_of(k)]
                inverse = 1.0 / total
                grids = [zero] * HEADS
                for k in range(SLOTS):
                    alpha = grown[u][:, tile_of(k)] * inverse
                    al_ref[layer, ids[u], :, tile_of(k)] = alpha
                    if k == DEG:
                        spot = own_spot
                    else:
                        spot = jnp.bitwise_and(edge_ref[k : k + 1, ats[u]], GRAPH - 1).astype(f32)
                        spot = jnp.broadcast_to(spot, (16, LANES)).astype(bf16)
                    hit = spots == spot[None]
                    for h in range(HEADS):
                        part = jnp.broadcast_to(alpha[h : h + 1], (16, LANES)).astype(bf16)
                        grids[h] = grids[h] + jnp.where(hit, part[None], zero)
                grids_all.append(grids)
            for u in ways:
                pooled = None
                for h in range(HEADS):
                    upper = jnp.where(first_half, grids_all[u][h], zero).reshape(GRAPH, LANES)
                    lower = jnp.where(first_half, zero, grids_all[u][h]).reshape(GRAPH, LANES)
                    grid = jnp.concatenate([upper, lower], axis=0)
                    att_ref[layer, ids[u], h] = grid
                    total = dot_nn(left[u][head_of(h)], grid)
                    if layer == 0:
                        pre = total + bias_one[head_of(h)]
                        grown_one = jnp.exp(jnp.minimum(pre, 0.0))
                        h_ref[1, head_of(h), ats[u]] = (jnp.maximum(pre, 0.0) + (grown_one - 1.0)).astype(bf16)
                        slope_ref[1, head_of(h), ats[u]] = grown_one
                    else:
                        rounded = total.astype(bf16).astype(f32)
                        pooled = rounded if pooled is None else pooled + rounded
                if layer == 1:
                    pool_ref[:, ats[u]] = (pooled * (1.0 / HEADS) + bias_two).astype(bf16)

    @pl.loop(0, chunks, unroll=4)
    def _(c):
        at = lanes_of(c, chunk)
        logits = dot_nn(wo_t, pool_ref[:, at]) + bias_out
        shifted = logits - jnp.max(logits, axis=0, keepdims=True)
        log_prob = shifted - jnp.log(jnp.sum(jnp.exp(shifted), axis=0, keepdims=True))
        class_id = lax.broadcasted_iota(jnp.int32, (CLASSES, chunk), 0)
        onehot = jnp.where(class_id == mark_ref[0:1, at], 1.0, 0.0)
        share = mark_ref[1:2, at].astype(f32) * inv_count
        term = jnp.sum(((smooth - 1.0) * onehot - smooth / CLASSES) * log_prob, axis=0, keepdims=True)
        loss_ref[...] += term * share
        d_logits = (jnp.exp(log_prob) - (1.0 - smooth) * onehot - smooth / CLASSES) * share
        d_logits = d_logits.astype(bf16)
        dlog_ref[:, at] = d_logits
        d_pooled = (dot_nn(wo_ref[...], d_logits) * (1.0 / HEADS)).astype(bf16)
        for h in range(HEADS):
            do_ref[head_of(h), at] = d_pooled

    for layer in (1, 0):

        @pl.loop(0, blocks // WAYS)
        def _(step):
            ids = [step * WAYS + u for u in range(WAYS)]
            ats = [lanes_of(i, LANES) for i in ids]
            ways = range(WAYS)
            d_out = [do_ref[:, ats[u]] for u in ways]
            d_alpha = []
            for u in ways:
                for h in range(HEADS):
                    d_head = d_out[u][head_of(h)].reshape(4, 16, LANES)
                    for k in range(SLOTS):
                        t = t_ref[layer, ids[u], head_of(h), tile_of(k)].reshape(4, 16, LANES)
                        product = t * d_head
                        sum_ref[u, h * 16 : (h + 1) * 16, tile_of(k)] = (product[0] + product[1]) + (
                            product[2] + product[3]
                        )
                d_alpha.append(dot_nn(fold, sum_ref[u])[0:8])
            for u in ways:
                alpha = al_ref[layer, ids[u]]
                weighted = alpha * d_alpha[u]
                total = weighted[:, tile_of(0)]
                for k in range(1, SLOTS):
                    total = total + weighted[:, tile_of(k)]
                for k in range(SLOTS):
                    d_score = weighted[:, tile_of(k)] - alpha[:, tile_of(k)] * total
                    for h in range(HEADS):
                        one = jnp.broadcast_to(d_score[h : h + 1], (16, LANES))
                        two = (one * leak_slope).astype(bf16)[None]
                        one = one.astype(bf16)[None]
                        t = t_ref[layer, ids[u], head_of(h), tile_of(k)].reshape(4, 16, LANES)
                        w_ref[u, head_of(h), tile_of(k)] = jnp.where(t > 0, one, two).reshape(HSIZE, LANES)
            for u in ways:
                together = jnp.concatenate([e_ref[ids[u]], eye_ref[...]], axis=0)
                spread = dot_nt(w_ref[u, :, 0:mixed], together)
                own = w_ref[u, :, tile_of(DEG)].astype(f32)
                left_w = spread[:, 0:LANES] + own
                right_w = spread[:, LANES : 2 * LANES] + own
                left = both_ref[layer, 0:HID, ats[u]].astype(f32)
                right = both_ref[layer, HID : 2 * HID, ats[u]].astype(f32)
                da_ref[layer] += left * left_w + right * right_w
                wide = a_ref[layer]
                for h in range(HEADS):
                    passed = dot_nt(d_out[u][head_of(h)], att_ref[layer, ids[u], h])
                    d_left = wide[head_of(h)] * left_w[head_of(h)] + passed
                    both_ref[1 + layer, head_of(h), ats[u]] = d_left.astype(bf16)
                both_ref[1 + layer, HID : 2 * HID, ats[u]] = (wide * right_w).astype(bf16)

        @pl.loop(0, chunks, unroll=4)
        def _(c):
            at = lanes_of(c, chunk)
            d_in = dot_nn(wg_ref[layer], both_ref[1 + layer, :, at]).astype(bf16).astype(f32)
            d_in = d_in * slope_ref[layer, :, at]
            do_ref[:, at] = d_in.astype(bf16)
            if layer == 1:
                for k in range(4):
                    gb_ref[...] += d_in[:, tile_of(k)]

    for layer in range(2):
        for side in range(2):
            start = (2 * layer + side) * HID
            out_ref[start : start + HID, :] = dot_nt(
                h_ref[layer], both_ref[1 + layer, side * HID : (side + 1) * HID, :]
            ).astype(bf16)
    ones = jnp.ones((nodes, LANES), bf16)
    with_sums = dot_nn(do_ref[...], jnp.concatenate([node_ref[...], ones], axis=1))
    out_ref[ROW_IN : ROW_IN + FEAT, :] = with_sums[:, 0:FEAT].T.astype(bf16)
    out_ref[ROW_OUT : ROW_OUT + HSIZE, :] = jnp.zeros((HSIZE, HID), bf16)
    out_ref[ROW_OUT : ROW_OUT + HSIZE, 0:CLASSES] = dot_nt(pool_ref[...], dlog_ref[...]).astype(bf16)
    lane_wide = lax.broadcasted_iota(jnp.int32, (HID, LANES), 1)
    columns = jnp.where(lane_wide == 0, with_sums[:, FEAT:], 0.0)
    for layer in range(2):
        da = jnp.sum(da_ref[layer], axis=1, keepdims=True)
        columns = columns + jnp.where(lane_wide == 1 + layer, da, 0.0)
    columns = columns + jnp.where(lane_wide == 3, jnp.sum(gb_ref[...], axis=1, keepdims=True), 0.0)
    g_bias_out = dot_nn(dlog_ref[...], ones)
    g_bias_two = lax.dot_general(
        wo_ref[...].astype(f32), g_bias_out, (((1,), (0,)), ((), ())),
        precision=highest, preferred_element_type=f32,
    )
    loss = jnp.broadcast_to(jnp.sum(loss_ref[...], axis=1, keepdims=True), (8, LANES))
    rest = HID - HSIZE - CLASSES - 8
    last = jnp.concatenate([g_bias_two, g_bias_out, loss, jnp.zeros((rest, LANES), f32)], axis=0)
    columns = columns + jnp.where(lane_wide == 4, last, 0.0)
    out_ref[ROW_MISC : ROW_MISC + 16, :] = parted(columns.T[0:8]).astype(bf16)
    out_ref[ROW_MISC + 16 :, :] = jnp.zeros((ROWS - ROW_MISC - 16, HID), bf16)
    core = jnp.bitwise_and(dom_ref[0], 1)
    width = ROWS // 2
    keep_ref[...] = out_ref[pl.ds(pl.multiple_of(core * width, width), width), :]
    send_out_ref[...] = out_ref[pl.ds(pl.multiple_of((1 - core) * width, width), width), :]


def run_model(
    section_id, dom_id, spot, features, src_all, labels, label_mask, send_index, pieces, shards, small_params
):
    nodes = features.shape[1]
    blocks = nodes // LANES
    scratch = [
        pltpu.VMEM((blocks, LANES, DEG * LANES), bf16),
        pltpu.VMEM((2, blocks, HID, SLOTS * LANES), bf16),
        pltpu.VMEM((2, blocks, 8, SLOTS * LANES), f32),
        pltpu.VMEM((2, blocks, HEADS, LANES, LANES), bf16),
        pltpu.VMEM((2, HID, nodes), bf16),
        pltpu.VMEM((2, HID, nodes), f32),
        pltpu.VMEM((3, 2 * HID, nodes), bf16),
        pltpu.VMEM((HID, nodes), bf16),
        pltpu.VMEM((HSIZE, nodes), bf16),
        pltpu.VMEM((CLASSES, nodes), bf16),
        pltpu.VMEM((WAYS, HID, SLOTS * LANES), bf16),
        pltpu.VMEM((WAYS, HEADS * 16, SLOTS * LANES), bf16),
        pltpu.VMEM((2, HID, LANES), f32),
        pltpu.VMEM((2, HID, LANES), f32),
        pltpu.VMEM((HID, LANES), f32),
        pltpu.VMEM((1, 4 * LANES), f32),
        pltpu.VMEM((nodes, FEAT), bf16),
        pltpu.VMEM((DEG, nodes), jnp.int32),
        pltpu.VMEM((8, nodes), jnp.int32),
        pltpu.VMEM((FEAT, HID), bf16),
        pltpu.VMEM((2, 2 * HID, HID), bf16),
        pltpu.VMEM((2, HID, 2 * HID), bf16),
        pltpu.VMEM((HSIZE, CLASSES), bf16),
        pltpu.VMEM((HSIZE, LANES), f32),
        pltpu.VMEM((2, 16, HID), bf16),
        pltpu.VMEM((ROWS, HID), bf16),
        pltpu.VMEM((LANES, DEG * LANES), bf16),
        pltpu.VMEM((GROUPS, 32, HID), bf16),
    ]
    def body(*refs):
        ahead, cut = (8, 8 + len(pieces))
        after = cut + len(shards)
        head = refs[:ahead] + (refs[ahead:cut], refs[cut:after]) + refs[after:]
        pl.run_scoped(lambda *buffers: model_kernel(*head, *buffers), *scratch)

    grid_spec = pltpu.PrefetchScalarGridSpec(
        num_scalar_prefetch=3,
        grid=(1,),
        in_specs=[
            pl.BlockSpec((1, nodes, FEAT), lambda i, m, d, p: (m[0], 0, 0)),
            pl.BlockSpec((1, DEG, nodes), lambda i, m, d, p: (m[0], 0, 0)),
        ]
        + vmem(4 + len(pieces) + len(shards)),
        out_specs=vmem(2),
    )
    return pl.pallas_call(
        body,
        grid_spec=grid_spec,
        out_shape=[jax.ShapeDtypeStruct((ROWS // 2, HID), bf16)] * 2,
        compiler_params=pltpu.CompilerParams(vmem_limit_bytes=50 * 1024 * 1024),
        name="model",
    )(section_id, dom_id, spot, features, src_all, labels, label_mask, send_index, *pieces, *shards, small_params)


def settled(total, is_last):
    base = ROW_MISC % PIECE
    block = total[base : base + 16]
    block = jnp.where(is_last == 1, parted(block[0:8] + block[8:16]), block)
    return jnp.concatenate([total[:base], block, total[base + 16 :]], axis=0).astype(bf16)


def last_piece(core, section):
    return jnp.where((core == 1) & (section == 3), 1, 0)


def split_kernel(section_ref, dom_ref, keep_ref, got_ref, *out_refs):
    section = section_ref[0]
    core = jnp.bitwise_and(dom_ref[0], 1)
    for j, out_ref in enumerate(out_refs):
        part = jnp.bitwise_xor(section, j)
        at = pl.ds(pl.multiple_of(part * PIECE, PIECE), PIECE)
        total = keep_ref[at, :].astype(f32) + got_ref[at, :].astype(f32)
        out_ref[...] = settled(total, last_piece(core, part))


def join_kernel(section_ref, dom_ref, own_ref, one_ref, two_ref, three_ref, out_ref):
    pair = own_ref[...].astype(f32) + one_ref[...].astype(f32)
    other = two_ref[...].astype(f32) + three_ref[...].astype(f32)
    core = jnp.bitwise_and(dom_ref[0], 1)
    out_ref[...] = settled(pair + other, last_piece(core, section_ref[0]))


def small_call(kernel, name, ids, count, operands):
    shape = jax.ShapeDtypeStruct((PIECE, HID), bf16)
    return pl.pallas_call(
        kernel,
        out_shape=[shape] * count if count > 1 else shape,
        in_specs=[pl.BlockSpec(memory_space=pltpu.SMEM)] * 2 + vmem(len(operands)),
        out_specs=vmem(count) if count > 1 else vmem(1)[0],
        compiler_params=pltpu.CompilerParams(vmem_limit_bytes=8 * 1024 * 1024),
        name=name,
    )(*ids, *operands)


def sum_gradients(ids, keep, send):
    if lax.axis_size("dom") == 8 and lax.axis_size("section") == 4:
        got = crossed(send, "dom", 1)
        parts = small_call(split_kernel, "split", ids, 4, (keep, got))
        came = [crossed(parts[j], "section", j) for j in range(1, 4)]
        mine = small_call(join_kernel, "join", ids, 1, (parts[0], *came))
        came = [crossed(mine, "dom", 2 * j) for j in range(1, 4)]
        mine = small_call(join_kernel, "join", ids, 1, (mine, *came))
        near = [mine] + [crossed(mine, "section", j) for j in range(1, 4)]
        return near + [crossed(piece, "dom", 1) for piece in near], ids
    all_size = lax.axis_size("dom") * lax.axis_size("section")
    swap = jnp.bitwise_and(ids[1][0], 1) == 1
    partial = jnp.concatenate([jnp.where(swap, send, keep), jnp.where(swap, keep, send)], axis=0)
    parts = lax.all_to_all(partial.reshape(all_size, -1, HID), ("section", "dom"), 0, 0)
    mine = jnp.sum(parts.astype(f32), axis=0)
    shared = jnp.broadcast_to(mine.astype(bf16)[None], (all_size,) + mine.shape)
    summed = lax.all_to_all(shared, ("section", "dom"), 0, 0).reshape(8, PIECE, HID)
    return [summed[j] for j in range(8)], (ids[0] * 0, ids[1] * 0)


def adamw_step(parameter, gradient, moment_one, moment_two):
    moment_one = beta_one * moment_one + (1.0 - beta_one) * gradient
    moment_two = beta_two * moment_two + (1.0 - beta_two) * gradient * gradient
    corr_one = 1.0 - beta_one**STEPS
    corr_two = 1.0 - beta_two**STEPS
    update = moment_one / corr_one / (jnp.sqrt(moment_two / corr_two) + adam_eps)
    return (parameter - adam_rate * (update + adam_decay * parameter), moment_one, moment_two)


def average(old_value, new_value):
    return ema_keep * old_value + (1.0 - ema_keep) * new_value


def dot_tn(a, b):
    return lax.dot_general(a, b, (((0,), (0,)), ((), ())), preferred_element_type=f32)


def halves(value):
    high = value.astype(bf16)
    return high, (value - high.astype(f32)).astype(bf16)


def wide_rows(total):
    return max(total, 16)


def own_rows(gradient, start, count):
    total = gradient.shape[0]
    row = lax.broadcasted_iota(jnp.int32, (wide_rows(count), total), 0) + start
    lane = lax.broadcasted_iota(jnp.int32, (wide_rows(count), total), 1)
    pick = jnp.where(row == lane, 1.0, 0.0).astype(bf16)
    return dot_nn(pick, gradient).astype(bf16)


def precondition(gradient, weight, stat_l, stat_r, root_l, root_r, ema, outs, scale, start):
    (new_w, new_l, new_r, new_ema) = outs
    count = weight.shape[0]
    square = (1.0 - shampoo_decay) * scale * scale
    mine = own_rows(gradient, start, count)
    new_l[...] = shampoo_decay * stat_l + square * dot_nt(mine, gradient)[0:count]
    new_r[...] = shampoo_decay * stat_r + square * dot_tn(gradient, gradient)
    high, low = halves(root_l)
    middle = dot_nn(high, gradient) + dot_nn(low, gradient)
    m_high, m_low = halves(middle * scale)
    r_high, r_low = halves(root_r)
    update = dot_nn(m_high, r_high) + dot_nn(m_low, r_high) + dot_nn(m_high, r_low)
    weight = weight - shampoo_rate * (update + weight_decay * weight)
    new_w[...] = weight
    new_ema[...] = average(ema, weight)


def update_kernel(
    dom_ref,
    section_ref,
    spot_ref,
    piece_0,
    piece_1,
    piece_2,
    piece_3,
    piece_4,
    piece_5,
    piece_6,
    piece_7,
    w_in,
    w_gat,
    w_out,
    small,
    l_in,
    r_in,
    l_gat,
    r_gat,
    l_out,
    r_out,
    rl_in,
    rr_in,
    rl_gat,
    rr_gat,
    rl_out,
    rr_out,
    first,
    second,
    e_in,
    e_gat,
    e_out,
    e_small,
    n_w_in,
    n_w_gat,
    n_w_out,
    n_small,
    n_l_in,
    n_r_in,
    n_l_gat,
    n_r_gat,
    n_l_out,
    n_r_out,
    n_first,
    n_second,
    n_e_in,
    n_e_gat,
    n_e_out,
    n_e_small,
    loss_ref,
    norm_ref,
    sum_ref,
):
    dom = dom_ref[0]
    core = jnp.bitwise_and(spot_ref[0], 1)
    pieces = (piece_0, piece_1, piece_2, piece_3, piece_4, piece_5, piece_6, piece_7)
    for j, piece in enumerate(pieces):
        spot = jnp.bitwise_xor(core, j >> 2) * 4 + jnp.bitwise_xor(section_ref[0], j & 3)
        sum_ref[pl.ds(pl.multiple_of(spot * PIECE, PIECE), PIECE), :] = piece[...]
    grads = sum_ref[0:ROW_MISC, :].astype(f32)
    squares = jnp.sum(grads * grads)
    misc = sum_ref[ROW_MISC : ROW_MISC + 16, :].astype(f32)
    misc = misc[0:8] + misc[8:16]
    row = lax.broadcasted_iota(jnp.int32, (8, HID), 0)
    lane = lax.broadcasted_iota(jnp.int32, (8, HID), 1)
    spot = HSIZE + CLASSES
    loss_ref[0] = jnp.sum(jnp.where((row == 4) & (lane == spot), misc, 0.0))
    small_part = jnp.where((row < 4) | ((row == 4) & (lane < spot)), misc, 0.0)
    squares = squares + jnp.sum(small_part * small_part)
    norm = jnp.sqrt(jnp.broadcast_to(squares, (1, 1)))
    scale = jnp.minimum(1.0, clip_norm / norm)
    norm_ref[0] = jnp.sum(norm)
    for layer in range(2):
        for side in range(2):
            at = (layer, side)
            begin = (2 * layer + side) * HID
            precondition(
                sum_ref[begin : begin + HID, :],
                w_gat[at],
                l_gat[at],
                r_gat[at],
                rl_gat[at],
                rr_gat[at],
                e_gat[at],
                (n_w_gat.at[at], n_l_gat.at[at], n_r_gat.at[at], n_e_gat.at[at]),
                scale,
                dom * w_gat.shape[2],
            )
    precondition(
        sum_ref[ROW_IN:ROW_OUT, :],
        w_in[...],
        l_in[...],
        r_in[...],
        rl_in[...],
        rr_in[...],
        e_in[...],
        (n_w_in, n_l_in, n_r_in, n_e_in),
        scale,
        dom * w_in.shape[0],
    )
    precondition(
        sum_ref[ROW_OUT:ROW_MISC, 0:CLASSES],
        w_out[...],
        l_out[...],
        r_out[...],
        rl_out[...],
        rr_out[...],
        e_out[...],
        (n_w_out, n_l_out, n_r_out, n_e_out),
        scale,
        dom * w_out.shape[0],
    )
    for place in range(5):
        width = HID if place < 4 else spot
        at = pl.ds(place * HID, width)
        gradient = misc[place : place + 1, 0:width] * scale

        def line(ref):
            return ref[at].reshape(1, width)

        new_value, moment_one, moment_two = adamw_step(line(small), gradient, line(first), line(second))
        n_small[at] = new_value.reshape(width)
        n_first[at] = moment_one.reshape(width)
        n_second[at] = moment_two.reshape(width)
        n_e_small[at] = average(line(e_small), new_value).reshape(width)


def per_device(
    features,
    sources,
    send_index,
    labels,
    label_mask,
    w_in,
    w_gat,
    w_out,
    small_params,
    stat_l_in,
    stat_r_in,
    stat_l_gat,
    stat_r_gat,
    stat_l_out,
    stat_r_out,
    root_l_in,
    root_r_in,
    root_l_gat,
    root_r_gat,
    root_l_out,
    root_r_out,
    adam_first,
    adam_second,
    ema_in,
    ema_gat,
    ema_out,
    ema_small,
):
    dom_id = lax.axis_index("dom").astype(jnp.int32).reshape(1)
    section_id = lax.axis_index("section").astype(jnp.int32).reshape(1)
    size = lax.axis_size("dom")
    src_all = jnp.swapaxes(sources, 1, 2)
    packed = pack_inputs(section_id, features, src_all, labels, label_mask, send_index, w_in, w_gat, w_out)
    pieces, spot = gather_weights(dom_id, packed, w_in, w_gat, w_out, label_mask)
    shards = ()
    if size == GROUPS:
        (pieces, shards) = (pieces[1:], (w_in, w_gat, w_out))
    keep, send = run_model(
        section_id,
        dom_id,
        spot,
        features,
        src_all,
        labels,
        label_mask,
        send_index,
        pieces,
        shards,
        small_params,
    )
    pieces, spots = sum_gradients((section_id, dom_id), keep, send)
    state = (
        w_in,
        w_gat,
        w_out,
        small_params,
        stat_l_in,
        stat_r_in,
        stat_l_gat,
        stat_r_gat,
        stat_l_out,
        stat_r_out,
        root_l_in,
        root_r_in,
        root_l_gat,
        root_r_gat,
        root_l_out,
        root_r_out,
        adam_first,
        adam_second,
        ema_in,
        ema_gat,
        ema_out,
        ema_small,
    )
    like = state[:10] + (adam_first, adam_second, ema_in, ema_gat, ema_out, ema_small)
    results = pl.pallas_call(
        update_kernel,
        out_shape=[jax.ShapeDtypeStruct(v.shape, f32) for v in like] + [jax.ShapeDtypeStruct((1,), f32)] * 2,
        in_specs=[pl.BlockSpec(memory_space=pltpu.SMEM)] * 3 + vmem(30),
        out_specs=vmem(16) + [pl.BlockSpec(memory_space=pltpu.SMEM)] * 2,
        scratch_shapes=[pltpu.VMEM((ROWS, HID), bf16)],
        compiler_params=pltpu.CompilerParams(vmem_limit_bytes=16 * 1024 * 1024),
        name="update",
    )(dom_id, *spots, *pieces, *state)
    return tuple(results[:16]) + (results[16].reshape(()), results[17].reshape(()))


def solution(mesh):
    placed = (
        P(None, "dom", None),
        P(None, "dom", None),
        P(None, "dom"),
        P(None, "dom"),
        P(None, "dom"),
        P("dom", None),
        P(None, None, "dom", None),
        P("dom", None),
        P(),
        P("dom", None),
        P(),
        P(None, None, "dom", None),
        P(),
        P("dom", None),
        P(),
        P("dom", None),
        P(),
        P(None, None, "dom", None),
        P(),
        P("dom", None),
        P(),
        P(),
        P(),
        P("dom", None),
        P(None, None, "dom", None),
        P("dom", None),
        P(),
    )
    return jax.shard_map(
        per_device,
        mesh=mesh,
        in_specs=placed,
        out_specs=(
            P("dom", None),
            P(None, None, "dom", None),
            P("dom", None),
            P(),
            P("dom", None),
            P(),
            P(None, None, "dom", None),
            P(),
            P("dom", None),
            P(),
            P(),
            P(),
            P("dom", None),
            P(None, None, "dom", None),
            P("dom", None),
            P(),
            P(),
            P(),
        ),
        check_vma=False,
    )
```

```python
import jax
import jax.numpy as jnp
from jax import lax
from jax.experimental import pallas as pl
from jax.experimental.pallas import tpu as pltpu
from jax.sharding import PartitionSpec as P

FEAT = 128
HEADS = 4
HSIZE = 64
CLASSES = 40
STEPS = 5
HID = 256
SMALL = 1128


highest = lax.Precision.HIGHEST
leak_slope = 0.2
smooth = 0.1
clip_norm = 0.001
shampoo_rate = 0.3
shampoo_decay = 0.5
weight_decay = 0.0001
adam_rate = 0.1
beta_one = 0.9
beta_two = 0.999
adam_eps = 1e-08
adam_decay = 0.01
ema_keep = 0.9


def split_small(small_params):
    bias_in = small_params[0:HID]
    attention = small_params[HID : 3 * HID].reshape(2, HEADS, HSIZE)
    bias_one = small_params[3 * HID : 4 * HID]
    bias_two = small_params[4 * HID : 4 * HID + HSIZE]
    bias_out = small_params[4 * HID + HSIZE :]
    return (bias_in, attention, bias_one, bias_two, bias_out)


GRAPH = 64
LANES = 128
DEG = 8
SLOTS = DEG + 1
WAYS = 4
ROWS = 1280
GROUPS = 8
IN_G = FEAT // GROUPS
GAT_G = HID // GROUPS
OUT_G = HSIZE // GROUPS
TAIL_G = IN_G + 4 * GAT_G
PACK_G = TAIL_G + 2 * OUT_G
HALO_G = PACK_G + 16
CODES = slice(HID - LANES, HID)
PIECE = ROWS // 8
HALF = GRAPH // 2
ROW_IN = 4 * HID
ROW_OUT = ROW_IN + FEAT
ROW_MISC = ROW_OUT + HSIZE

bf16 = jnp.bfloat16
f32 = jnp.float32


def dot_nn(a, b):
    return lax.dot_general(a, b, (((1,), (0,)), ((), ())), preferred_element_type=f32)


def dot_nt(a, b):
    return lax.dot_general(a, b, (((1,), (1,)), ((), ())), preferred_element_type=f32)


def tile_of(k):
    return slice(k * LANES, (k + 1) * LANES)


def head_of(h):
    return slice(h * HSIZE, (h + 1) * HSIZE)


def row_of(ref, micro, width):
    picked = ref[0:1, 0:width]
    for other in range(1, ref.shape[0]):
        picked = jnp.where(micro == other, ref[other : other + 1, 0:width], picked)
    return picked


def pack_kernel(
    section_ref,
    feat_ref,
    src_ref,
    lab_ref,
    msk_ref,
    send_ref,
    win_ref,
    wgat_ref,
    wout_ref,
    pack_ref,
    tail_ref,
):
    micro = section_ref[0]
    nodes = lab_ref.shape[1]
    pack_ref[PACK_G:HALO_G, 0:FEAT] = feat_ref[0, 0:16]
    pack_ref[PACK_G:HALO_G, FEAT : 2 * FEAT] = feat_ref[0, 16:32]
    shift = LANES - HALF
    tail_ref[...] = jnp.zeros_like(tail_ref)
    far = src_ref[0]
    far = jnp.where(far >= nodes, far - nodes + GRAPH, far)
    tail_ref[0:DEG, CODES] = pltpu.roll(far, shift, 1).astype(f32)
    tail_ref[DEG : DEG + 1, CODES] = pltpu.roll(row_of(lab_ref, micro, LANES), shift, 1).astype(f32)
    tail_ref[DEG + 1 : DEG + 2, CODES] = pltpu.roll(row_of(msk_ref, micro, LANES), shift, 1).astype(f32)
    send = row_of(send_ref, micro, 2 * HALF)
    tail_ref[DEG + 2 : DEG + 3, CODES] = jnp.concatenate([send, send], axis=1).astype(f32)
    if win_ref.shape[0] != IN_G:
        pack_ref[0:TAIL_G, :] = jnp.zeros((TAIL_G, HID), bf16)
        pack_ref[TAIL_G:PACK_G, :] = tail_ref[...].astype(bf16)
        return
    pack_ref[0:IN_G, :] = win_ref[...].astype(bf16)
    for layer in range(2):
        for side in range(2):
            start = IN_G + (2 * layer + side) * GAT_G
            pack_ref[start : start + GAT_G, :] = wgat_ref[layer, side].astype(bf16)
    tail_ref[0:OUT_G, 0:CLASSES] = wout_ref[...]
    count = jnp.sum(jnp.sum(msk_ref[...].astype(f32), axis=1, keepdims=True), axis=0, keepdims=True)
    high = jnp.floor(count * (1.0 / 256.0))
    lane = lax.broadcasted_iota(jnp.int32, (1, LANES), 1)
    low = jnp.where(lane == 1, count - 256.0 * high, 0.0)
    tail_ref[OUT_G : OUT_G + 1, 0:LANES] = jnp.where(lane == 0, high, low)
    pack_ref[TAIL_G:PACK_G, :] = tail_ref[...].astype(bf16)


def vmem(count):
    return [pl.BlockSpec(memory_space=pltpu.VMEM)] * count


def pack_inputs(section_id, features, src_all, labels, label_mask, send_index, w_in, w_gat, w_out):
    grid_spec = pltpu.PrefetchScalarGridSpec(
        num_scalar_prefetch=1,
        grid=(1,),
        in_specs=[
            pl.BlockSpec((1, HALF, FEAT), lambda i, m: (m[0], 0, 0)),
            pl.BlockSpec((1, DEG, LANES), lambda i, m: (m[0], 0, 0)),
        ]
        + vmem(6),
        out_specs=vmem(1)[0],
        scratch_shapes=[pltpu.VMEM((2 * OUT_G, HID), f32)],
    )
    return pl.pallas_call(
        pack_kernel,
        grid_spec=grid_spec,
        out_shape=jax.ShapeDtypeStruct((HALO_G, HID), bf16),
        compiler_params=pltpu.CompilerParams(vmem_limit_bytes=58 * 1024 * 1024),
        name="pack",
    )(section_id, features, src_all, labels, label_mask, send_index, w_in, w_gat, w_out)


def crossed(value, axis, mask):
    return lax.ppermute(value, axis, [(i, i ^ mask) for i in range(lax.axis_size(axis))])


def gather_weights(dom_id, packed, w_in, w_gat, w_out, label_mask):
    size = lax.axis_size("dom")
    if size == GROUPS:
        near = [packed] + [crossed(packed, "dom", 2 * j) for j in range(1, 4)]
        return near + [crossed(piece, "dom", 1) for piece in near], dom_id
    halo = lax.ppermute(packed[TAIL_G:], "dom", [((i + 1) % size, i) for i in range(size)])
    halo = jnp.broadcast_to(halo[None], (GROUPS,) + halo.shape)
    rows_in, rows_gat, rows_out = (w_in.shape[0], w_gat.shape[2], w_out.shape[0])
    count = jnp.sum(label_mask)
    digits = jnp.stack([lax.div(count, 256), lax.rem(count, 256)]).astype(bf16)
    packed = jnp.concatenate(
        [
            w_in.astype(bf16),
            w_gat.astype(bf16).reshape(4 * rows_gat, HID),
            jnp.pad(w_out.astype(bf16), ((0, 0), (0, HID - CLASSES))),
            jnp.pad(digits[None, :], ((0, 0), (0, HID - 2))),
        ],
        axis=0,
    )
    whole = lax.all_gather(packed, "dom", axis=0, tiled=False)
    cut = rows_in + 4 * rows_gat
    part_in = whole[:, :rows_in].reshape(GROUPS, IN_G, HID)
    part_gat = whole[:, rows_in:cut].reshape(GROUPS, size // GROUPS, 4, rows_gat, HID)
    part_gat = part_gat.transpose(0, 2, 1, 3, 4).reshape(GROUPS, 4 * GAT_G, HID)
    part_out = whole[:, cut : cut + rows_out].reshape(GROUPS, OUT_G, HID)
    counts = whole[:, cut + rows_out].reshape(GROUPS, size // GROUPS, HID)
    counts = jnp.pad(counts, ((0, 0), (0, OUT_G - size // GROUPS), (0, 0)))
    tail = jnp.concatenate([part_out, counts], axis=1)
    tail = jnp.concatenate([tail[:, :, :LANES], halo[:, : 2 * OUT_G, LANES:]], axis=2)
    whole = jnp.concatenate([part_in, part_gat, tail, halo[:, 2 * OUT_G :]], axis=1)
    return [whole[g] for g in (0, 2, 4, 6, 1, 3, 5, 7)], dom_id * 0


def parted(rows):
    high = rows.astype(bf16).astype(f32)
    return jnp.concatenate([high, rows - high], axis=0)


def column_of(row):
    return jnp.broadcast_to(row.reshape(1, -1), (LANES, row.shape[0])).T


def model_kernel(
    section_ref,
    dom_ref,
    spot_ref,
    feat_ref,
    src_ref,
    lab_ref,
    msk_ref,
    send_ref,
    piece_refs,
    shard_refs,
    small_ref,
    keep_ref,
    send_out_ref,
    e_ref,
    t_ref,
    al_ref,
    att_ref,
    h_ref,
    slope_ref,
    both_ref,
    do_ref,
    pool_ref,
    dlog_ref,
    w_ref,
    sum_ref,
    a_ref,
    da_ref,
    gb_ref,
    loss_ref,
    node_ref,
    edge_ref,
    mark_ref,
    wi_ref,
    wgt_ref,
    wg_ref,
    wo_ref,
    wof_ref,
    am_ref,
    out_ref,
    eye_ref,
    halo_ref,
):
    nodes = feat_ref.shape[1]
    blocks = nodes // LANES
    chunk = 4 * LANES
    chunks = nodes // chunk
    mixed = DEG * LANES
    micro = section_ref[0]
    after = jnp.bitwise_and(spot_ref[0] + 1, GROUPS - 1)
    final = nodes - LANES

    digits = jnp.zeros((OUT_G, LANES), f32)
    own_count = jnp.zeros((1, 1), f32)
    first = GROUPS - len(piece_refs)
    if first == 1:
        (win_ref, wgat_ref, wout_ref) = shard_refs
        group = spot_ref[0]
        at_in = pl.ds(pl.multiple_of(group * IN_G, IN_G), IN_G)
        at_gat = pl.ds(pl.multiple_of(group * GAT_G, GAT_G), GAT_G)
        at_out = pl.ds(pl.multiple_of(group * OUT_G, OUT_G), OUT_G)
        wi_ref[at_in, :] = win_ref[...].astype(bf16)
        for layer in range(2):
            for side in range(2):
                wg_ref[layer, at_gat, side * HID : (side + 1) * HID] = wgat_ref[layer, side].astype(bf16)
        wof_ref[at_out, :] = jnp.zeros((OUT_G, LANES), f32)
        wof_ref[at_out, 0:CLASSES] = wout_ref[...]
        marked = jnp.sum(msk_ref[...].astype(f32), axis=1, keepdims=True)
        own_count = jnp.sum(marked, axis=0, keepdims=True)
    for j, piece in enumerate(piece_refs, first):
        group = jnp.bitwise_xor(spot_ref[0], 2 * (j & 3) + (j >> 2))

        def rows_of(width):
            return pl.ds(pl.multiple_of(group * width, width), width)

        wi_ref[rows_of(IN_G), :] = piece[0:IN_G, :]
        for layer in range(2):
            for side in range(2):
                start = IN_G + (2 * layer + side) * GAT_G
                wg_ref[layer, rows_of(GAT_G), side * HID : (side + 1) * HID] = piece[start : start + GAT_G, :]
        tail = piece[TAIL_G:PACK_G, :].astype(f32)
        wof_ref[rows_of(OUT_G), :] = tail[0:OUT_G, 0:LANES]
        digits = digits + tail[OUT_G : 2 * OUT_G, 0:LANES]
        halo_ref[group] = piece[TAIL_G:HALO_G, :]

    node_ref[0 : nodes - HALF, :] = feat_ref[0, HALF:nodes, :]
    node_ref[nodes - HALF : nodes - 16, :] = halo_ref[after, 16:32, 0:FEAT]
    node_ref[nodes - 16 : nodes, :] = halo_ref[after, 16:32, FEAT : 2 * FEAT]
    ints = halo_ref[after, 0:16, CODES].astype(f32).astype(jnp.int32)
    lane_row = lax.broadcasted_iota(jnp.int32, (1, LANES), 1)
    kept = lane_row < LANES - HALF
    edge_ref[...] = pltpu.roll(src_ref[0], nodes - HALF, 1)
    edge_ref[:, final:nodes] = jnp.where(
        kept,
        edge_ref[:, final:nodes],
        jnp.where(ints[0:DEG] >= GRAPH, ints[0:DEG] + (nodes - GRAPH), ints[0:DEG]),
    )
    for place, ref in enumerate((lab_ref, msk_ref)):
        mark_ref[place : place + 1, :] = pltpu.roll(row_of(ref, micro, nodes), nodes - HALF, 1)
        came = ints[DEG + place : DEG + place + 1]
        mark_ref[place : place + 1, final:nodes] = jnp.where(kept, mark_ref[place : place + 1, final:nodes], came)
    send = row_of(send_ref, micro, 2 * HALF)
    send = jnp.concatenate([send, send], axis=1)
    arrived = pltpu.roll(ints[DEG + 2 : DEG + 3], HALF, 1)
    table = jnp.where(
        lane_row < HALF, pltpu.roll(send, HALF, 1) - (nodes - HALF), arrived + HALF
    )
    spot_row = lax.broadcasted_iota(jnp.int32, (GRAPH, LANES), 0)
    spot_lane = lax.broadcasted_iota(jnp.int32, (GRAPH, LANES), 1)
    table = jnp.sum(jnp.where(spot_row == spot_lane, table.astype(f32), 0.0), axis=1, keepdims=True)
    looked = []
    for k in range(DEG):
        far = edge_ref[k : k + 1, final:nodes] - nodes == spot_row
        looked.append(jnp.sum(jnp.where(far, table, 0.0), axis=0, keepdims=True))
    looked = jnp.concatenate(looked, axis=0).astype(jnp.int32)
    raw = edge_ref[:, final:nodes]
    looked = jnp.where(raw >= nodes, looked, jnp.bitwise_and(raw - HALF, GRAPH - 1))
    local = jnp.bitwise_and(edge_ref[...] - HALF, GRAPH - 1)
    lane_all = lax.broadcasted_iota(jnp.int32, (DEG, nodes), 1)
    second = jnp.bitwise_and(lane_all, GRAPH)
    edge_ref[...] = local + second
    edge_ref[:, final:nodes] = looked + jnp.bitwise_and(
        lax.broadcasted_iota(jnp.int32, (DEG, LANES), 1), GRAPH
    )

    for layer in range(2):
        for side in range(2):
            wgt_ref[layer, side * HID : (side + 1) * HID, :] = wg_ref[
                layer, :, side * HID : (side + 1) * HID
            ].T
    wi_t = wi_ref[...].T
    wo_ref[...] = wof_ref[:, 0:CLASSES].astype(bf16)
    wo_t = wof_ref[...].T[0:CLASSES].astype(bf16)
    digits = jnp.sum(digits, axis=0, keepdims=True)
    inv_count = 1.0 / (digits[:, 0:1] * 256.0 + digits[:, 1:2] + own_count)

    row_id = lax.broadcasted_iota(jnp.int32, (LANES, LANES), 0)
    lane_id = lax.broadcasted_iota(jnp.int32, (LANES, LANES), 1)
    eye = jnp.where(row_id == lane_id, 1.0, 0.0).astype(bf16)
    head_row = lax.broadcasted_iota(jnp.int32, (16, HID), 0)
    head_col = lax.broadcasted_iota(jnp.int32, (16, HID), 1)
    head_mask = jnp.where(head_col // HSIZE == head_row, 1.0, 0.0)

    bias_in = column_of(small_ref[0:HID])[:, 0:1]
    bias_one = column_of(small_ref[3 * HID : 4 * HID])[:, 0:1]
    bias_two = column_of(small_ref[4 * HID : 4 * HID + HSIZE])[:, 0:1]
    bias_out = column_of(small_ref[4 * HID + HSIZE : SMALL])[:, 0:1]
    for layer in range(2):
        row = small_ref[(1 + layer) * HID : (2 + layer) * HID]
        a_ref[layer] = column_of(row)
        row = row.reshape(1, HID)
        high = row.astype(bf16).astype(f32)
        am_ref[layer] = jnp.concatenate([head_mask[0:8] * high, head_mask[0:8] * (row - high)], axis=0).astype(bf16)
    fold_row = lax.broadcasted_iota(jnp.int32, (16, HEADS * 16), 0)
    fold_col = lax.broadcasted_iota(jnp.int32, (16, HEADS * 16), 1)
    fold = jnp.where(fold_col // 16 == fold_row, 1.0, 0.0).astype(bf16)
    spots = lax.broadcasted_iota(jnp.int32, (GRAPH, LANES), 0).astype(f32).astype(bf16)
    spots = spots.reshape(4, 16, LANES)
    half_lane = lax.broadcasted_iota(jnp.int32, (16, LANES), 1)
    first_half = (half_lane < GRAPH).astype(f32).astype(bf16)[None] > 0
    own_spot = jnp.bitwise_and(half_lane, GRAPH - 1).astype(f32).astype(bf16)
    zero = jnp.zeros((4, 16, LANES), bf16)
    da_ref[...] = jnp.zeros_like(da_ref)
    gb_ref[...] = jnp.zeros_like(gb_ref)
    loss_ref[...] = jnp.zeros_like(loss_ref)

    def lanes_of(i, width):
        return pl.ds(pl.multiple_of(i * width, width), width)

    @pl.loop(0, chunks, unroll=4)
    def _(c):
        at = lanes_of(c, chunk)
        pre = dot_nt(wi_t, node_ref[at, :]) + bias_in
        grown = jnp.exp(jnp.minimum(pre, 0.0))
        h_ref[0, :, at] = (jnp.maximum(pre, 0.0) + (grown - 1.0)).astype(bf16)
        slope_ref[0, :, at] = grown

    wide_spots = lax.broadcasted_iota(jnp.int32, (LANES, LANES), 0).astype(f32).astype(bf16)
    wide_spots = wide_spots.reshape(8, 16, LANES)
    for k in range(DEG):
        eye_ref[:, tile_of(k)] = eye

    def one_hot(u_at):
        parts = []
        for k in range(DEG):
            spot = jnp.broadcast_to(edge_ref[k : k + 1, u_at].astype(f32), (16, LANES)).astype(bf16)
            hit = wide_spots == spot[None]
            hit = jnp.where(hit, jnp.ones((8, 16, LANES), bf16), jnp.zeros((8, 16, LANES), bf16))
            parts.append(hit.reshape(LANES, LANES))
        return parts

    for layer in range(2):

        @pl.loop(0, chunks, unroll=4)
        def _(c):
            at = lanes_of(c, chunk)
            both_ref[layer, :, at] = dot_nn(wgt_ref[layer], h_ref[layer, :, at]).astype(bf16)

        @pl.loop(0, blocks // WAYS)
        def _(step):
            ids = [step * WAYS + u for u in range(WAYS)]
            ats = [lanes_of(i, LANES) for i in ids]
            ways = range(WAYS)
            left = [both_ref[layer, 0:HID, ats[u]] for u in ways]
            grown = []
            for u in ways:
                right = both_ref[layer, HID : 2 * HID, ats[u]]
                left_f = left[u].astype(f32)
                if layer == 0:
                    parts = one_hot(ats[u])
                    for k in range(DEG):
                        e_ref[ids[u], :, tile_of(k)] = parts[k]
                    hot = jnp.concatenate(parts[0:2], axis=1)
                else:
                    hot = e_ref[ids[u], :, 0 : 2 * LANES]
                mixed_rows = [dot_nn(left[u], hot).astype(bf16)]
                for k in range(2, DEG):
                    index = jnp.broadcast_to(edge_ref[k : k + 1, ats[u]], (HID, LANES))
                    picked = jnp.take_along_axis(left_f, index, axis=1, mode="promise_in_bounds")
                    mixed_rows.append(picked.astype(bf16))
                mixed_rows = jnp.concatenate(mixed_rows, axis=1)
                mixed_rows = mixed_rows + jnp.concatenate([right] * DEG, axis=1)
                own = left[u] + right
                t_ref[layer, ids[u], :, 0:mixed] = mixed_rows
                t_ref[layer, ids[u], :, tile_of(DEG)] = own
                t = jnp.concatenate([mixed_rows, own], axis=1)
                z = jnp.maximum(t, t * leak_slope)
                scores = dot_nn(am_ref[layer], z)
                grown.append(jnp.exp(scores[0:8] + scores[8:16]))
            grids_all = []
            for u in ways:
                total = grown[u][:, tile_of(0)]
                for k in range(1, SLOTS):
                    total = total + grown[u][:, tile_of(k)]
                inverse = 1.0 / total
                grids = [zero] * HEADS
                for k in range(SLOTS):
                    alpha = grown[u][:, tile_of(k)] * inverse
                    al_ref[layer, ids[u], :, tile_of(k)] = alpha
                    if k == DEG:
                        spot = own_spot
                    else:
                        spot = jnp.bitwise_and(edge_ref[k : k + 1, ats[u]], GRAPH - 1).astype(f32)
                        spot = jnp.broadcast_to(spot, (16, LANES)).astype(bf16)
                    hit = spots == spot[None]
                    for h in range(HEADS):
                        part = jnp.broadcast_to(alpha[h : h + 1], (16, LANES)).astype(bf16)
                        grids[h] = grids[h] + jnp.where(hit, part[None], zero)
                grids_all.append(grids)
            for u in ways:
                pooled = None
                for h in range(HEADS):
                    upper = jnp.where(first_half, grids_all[u][h], zero).reshape(GRAPH, LANES)
                    lower = jnp.where(first_half, zero, grids_all[u][h]).reshape(GRAPH, LANES)
                    grid = jnp.concatenate([upper, lower], axis=0)
                    att_ref[layer, ids[u], h] = grid
                    total = dot_nn(left[u][head_of(h)], grid)
                    if layer == 0:
                        pre = total + bias_one[head_of(h)]
                        grown_one = jnp.exp(jnp.minimum(pre, 0.0))
                        h_ref[1, head_of(h), ats[u]] = (jnp.maximum(pre, 0.0) + (grown_one - 1.0)).astype(bf16)
                        slope_ref[1, head_of(h), ats[u]] = grown_one
                    else:
                        rounded = total.astype(bf16).astype(f32)
                        pooled = rounded if pooled is None else pooled + rounded
                if layer == 1:
                    pool_ref[:, ats[u]] = (pooled * (1.0 / HEADS) + bias_two).astype(bf16)

    @pl.loop(0, chunks, unroll=4)
    def _(c):
        at = lanes_of(c, chunk)
        logits = dot_nn(wo_t, pool_ref[:, at]) + bias_out
        shifted = logits - jnp.max(logits, axis=0, keepdims=True)
        log_prob = shifted - jnp.log(jnp.sum(jnp.exp(shifted), axis=0, keepdims=True))
        class_id = lax.broadcasted_iota(jnp.int32, (CLASSES, chunk), 0)
        onehot = jnp.where(class_id == mark_ref[0:1, at], 1.0, 0.0)
        share = mark_ref[1:2, at].astype(f32) * inv_count
        term = jnp.sum(((smooth - 1.0) * onehot - smooth / CLASSES) * log_prob, axis=0, keepdims=True)
        loss_ref[...] += term * share
        d_logits = (jnp.exp(log_prob) - (1.0 - smooth) * onehot - smooth / CLASSES) * share
        d_logits = d_logits.astype(bf16)
        dlog_ref[:, at] = d_logits
        d_pooled = (dot_nn(wo_ref[...], d_logits) * (1.0 / HEADS)).astype(bf16)
        for h in range(HEADS):
            do_ref[head_of(h), at] = d_pooled

    for layer in (1, 0):

        @pl.loop(0, blocks // WAYS)
        def _(step):
            ids = [step * WAYS + u for u in range(WAYS)]
            ats = [lanes_of(i, LANES) for i in ids]
            ways = range(WAYS)
            d_out = [do_ref[:, ats[u]] for u in ways]
            d_alpha = []
            for u in ways:
                for h in range(HEADS):
                    d_head = d_out[u][head_of(h)].reshape(4, 16, LANES)
                    for k in range(SLOTS):
                        t = t_ref[layer, ids[u], head_of(h), tile_of(k)].reshape(4, 16, LANES)
                        product = t * d_head
                        sum_ref[u, h * 16 : (h + 1) * 16, tile_of(k)] = (product[0] + product[1]) + (
                            product[2] + product[3]
                        )
                d_alpha.append(dot_nn(fold, sum_ref[u])[0:8])
            for u in ways:
                alpha = al_ref[layer, ids[u]]
                weighted = alpha * d_alpha[u]
                total = weighted[:, tile_of(0)]
                for k in range(1, SLOTS):
                    total = total + weighted[:, tile_of(k)]
                for k in range(SLOTS):
                    d_score = weighted[:, tile_of(k)] - alpha[:, tile_of(k)] * total
                    for h in range(HEADS):
                        one = jnp.broadcast_to(d_score[h : h + 1], (16, LANES))
                        two = (one * leak_slope).astype(bf16)[None]
                        one = one.astype(bf16)[None]
                        t = t_ref[layer, ids[u], head_of(h), tile_of(k)].reshape(4, 16, LANES)
                        w_ref[u, head_of(h), tile_of(k)] = jnp.where(t > 0, one, two).reshape(HSIZE, LANES)
            for u in ways:
                together = jnp.concatenate([e_ref[ids[u]], eye_ref[...]], axis=0)
                spread = dot_nt(w_ref[u, :, 0:mixed], together)
                own = w_ref[u, :, tile_of(DEG)].astype(f32)
                left_w = spread[:, 0:LANES] + own
                right_w = spread[:, LANES : 2 * LANES] + own
                left = both_ref[layer, 0:HID, ats[u]].astype(f32)
                right = both_ref[layer, HID : 2 * HID, ats[u]].astype(f32)
                da_ref[layer] += left * left_w + right * right_w
                wide = a_ref[layer]
                for h in range(HEADS):
                    passed = dot_nt(d_out[u][head_of(h)], att_ref[layer, ids[u], h])
                    d_left = wide[head_of(h)] * left_w[head_of(h)] + passed
                    both_ref[1 + layer, head_of(h), ats[u]] = d_left.astype(bf16)
                both_ref[1 + layer, HID : 2 * HID, ats[u]] = (wide * right_w).astype(bf16)

        @pl.loop(0, chunks, unroll=4)
        def _(c):
            at = lanes_of(c, chunk)
            d_in = dot_nn(wg_ref[layer], both_ref[1 + layer, :, at]).astype(bf16).astype(f32)
            d_in = d_in * slope_ref[layer, :, at]
            do_ref[:, at] = d_in.astype(bf16)
            if layer == 1:
                for k in range(4):
                    gb_ref[...] += d_in[:, tile_of(k)]

    for layer in range(2):
        for side in range(2):
            start = (2 * layer + side) * HID
            out_ref[start : start + HID, :] = dot_nt(
                h_ref[layer], both_ref[1 + layer, side * HID : (side + 1) * HID, :]
            ).astype(bf16)
    ones = jnp.ones((nodes, LANES), bf16)
    with_sums = dot_nn(do_ref[...], jnp.concatenate([node_ref[...], ones], axis=1))
    out_ref[ROW_IN : ROW_IN + FEAT, :] = with_sums[:, 0:FEAT].T.astype(bf16)
    out_ref[ROW_OUT : ROW_OUT + HSIZE, :] = jnp.zeros((HSIZE, HID), bf16)
    out_ref[ROW_OUT : ROW_OUT + HSIZE, 0:CLASSES] = dot_nt(pool_ref[...], dlog_ref[...]).astype(bf16)
    lane_wide = lax.broadcasted_iota(jnp.int32, (HID, LANES), 1)
    columns = jnp.where(lane_wide == 0, with_sums[:, FEAT:], 0.0)
    for layer in range(2):
        da = jnp.sum(da_ref[layer], axis=1, keepdims=True)
        columns = columns + jnp.where(lane_wide == 1 + layer, da, 0.0)
    columns = columns + jnp.where(lane_wide == 3, jnp.sum(gb_ref[...], axis=1, keepdims=True), 0.0)
    g_bias_out = dot_nn(dlog_ref[...], ones)
    g_bias_two = lax.dot_general(
        wo_ref[...].astype(f32), g_bias_out, (((1,), (0,)), ((), ())),
        precision=highest, preferred_element_type=f32,
    )
    loss = jnp.broadcast_to(jnp.sum(loss_ref[...], axis=1, keepdims=True), (8, LANES))
    rest = HID - HSIZE - CLASSES - 8
    last = jnp.concatenate([g_bias_two, g_bias_out, loss, jnp.zeros((rest, LANES), f32)], axis=0)
    columns = columns + jnp.where(lane_wide == 4, last, 0.0)
    out_ref[ROW_MISC : ROW_MISC + 16, :] = parted(columns.T[0:8]).astype(bf16)
    out_ref[ROW_MISC + 16 :, :] = jnp.zeros((ROWS - ROW_MISC - 16, HID), bf16)
    core = jnp.bitwise_and(dom_ref[0], 1)
    width = ROWS // 2
    keep_ref[...] = out_ref[pl.ds(pl.multiple_of(core * width, width), width), :]
    send_out_ref[...] = out_ref[pl.ds(pl.multiple_of((1 - core) * width, width), width), :]


def run_model(
    section_id, dom_id, spot, features, src_all, labels, label_mask, send_index, pieces, shards, small_params
):
    nodes = features.shape[1]
    blocks = nodes // LANES
    scratch = [
        pltpu.VMEM((blocks, LANES, DEG * LANES), bf16),
        pltpu.VMEM((2, blocks, HID, SLOTS * LANES), bf16),
        pltpu.VMEM((2, blocks, 8, SLOTS * LANES), f32),
        pltpu.VMEM((2, blocks, HEADS, LANES, LANES), bf16),
        pltpu.VMEM((2, HID, nodes), bf16),
        pltpu.VMEM((2, HID, nodes), f32),
        pltpu.VMEM((3, 2 * HID, nodes), bf16),
        pltpu.VMEM((HID, nodes), bf16),
        pltpu.VMEM((HSIZE, nodes), bf16),
        pltpu.VMEM((CLASSES, nodes), bf16),
        pltpu.VMEM((WAYS, HID, SLOTS * LANES), bf16),
        pltpu.VMEM((WAYS, HEADS * 16, SLOTS * LANES), bf16),
        pltpu.VMEM((2, HID, LANES), f32),
        pltpu.VMEM((2, HID, LANES), f32),
        pltpu.VMEM((HID, LANES), f32),
        pltpu.VMEM((1, 4 * LANES), f32),
        pltpu.VMEM((nodes, FEAT), bf16),
        pltpu.VMEM((DEG, nodes), jnp.int32),
        pltpu.VMEM((8, nodes), jnp.int32),
        pltpu.VMEM((FEAT, HID), bf16),
        pltpu.VMEM((2, 2 * HID, HID), bf16),
        pltpu.VMEM((2, HID, 2 * HID), bf16),
        pltpu.VMEM((HSIZE, CLASSES), bf16),
        pltpu.VMEM((HSIZE, LANES), f32),
        pltpu.VMEM((2, 16, HID), bf16),
        pltpu.VMEM((ROWS, HID), bf16),
        pltpu.VMEM((LANES, DEG * LANES), bf16),
        pltpu.VMEM((GROUPS, 32, HID), bf16),
    ]
    def body(*refs):
        ahead, cut = (8, 8 + len(pieces))
        after = cut + len(shards)
        head = refs[:ahead] + (refs[ahead:cut], refs[cut:after]) + refs[after:]
        pl.run_scoped(lambda *buffers: model_kernel(*head, *buffers), *scratch)

    grid_spec = pltpu.PrefetchScalarGridSpec(
        num_scalar_prefetch=3,
        grid=(1,),
        in_specs=[
            pl.BlockSpec((1, nodes, FEAT), lambda i, m, d, p: (m[0], 0, 0)),
            pl.BlockSpec((1, DEG, nodes), lambda i, m, d, p: (m[0], 0, 0)),
        ]
        + vmem(4 + len(pieces) + len(shards)),
        out_specs=vmem(2),
    )
    return pl.pallas_call(
        body,
        grid_spec=grid_spec,
        out_shape=[jax.ShapeDtypeStruct((ROWS // 2, HID), bf16)] * 2,
        compiler_params=pltpu.CompilerParams(vmem_limit_bytes=50 * 1024 * 1024),
        name="model",
    )(section_id, dom_id, spot, features, src_all, labels, label_mask, send_index, *pieces, *shards, small_params)


def settled(total, is_last):
    base = ROW_MISC % PIECE
    block = total[base : base + 16]
    block = jnp.where(is_last == 1, parted(block[0:8] + block[8:16]), block)
    return jnp.concatenate([total[:base], block, total[base + 16 :]], axis=0).astype(bf16)


def last_piece(core, section):
    return jnp.where((core == 1) & (section == 3), 1, 0)


def split_kernel(section_ref, dom_ref, keep_ref, got_ref, *out_refs):
    section = section_ref[0]
    core = jnp.bitwise_and(dom_ref[0], 1)
    for j, out_ref in enumerate(out_refs):
        part = jnp.bitwise_xor(section, j)
        at = pl.ds(pl.multiple_of(part * PIECE, PIECE), PIECE)
        total = keep_ref[at, :].astype(f32) + got_ref[at, :].astype(f32)
        out_ref[...] = settled(total, last_piece(core, part))


def join_kernel(section_ref, dom_ref, own_ref, one_ref, two_ref, three_ref, out_ref):
    pair = own_ref[...].astype(f32) + one_ref[...].astype(f32)
    other = two_ref[...].astype(f32) + three_ref[...].astype(f32)
    core = jnp.bitwise_and(dom_ref[0], 1)
    out_ref[...] = settled(pair + other, last_piece(core, section_ref[0]))


def small_call(kernel, name, ids, count, operands):
    shape = jax.ShapeDtypeStruct((PIECE, HID), bf16)
    return pl.pallas_call(
        kernel,
        out_shape=[shape] * count if count > 1 else shape,
        in_specs=[pl.BlockSpec(memory_space=pltpu.SMEM)] * 2 + vmem(len(operands)),
        out_specs=vmem(count) if count > 1 else vmem(1)[0],
        compiler_params=pltpu.CompilerParams(vmem_limit_bytes=8 * 1024 * 1024),
        name=name,
    )(*ids, *operands)


def sum_gradients(ids, keep, send):
    if lax.axis_size("dom") == 8 and lax.axis_size("section") == 4:
        got = crossed(send, "dom", 1)
        parts = small_call(split_kernel, "split", ids, 4, (keep, got))
        came = [crossed(parts[j], "section", j) for j in range(1, 4)]
        mine = small_call(join_kernel, "join", ids, 1, (parts[0], *came))
        came = [crossed(mine, "dom", 2 * j) for j in range(1, 4)]
        mine = small_call(join_kernel, "join", ids, 1, (mine, *came))
        near = [mine] + [crossed(mine, "section", j) for j in range(1, 4)]
        return near + [crossed(piece, "dom", 1) for piece in near], ids
    all_size = lax.axis_size("dom") * lax.axis_size("section")
    swap = jnp.bitwise_and(ids[1][0], 1) == 1
    partial = jnp.concatenate([jnp.where(swap, send, keep), jnp.where(swap, keep, send)], axis=0)
    parts = lax.all_to_all(partial.reshape(all_size, -1, HID), ("section", "dom"), 0, 0)
    mine = jnp.sum(parts.astype(f32), axis=0)
    shared = jnp.broadcast_to(mine.astype(bf16)[None], (all_size,) + mine.shape)
    summed = lax.all_to_all(shared, ("section", "dom"), 0, 0).reshape(8, PIECE, HID)
    return [summed[j] for j in range(8)], (ids[0] * 0, ids[1] * 0)


def adamw_step(parameter, gradient, moment_one, moment_two):
    moment_one = beta_one * moment_one + (1.0 - beta_one) * gradient
    moment_two = beta_two * moment_two + (1.0 - beta_two) * gradient * gradient
    corr_one = 1.0 - beta_one**STEPS
    corr_two = 1.0 - beta_two**STEPS
    update = moment_one / corr_one / (jnp.sqrt(moment_two / corr_two) + adam_eps)
    return (parameter - adam_rate * (update + adam_decay * parameter), moment_one, moment_two)


def average(old_value, new_value):
    return ema_keep * old_value + (1.0 - ema_keep) * new_value


def dot_tn(a, b):
    return lax.dot_general(a, b, (((0,), (0,)), ((), ())), preferred_element_type=f32)


def halves(value):
    high = value.astype(bf16)
    return high, (value - high.astype(f32)).astype(bf16)


def wide_rows(total):
    return max(total, 16)


def own_rows(gradient, start, count):
    total = gradient.shape[0]
    row = lax.broadcasted_iota(jnp.int32, (wide_rows(count), total), 0) + start
    lane = lax.broadcasted_iota(jnp.int32, (wide_rows(count), total), 1)
    pick = jnp.where(row == lane, 1.0, 0.0).astype(bf16)
    return dot_nn(pick, gradient).astype(bf16)


def precondition(gradient, weight, stat_l, stat_r, root_l, root_r, ema, outs, scale, start):
    (new_w, new_l, new_r, new_ema) = outs
    count = weight.shape[0]
    square = (1.0 - shampoo_decay) * scale * scale
    mine = own_rows(gradient, start, count)
    new_l[...] = shampoo_decay * stat_l + square * dot_nt(mine, gradient)[0:count]
    new_r[...] = shampoo_decay * stat_r + square * dot_tn(gradient, gradient)
    high, low = halves(root_l)
    middle = dot_nn(high, gradient) + dot_nn(low, gradient)
    m_high, m_low = halves(middle * scale)
    r_high, r_low = halves(root_r)
    update = dot_nn(m_high, r_high) + dot_nn(m_low, r_high) + dot_nn(m_high, r_low)
    weight = weight - shampoo_rate * (update + weight_decay * weight)
    new_w[...] = weight
    new_ema[...] = average(ema, weight)


def update_kernel(
    dom_ref,
    section_ref,
    spot_ref,
    piece_0,
    piece_1,
    piece_2,
    piece_3,
    piece_4,
    piece_5,
    piece_6,
    piece_7,
    w_in,
    w_gat,
    w_out,
    small,
    l_in,
    r_in,
    l_gat,
    r_gat,
    l_out,
    r_out,
    rl_in,
    rr_in,
    rl_gat,
    rr_gat,
    rl_out,
    rr_out,
    first,
    second,
    e_in,
    e_gat,
    e_out,
    e_small,
    n_w_in,
    n_w_gat,
    n_w_out,
    n_small,
    n_l_in,
    n_r_in,
    n_l_gat,
    n_r_gat,
    n_l_out,
    n_r_out,
    n_first,
    n_second,
    n_e_in,
    n_e_gat,
    n_e_out,
    n_e_small,
    loss_ref,
    norm_ref,
    sum_ref,
):
    dom = dom_ref[0]
    core = jnp.bitwise_and(spot_ref[0], 1)
    pieces = (piece_0, piece_1, piece_2, piece_3, piece_4, piece_5, piece_6, piece_7)
    for j, piece in enumerate(pieces):
        spot = jnp.bitwise_xor(core, j >> 2) * 4 + jnp.bitwise_xor(section_ref[0], j & 3)
        sum_ref[pl.ds(pl.multiple_of(spot * PIECE, PIECE), PIECE), :] = piece[...]
    grads = sum_ref[0:ROW_MISC, :].astype(f32)
    squares = jnp.sum(grads * grads)
    misc = sum_ref[ROW_MISC : ROW_MISC + 16, :].astype(f32)
    misc = misc[0:8] + misc[8:16]
    row = lax.broadcasted_iota(jnp.int32, (8, HID), 0)
    lane = lax.broadcasted_iota(jnp.int32, (8, HID), 1)
    spot = HSIZE + CLASSES
    loss_ref[0] = jnp.sum(jnp.where((row == 4) & (lane == spot), misc, 0.0))
    small_part = jnp.where((row < 4) | ((row == 4) & (lane < spot)), misc, 0.0)
    squares = squares + jnp.sum(small_part * small_part)
    norm = jnp.sqrt(jnp.broadcast_to(squares, (1, 1)))
    scale = jnp.minimum(1.0, clip_norm / norm)
    norm_ref[0] = jnp.sum(norm)
    for layer in range(2):
        for side in range(2):
            at = (layer, side)
            begin = (2 * layer + side) * HID
            precondition(
                sum_ref[begin : begin + HID, :],
                w_gat[at],
                l_gat[at],
                r_gat[at],
                rl_gat[at],
                rr_gat[at],
                e_gat[at],
                (n_w_gat.at[at], n_l_gat.at[at], n_r_gat.at[at], n_e_gat.at[at]),
                scale,
                dom * w_gat.shape[2],
            )
    precondition(
        sum_ref[ROW_IN:ROW_OUT, :],
        w_in[...],
        l_in[...],
        r_in[...],
        rl_in[...],
        rr_in[...],
        e_in[...],
        (n_w_in, n_l_in, n_r_in, n_e_in),
        scale,
        dom * w_in.shape[0],
    )
    precondition(
        sum_ref[ROW_OUT:ROW_MISC, 0:CLASSES],
        w_out[...],
        l_out[...],
        r_out[...],
        rl_out[...],
        rr_out[...],
        e_out[...],
        (n_w_out, n_l_out, n_r_out, n_e_out),
        scale,
        dom * w_out.shape[0],
    )
    for place in range(5):
        width = HID if place < 4 else spot
        at = pl.ds(place * HID, width)
        gradient = misc[place : place + 1, 0:width] * scale

        def line(ref):
            return ref[at].reshape(1, width)

        new_value, moment_one, moment_two = adamw_step(line(small), gradient, line(first), line(second))
        n_small[at] = new_value.reshape(width)
        n_first[at] = moment_one.reshape(width)
        n_second[at] = moment_two.reshape(width)
        n_e_small[at] = average(line(e_small), new_value).reshape(width)


def per_device(
    features,
    sources,
    send_index,
    labels,
    label_mask,
    w_in,
    w_gat,
    w_out,
    small_params,
    stat_l_in,
    stat_r_in,
    stat_l_gat,
    stat_r_gat,
    stat_l_out,
    stat_r_out,
    root_l_in,
    root_r_in,
    root_l_gat,
    root_r_gat,
    root_l_out,
    root_r_out,
    adam_first,
    adam_second,
    ema_in,
    ema_gat,
    ema_out,
    ema_small,
):
    dom_id = lax.axis_index("dom").astype(jnp.int32).reshape(1)
    section_id = lax.axis_index("section").astype(jnp.int32).reshape(1)
    size = lax.axis_size("dom")
    src_all = jnp.swapaxes(sources, 1, 2)
    packed = pack_inputs(section_id, features, src_all, labels, label_mask, send_index, w_in, w_gat, w_out)
    pieces, spot = gather_weights(dom_id, packed, w_in, w_gat, w_out, label_mask)
    shards = ()
    if size == GROUPS:
        (pieces, shards) = (pieces[1:], (w_in, w_gat, w_out))
    keep, send = run_model(
        section_id,
        dom_id,
        spot,
        features,
        src_all,
        labels,
        label_mask,
        send_index,
        pieces,
        shards,
        small_params,
    )
    pieces, spots = sum_gradients((section_id, dom_id), keep, send)
    state = (
        w_in,
        w_gat,
        w_out,
        small_params,
        stat_l_in,
        stat_r_in,
        stat_l_gat,
        stat_r_gat,
        stat_l_out,
        stat_r_out,
        root_l_in,
        root_r_in,
        root_l_gat,
        root_r_gat,
        root_l_out,
        root_r_out,
        adam_first,
        adam_second,
        ema_in,
        ema_gat,
        ema_out,
        ema_small,
    )
    like = state[:10] + (adam_first, adam_second, ema_in, ema_gat, ema_out, ema_small)
    results = pl.pallas_call(
        update_kernel,
        out_shape=[jax.ShapeDtypeStruct(v.shape, f32) for v in like] + [jax.ShapeDtypeStruct((1,), f32)] * 2,
        in_specs=[pl.BlockSpec(memory_space=pltpu.SMEM)] * 3 + vmem(30),
        out_specs=vmem(16) + [pl.BlockSpec(memory_space=pltpu.SMEM)] * 2,
        scratch_shapes=[pltpu.VMEM((ROWS, HID), bf16)],
        compiler_params=pltpu.CompilerParams(vmem_limit_bytes=16 * 1024 * 1024),
        name="update",
    )(dom_id, *spots, *pieces, *state)
    return tuple(results[:16]) + (results[16].reshape(()), results[17].reshape(()))


def solution(mesh):
    placed = (
        P(None, "dom", None),
        P(None, "dom", None),
        P(None, "dom"),
        P(None, "dom"),
        P(None, "dom"),
        P("dom", None),
        P(None, None, "dom", None),
        P("dom", None),
        P(),
        P("dom", None),
        P(),
        P(None, None, "dom", None),
        P(),
        P("dom", None),
        P(),
        P("dom", None),
        P(),
        P(None, None, "dom", None),
        P(),
        P("dom", None),
        P(),
        P(),
        P(),
        P("dom", None),
        P(None, None, "dom", None),
        P("dom", None),
        P(),
    )
    return jax.shard_map(
        per_device,
        mesh=mesh,
        in_specs=placed,
        out_specs=(
            P("dom", None),
            P(None, None, "dom", None),
            P("dom", None),
            P(),
            P("dom", None),
            P(),
            P(None, None, "dom", None),
            P(),
            P("dom", None),
            P(),
            P(),
            P(),
            P("dom", None),
            P(None, None, "dom", None),
            P("dom", None),
            P(),
            P(),
            P(),
        ),
        check_vma=False,
    )
```

```python
import jax
import jax.numpy as jnp
from jax import lax
from jax.experimental import pallas as pl
from jax.experimental.pallas import tpu as pltpu
from jax.sharding import PartitionSpec as P

FEAT = 128
HEADS = 4
HSIZE = 64
CLASSES = 40
STEPS = 5
HID = 256
SMALL = 1128


highest = lax.Precision.HIGHEST
leak_slope = 0.2
smooth = 0.1
clip_norm = 0.001
shampoo_rate = 0.3
shampoo_decay = 0.5
weight_decay = 0.0001
adam_rate = 0.1
beta_one = 0.9
beta_two = 0.999
adam_eps = 1e-08
adam_decay = 0.01
ema_keep = 0.9


def split_small(small_params):
    bias_in = small_params[0:HID]
    attention = small_params[HID : 3 * HID].reshape(2, HEADS, HSIZE)
    bias_one = small_params[3 * HID : 4 * HID]
    bias_two = small_params[4 * HID : 4 * HID + HSIZE]
    bias_out = small_params[4 * HID + HSIZE :]
    return (bias_in, attention, bias_one, bias_two, bias_out)


GRAPH = 64
LANES = 128
DEG = 8
SLOTS = DEG + 1
WAYS = 4
ROWS = 1280
GROUPS = 8
IN_G = FEAT // GROUPS
GAT_G = HID // GROUPS
OUT_G = HSIZE // GROUPS
TAIL_G = IN_G + 4 * GAT_G
PACK_G = TAIL_G + 2 * OUT_G
HALO_G = PACK_G + 16
CODES = slice(HID - LANES, HID)
PIECE = ROWS // 8
HALF = GRAPH // 2
ROW_IN = 4 * HID
ROW_OUT = ROW_IN + FEAT
ROW_MISC = ROW_OUT + HSIZE

bf16 = jnp.bfloat16
f32 = jnp.float32


def dot_nn(a, b):
    return lax.dot_general(a, b, (((1,), (0,)), ((), ())), preferred_element_type=f32)


def dot_nt(a, b):
    return lax.dot_general(a, b, (((1,), (1,)), ((), ())), preferred_element_type=f32)


def tile_of(k):
    return slice(k * LANES, (k + 1) * LANES)


def head_of(h):
    return slice(h * HSIZE, (h + 1) * HSIZE)


def row_of(ref, micro, width):
    picked = ref[0:1, 0:width]
    for other in range(1, ref.shape[0]):
        picked = jnp.where(micro == other, ref[other : other + 1, 0:width], picked)
    return picked


def pack_kernel(
    section_ref,
    feat_ref,
    src_ref,
    lab_ref,
    msk_ref,
    send_ref,
    win_ref,
    wgat_ref,
    wout_ref,
    pack_ref,
    tail_ref,
):
    micro = section_ref[0]
    nodes = lab_ref.shape[1]
    pack_ref[PACK_G:HALO_G, 0:FEAT] = feat_ref[0, 0:16]
    pack_ref[PACK_G:HALO_G, FEAT : 2 * FEAT] = feat_ref[0, 16:32]
    shift = LANES - HALF
    tail_ref[...] = jnp.zeros_like(tail_ref)
    far = src_ref[0]
    far = jnp.where(far >= nodes, far - nodes + GRAPH, far)
    tail_ref[0:DEG, CODES] = pltpu.roll(far, shift, 1).astype(f32)
    tail_ref[DEG : DEG + 1, CODES] = pltpu.roll(row_of(lab_ref, micro, LANES), shift, 1).astype(f32)
    tail_ref[DEG + 1 : DEG + 2, CODES] = pltpu.roll(row_of(msk_ref, micro, LANES), shift, 1).astype(f32)
    send = row_of(send_ref, micro, 2 * HALF)
    tail_ref[DEG + 2 : DEG + 3, CODES] = jnp.concatenate([send, send], axis=1).astype(f32)
    if win_ref.shape[0] != IN_G:
        pack_ref[0:TAIL_G, :] = jnp.zeros((TAIL_G, HID), bf16)
        pack_ref[TAIL_G:PACK_G, :] = tail_ref[...].astype(bf16)
        return
    pack_ref[0:IN_G, :] = win_ref[...].astype(bf16)
    for layer in range(2):
        for side in range(2):
            start = IN_G + (2 * layer + side) * GAT_G
            pack_ref[start : start + GAT_G, :] = wgat_ref[layer, side].astype(bf16)
    tail_ref[0:OUT_G, 0:CLASSES] = wout_ref[...]
    count = jnp.sum(jnp.sum(msk_ref[...].astype(f32), axis=1, keepdims=True), axis=0, keepdims=True)
    high = jnp.floor(count * (1.0 / 256.0))
    lane = lax.broadcasted_iota(jnp.int32, (1, LANES), 1)
    low = jnp.where(lane == 1, count - 256.0 * high, 0.0)
    tail_ref[OUT_G : OUT_G + 1, 0:LANES] = jnp.where(lane == 0, high, low)
    pack_ref[TAIL_G:PACK_G, :] = tail_ref[...].astype(bf16)


def vmem(count):
    return [pl.BlockSpec(memory_space=pltpu.VMEM)] * count


def pack_inputs(section_id, features, src_all, labels, label_mask, send_index, w_in, w_gat, w_out):
    grid_spec = pltpu.PrefetchScalarGridSpec(
        num_scalar_prefetch=1,
        grid=(1,),
        in_specs=[
            pl.BlockSpec((1, HALF, FEAT), lambda i, m: (m[0], 0, 0)),
            pl.BlockSpec((1, DEG, LANES), lambda i, m: (m[0], 0, 0)),
        ]
        + vmem(6),
        out_specs=vmem(1)[0],
        scratch_shapes=[pltpu.VMEM((2 * OUT_G, HID), f32)],
    )
    return pl.pallas_call(
        pack_kernel,
        grid_spec=grid_spec,
        out_shape=jax.ShapeDtypeStruct((HALO_G, HID), bf16),
        compiler_params=pltpu.CompilerParams(vmem_limit_bytes=58 * 1024 * 1024),
        name="pack",
    )(section_id, features, src_all, labels, label_mask, send_index, w_in, w_gat, w_out)


def crossed(value, axis, mask):
    return lax.ppermute(value, axis, [(i, i ^ mask) for i in range(lax.axis_size(axis))])


def gather_weights(dom_id, packed, w_in, w_gat, w_out, label_mask):
    size = lax.axis_size("dom")
    if size == GROUPS:
        near = [packed] + [crossed(packed, "dom", 2 * j) for j in range(1, 4)]
        return near + [crossed(piece, "dom", 1) for piece in near], dom_id
    halo = lax.ppermute(packed[TAIL_G:], "dom", [((i + 1) % size, i) for i in range(size)])
    halo = jnp.broadcast_to(halo[None], (GROUPS,) + halo.shape)
    rows_in, rows_gat, rows_out = (w_in.shape[0], w_gat.shape[2], w_out.shape[0])
    count = jnp.sum(label_mask)
    digits = jnp.stack([lax.div(count, 256), lax.rem(count, 256)]).astype(bf16)
    packed = jnp.concatenate(
        [
            w_in.astype(bf16),
            w_gat.astype(bf16).reshape(4 * rows_gat, HID),
            jnp.pad(w_out.astype(bf16), ((0, 0), (0, HID - CLASSES))),
            jnp.pad(digits[None, :], ((0, 0), (0, HID - 2))),
        ],
        axis=0,
    )
    whole = lax.all_gather(packed, "dom", axis=0, tiled=False)
    cut = rows_in + 4 * rows_gat
    part_in = whole[:, :rows_in].reshape(GROUPS, IN_G, HID)
    part_gat = whole[:, rows_in:cut].reshape(GROUPS, size // GROUPS, 4, rows_gat, HID)
    part_gat = part_gat.transpose(0, 2, 1, 3, 4).reshape(GROUPS, 4 * GAT_G, HID)
    part_out = whole[:, cut : cut + rows_out].reshape(GROUPS, OUT_G, HID)
    counts = whole[:, cut + rows_out].reshape(GROUPS, size // GROUPS, HID)
    counts = jnp.pad(counts, ((0, 0), (0, OUT_G - size // GROUPS), (0, 0)))
    tail = jnp.concatenate([part_out, counts], axis=1)
    tail = jnp.concatenate([tail[:, :, :LANES], halo[:, : 2 * OUT_G, LANES:]], axis=2)
    whole = jnp.concatenate([part_in, part_gat, tail, halo[:, 2 * OUT_G :]], axis=1)
    return [whole[g] for g in (0, 2, 4, 6, 1, 3, 5, 7)], dom_id * 0


def parted(rows):
    high = rows.astype(bf16).astype(f32)
    return jnp.concatenate([high, rows - high], axis=0)


def column_of(row):
    return jnp.broadcast_to(row.reshape(1, -1), (LANES, row.shape[0])).T


def model_kernel(
    section_ref,
    dom_ref,
    spot_ref,
    feat_ref,
    src_ref,
    lab_ref,
    msk_ref,
    send_ref,
    piece_refs,
    shard_refs,
    small_ref,
    keep_ref,
    send_out_ref,
    e_ref,
    t_ref,
    al_ref,
    att_ref,
    h_ref,
    slope_ref,
    both_ref,
    do_ref,
    pool_ref,
    dlog_ref,
    w_ref,
    sum_ref,
    a_ref,
    da_ref,
    gb_ref,
    loss_ref,
    node_ref,
    edge_ref,
    mark_ref,
    wi_ref,
    wgt_ref,
    wg_ref,
    wo_ref,
    wof_ref,
    am_ref,
    out_ref,
    eye_ref,
    halo_ref,
):
    nodes = feat_ref.shape[1]
    blocks = nodes // LANES
    chunk = 4 * LANES
    chunks = nodes // chunk
    mixed = DEG * LANES
    micro = section_ref[0]
    after = jnp.bitwise_and(spot_ref[0] + 1, GROUPS - 1)
    final = nodes - LANES

    digits = jnp.zeros((OUT_G, LANES), f32)
    own_count = jnp.zeros((1, 1), f32)
    first = GROUPS - len(piece_refs)
    if first == 1:
        (win_ref, wgat_ref, wout_ref) = shard_refs
        group = spot_ref[0]
        at_in = pl.ds(pl.multiple_of(group * IN_G, IN_G), IN_G)
        at_gat = pl.ds(pl.multiple_of(group * GAT_G, GAT_G), GAT_G)
        at_out = pl.ds(pl.multiple_of(group * OUT_G, OUT_G), OUT_G)
        wi_ref[at_in, :] = win_ref[...].astype(bf16)
        for layer in range(2):
            for side in range(2):
                wg_ref[layer, at_gat, side * HID : (side + 1) * HID] = wgat_ref[layer, side].astype(bf16)
        wof_ref[at_out, :] = jnp.zeros((OUT_G, LANES), f32)
        wof_ref[at_out, 0:CLASSES] = wout_ref[...]
        marked = jnp.sum(msk_ref[...].astype(f32), axis=1, keepdims=True)
        own_count = jnp.sum(marked, axis=0, keepdims=True)
    for j, piece in enumerate(piece_refs, first):
        group = jnp.bitwise_xor(spot_ref[0], 2 * (j & 3) + (j >> 2))

        def rows_of(width):
            return pl.ds(pl.multiple_of(group * width, width), width)

        wi_ref[rows_of(IN_G), :] = piece[0:IN_G, :]
        for layer in range(2):
            for side in range(2):
                start = IN_G + (2 * layer + side) * GAT_G
                wg_ref[layer, rows_of(GAT_G), side * HID : (side + 1) * HID] = piece[start : start + GAT_G, :]
        tail = piece[TAIL_G:PACK_G, :].astype(f32)
        wof_ref[rows_of(OUT_G), :] = tail[0:OUT_G, 0:LANES]
        digits = digits + tail[OUT_G : 2 * OUT_G, 0:LANES]
        halo_ref[group] = piece[TAIL_G:HALO_G, :]

    node_ref[0 : nodes - HALF, :] = feat_ref[0, HALF:nodes, :]
    node_ref[nodes - HALF : nodes - 16, :] = halo_ref[after, 16:32, 0:FEAT]
    node_ref[nodes - 16 : nodes, :] = halo_ref[after, 16:32, FEAT : 2 * FEAT]
    ints = halo_ref[after, 0:16, CODES].astype(f32).astype(jnp.int32)
    lane_row = lax.broadcasted_iota(jnp.int32, (1, LANES), 1)
    kept = lane_row < LANES - HALF
    edge_ref[...] = pltpu.roll(src_ref[0], nodes - HALF, 1)
    edge_ref[:, final:nodes] = jnp.where(
        kept,
        edge_ref[:, final:nodes],
        jnp.where(ints[0:DEG] >= GRAPH, ints[0:DEG] + (nodes - GRAPH), ints[0:DEG]),
    )
    for place, ref in enumerate((lab_ref, msk_ref)):
        mark_ref[place : place + 1, :] = pltpu.roll(row_of(ref, micro, nodes), nodes - HALF, 1)
        came = ints[DEG + place : DEG + place + 1]
        mark_ref[place : place + 1, final:nodes] = jnp.where(kept, mark_ref[place : place + 1, final:nodes], came)
    send = row_of(send_ref, micro, 2 * HALF)
    send = jnp.concatenate([send, send], axis=1)
    arrived = pltpu.roll(ints[DEG + 2 : DEG + 3], HALF, 1)
    table = jnp.where(
        lane_row < HALF, pltpu.roll(send, HALF, 1) - (nodes - HALF), arrived + HALF
    )
    spot_row = lax.broadcasted_iota(jnp.int32, (GRAPH, LANES), 0)
    spot_lane = lax.broadcasted_iota(jnp.int32, (GRAPH, LANES), 1)
    table = jnp.sum(jnp.where(spot_row == spot_lane, table.astype(f32), 0.0), axis=1, keepdims=True)
    looked = []
    for k in range(DEG):
        far = edge_ref[k : k + 1, final:nodes] - nodes == spot_row
        looked.append(jnp.sum(jnp.where(far, table, 0.0), axis=0, keepdims=True))
    looked = jnp.concatenate(looked, axis=0).astype(jnp.int32)
    raw = edge_ref[:, final:nodes]
    looked = jnp.where(raw >= nodes, looked, jnp.bitwise_and(raw - HALF, GRAPH - 1))
    local = jnp.bitwise_and(edge_ref[...] - HALF, GRAPH - 1)
    lane_all = lax.broadcasted_iota(jnp.int32, (DEG, nodes), 1)
    second = jnp.bitwise_and(lane_all, GRAPH)
    edge_ref[...] = local + second
    edge_ref[:, final:nodes] = looked + jnp.bitwise_and(
        lax.broadcasted_iota(jnp.int32, (DEG, LANES), 1), GRAPH
    )

    for layer in range(2):
        for side in range(2):
            wgt_ref[layer, side * HID : (side + 1) * HID, :] = wg_ref[
                layer, :, side * HID : (side + 1) * HID
            ].T
    wi_t = wi_ref[...].T
    wo_ref[...] = wof_ref[:, 0:CLASSES].astype(bf16)
    wo_t = wof_ref[...].T[0:CLASSES].astype(bf16)
    digits = jnp.sum(digits, axis=0, keepdims=True)
    inv_count = 1.0 / (digits[:, 0:1] * 256.0 + digits[:, 1:2] + own_count)

    row_id = lax.broadcasted_iota(jnp.int32, (LANES, LANES), 0)
    lane_id = lax.broadcasted_iota(jnp.int32, (LANES, LANES), 1)
    eye = jnp.where(row_id == lane_id, 1.0, 0.0).astype(bf16)
    head_row = lax.broadcasted_iota(jnp.int32, (16, HID), 0)
    head_col = lax.broadcasted_iota(jnp.int32, (16, HID), 1)
    head_mask = jnp.where(head_col // HSIZE == head_row, 1.0, 0.0)

    bias_in = column_of(small_ref[0:HID])[:, 0:1]
    bias_one = column_of(small_ref[3 * HID : 4 * HID])[:, 0:1]
    bias_two = column_of(small_ref[4 * HID : 4 * HID + HSIZE])[:, 0:1]
    bias_out = column_of(small_ref[4 * HID + HSIZE : SMALL])[:, 0:1]
    for layer in range(2):
        row = small_ref[(1 + layer) * HID : (2 + layer) * HID]
        a_ref[layer] = column_of(row)
        row = row.reshape(1, HID)
        high = row.astype(bf16).astype(f32)
        am_ref[layer] = jnp.concatenate([head_mask[0:8] * high, head_mask[0:8] * (row - high)], axis=0).astype(bf16)
    fold_row = lax.broadcasted_iota(jnp.int32, (16, HEADS * 16), 0)
    fold_col = lax.broadcasted_iota(jnp.int32, (16, HEADS * 16), 1)
    fold = jnp.where(fold_col // 16 == fold_row, 1.0, 0.0).astype(bf16)
    spots = lax.broadcasted_iota(jnp.int32, (GRAPH, LANES), 0).astype(f32).astype(bf16)
    spots = spots.reshape(4, 16, LANES)
    half_lane = lax.broadcasted_iota(jnp.int32, (16, LANES), 1)
    first_half = (half_lane < GRAPH).astype(f32).astype(bf16)[None] > 0
    own_spot = jnp.bitwise_and(half_lane, GRAPH - 1).astype(f32).astype(bf16)
    zero = jnp.zeros((4, 16, LANES), bf16)
    da_ref[...] = jnp.zeros_like(da_ref)
    gb_ref[...] = jnp.zeros_like(gb_ref)
    loss_ref[...] = jnp.zeros_like(loss_ref)

    def lanes_of(i, width):
        return pl.ds(pl.multiple_of(i * width, width), width)

    @pl.loop(0, chunks, unroll=4)
    def _(c):
        at = lanes_of(c, chunk)
        pre = dot_nt(wi_t, node_ref[at, :]) + bias_in
        grown = jnp.exp(jnp.minimum(pre, 0.0))
        h_ref[0, :, at] = (jnp.maximum(pre, 0.0) + (grown - 1.0)).astype(bf16)
        slope_ref[0, :, at] = grown

    wide_spots = lax.broadcasted_iota(jnp.int32, (LANES, LANES), 0).astype(f32).astype(bf16)
    wide_spots = wide_spots.reshape(8, 16, LANES)
    for k in range(DEG):
        eye_ref[:, tile_of(k)] = eye

    def one_hot(u_at):
        parts = []
        for k in range(DEG):
            spot = jnp.broadcast_to(edge_ref[k : k + 1, u_at].astype(f32), (16, LANES)).astype(bf16)
            hit = wide_spots == spot[None]
            hit = jnp.where(hit, jnp.ones((8, 16, LANES), bf16), jnp.zeros((8, 16, LANES), bf16))
            parts.append(hit.reshape(LANES, LANES))
        return parts

    for layer in range(2):

        @pl.loop(0, chunks, unroll=4)
        def _(c):
            at = lanes_of(c, chunk)
            both_ref[layer, :, at] = dot_nn(wgt_ref[layer], h_ref[layer, :, at]).astype(bf16)

        @pl.loop(0, blocks // WAYS)
        def _(step):
            ids = [step * WAYS + u for u in range(WAYS)]
            ats = [lanes_of(i, LANES) for i in ids]
            ways = range(WAYS)
            left = [both_ref[layer, 0:HID, ats[u]] for u in ways]
            grown = []
            for u in ways:
                right = both_ref[layer, HID : 2 * HID, ats[u]]
                left_f = left[u].astype(f32)
                if layer == 0:
                    parts = one_hot(ats[u])
                    for k in range(DEG):
                        e_ref[ids[u], :, tile_of(k)] = parts[k]
                    hot = jnp.concatenate(parts[0:2], axis=1)
                else:
                    hot = e_ref[ids[u], :, 0 : 2 * LANES]
                mixed_rows = [dot_nn(left[u], hot).astype(bf16)]
                for k in range(2, DEG):
                    index = jnp.broadcast_to(edge_ref[k : k + 1, ats[u]], (HID, LANES))
                    picked = jnp.take_along_axis(left_f, index, axis=1, mode="promise_in_bounds")
                    mixed_rows.append(picked.astype(bf16))
                mixed_rows = jnp.concatenate(mixed_rows, axis=1)
                mixed_rows = mixed_rows + jnp.concatenate([right] * DEG, axis=1)
                own = left[u] + right
                t_ref[layer, ids[u], :, 0:mixed] = mixed_rows
                t_ref[layer, ids[u], :, tile_of(DEG)] = own
                t = jnp.concatenate([mixed_rows, own], axis=1)
                z = jnp.maximum(t, t * leak_slope)
                scores = dot_nn(am_ref[layer], z)
                grown.append(jnp.exp(scores[0:8] + scores[8:16]))
            grids_all = []
            for u in ways:
                total = grown[u][:, tile_of(0)]
                for k in range(1, SLOTS):
                    total = total + grown[u][:, tile_of(k)]
                inverse = 1.0 / total
                grids = [None] * HEADS
                for k in range(SLOTS):
                    alpha = grown[u][:, tile_of(k)] * inverse
                    al_ref[layer, ids[u], :, tile_of(k)] = alpha
                    if k == DEG:
                        spot = own_spot
                    else:
                        spot = jnp.bitwise_and(edge_ref[k : k + 1, ats[u]], GRAPH - 1).astype(f32)
                        spot = jnp.broadcast_to(spot, (16, LANES)).astype(bf16)
                    hit = spots == spot[None]
                    for h in range(HEADS):
                        part = jnp.broadcast_to(alpha[h : h + 1], (16, LANES)).astype(bf16)
                        part = jnp.where(hit, part[None], zero)
                        grids[h] = part if k == 0 else grids[h] + part
                grids_all.append(grids)
            for u in ways:
                pooled = None
                for h in range(HEADS):
                    upper = jnp.where(first_half, grids_all[u][h], zero).reshape(GRAPH, LANES)
                    lower = jnp.where(first_half, zero, grids_all[u][h]).reshape(GRAPH, LANES)
                    grid = jnp.concatenate([upper, lower], axis=0)
                    att_ref[layer, ids[u], h] = grid
                    total = dot_nn(left[u][head_of(h)], grid)
                    if layer == 0:
                        pre = total + bias_one[head_of(h)]
                        grown_one = jnp.exp(jnp.minimum(pre, 0.0))
                        h_ref[1, head_of(h), ats[u]] = (jnp.maximum(pre, 0.0) + (grown_one - 1.0)).astype(bf16)
                        slope_ref[1, head_of(h), ats[u]] = grown_one
                    else:
                        rounded = total.astype(bf16).astype(f32)
                        pooled = rounded if pooled is None else pooled + rounded
                if layer == 1:
                    pool_ref[:, ats[u]] = (pooled * (1.0 / HEADS) + bias_two).astype(bf16)

    @pl.loop(0, chunks, unroll=4)
    def _(c):
        at = lanes_of(c, chunk)
        logits = dot_nn(wo_t, pool_ref[:, at]) + bias_out
        shifted = logits - jnp.max(logits, axis=0, keepdims=True)
        log_prob = shifted - jnp.log(jnp.sum(jnp.exp(shifted), axis=0, keepdims=True))
        class_id = lax.broadcasted_iota(jnp.int32, (CLASSES, chunk), 0)
        onehot = jnp.where(class_id == mark_ref[0:1, at], 1.0, 0.0)
        share = mark_ref[1:2, at].astype(f32) * inv_count
        term = jnp.sum(((smooth - 1.0) * onehot - smooth / CLASSES) * log_prob, axis=0, keepdims=True)
        loss_ref[...] += term * share
        d_logits = (jnp.exp(log_prob) - (1.0 - smooth) * onehot - smooth / CLASSES) * share
        d_logits = d_logits.astype(bf16)
        dlog_ref[:, at] = d_logits
        d_pooled = (dot_nn(wo_ref[...], d_logits) * (1.0 / HEADS)).astype(bf16)
        for h in range(HEADS):
            do_ref[head_of(h), at] = d_pooled

    for layer in (1, 0):

        @pl.loop(0, blocks // WAYS)
        def _(step):
            ids = [step * WAYS + u for u in range(WAYS)]
            ats = [lanes_of(i, LANES) for i in ids]
            ways = range(WAYS)
            d_out = [do_ref[:, ats[u]] for u in ways]
            d_alpha = []
            for u in ways:
                for h in range(HEADS):
                    d_head = d_out[u][head_of(h)].reshape(4, 16, LANES)
                    for k in range(SLOTS):
                        t = t_ref[layer, ids[u], head_of(h), tile_of(k)].reshape(4, 16, LANES)
                        product = t * d_head
                        sum_ref[u, h * 16 : (h + 1) * 16, tile_of(k)] = (product[0] + product[1]) + (
                            product[2] + product[3]
                        )
                d_alpha.append(dot_nn(fold, sum_ref[u])[0:8])
            for u in ways:
                alpha = al_ref[layer, ids[u]]
                weighted = alpha * d_alpha[u]
                total = weighted[:, tile_of(0)]
                for k in range(1, SLOTS):
                    total = total + weighted[:, tile_of(k)]
                for k in range(SLOTS):
                    d_score = weighted[:, tile_of(k)] - alpha[:, tile_of(k)] * total
                    for h in range(HEADS):
                        one = jnp.broadcast_to(d_score[h : h + 1], (16, LANES))
                        two = (one * leak_slope).astype(bf16)[None]
                        one = one.astype(bf16)[None]
                        t = t_ref[layer, ids[u], head_of(h), tile_of(k)].reshape(4, 16, LANES)
                        w_ref[u, head_of(h), tile_of(k)] = jnp.where(t > 0, one, two).reshape(HSIZE, LANES)
            for u in ways:
                together = jnp.concatenate([e_ref[ids[u]], eye_ref[...]], axis=0)
                spread = dot_nt(w_ref[u, :, 0:mixed], together)
                own = w_ref[u, :, tile_of(DEG)].astype(f32)
                left_w = spread[:, 0:LANES] + own
                right_w = spread[:, LANES : 2 * LANES] + own
                left = both_ref[layer, 0:HID, ats[u]].astype(f32)
                right = both_ref[layer, HID : 2 * HID, ats[u]].astype(f32)
                da_ref[layer] += left * left_w + right * right_w
                wide = a_ref[layer]
                for h in range(HEADS):
                    passed = dot_nt(d_out[u][head_of(h)], att_ref[layer, ids[u], h])
                    d_left = wide[head_of(h)] * left_w[head_of(h)] + passed
                    both_ref[1 + layer, head_of(h), ats[u]] = d_left.astype(bf16)
                both_ref[1 + layer, HID : 2 * HID, ats[u]] = (wide * right_w).astype(bf16)

        @pl.loop(0, chunks, unroll=4)
        def _(c):
            at = lanes_of(c, chunk)
            d_in = dot_nn(wg_ref[layer], both_ref[1 + layer, :, at]).astype(bf16).astype(f32)
            d_in = d_in * slope_ref[layer, :, at]
            do_ref[:, at] = d_in.astype(bf16)
            if layer == 1:
                for k in range(4):
                    gb_ref[...] += d_in[:, tile_of(k)]

    for layer in range(2):
        for side in range(2):
            start = (2 * layer + side) * HID
            out_ref[start : start + HID, :] = dot_nt(
                h_ref[layer], both_ref[1 + layer, side * HID : (side + 1) * HID, :]
            ).astype(bf16)
    ones = jnp.ones((nodes, LANES), bf16)
    with_sums = dot_nn(do_ref[...], jnp.concatenate([node_ref[...], ones], axis=1))
    out_ref[ROW_IN : ROW_IN + FEAT, :] = with_sums[:, 0:FEAT].T.astype(bf16)
    out_ref[ROW_OUT : ROW_OUT + HSIZE, :] = jnp.zeros((HSIZE, HID), bf16)
    out_ref[ROW_OUT : ROW_OUT + HSIZE, 0:CLASSES] = dot_nt(pool_ref[...], dlog_ref[...]).astype(bf16)
    lane_wide = lax.broadcasted_iota(jnp.int32, (HID, LANES), 1)
    columns = jnp.where(lane_wide == 0, with_sums[:, FEAT:], 0.0)
    for layer in range(2):
        da = jnp.sum(da_ref[layer], axis=1, keepdims=True)
        columns = columns + jnp.where(lane_wide == 1 + layer, da, 0.0)
    columns = columns + jnp.where(lane_wide == 3, jnp.sum(gb_ref[...], axis=1, keepdims=True), 0.0)
    g_bias_out = dot_nn(dlog_ref[...], ones)
    g_bias_two = lax.dot_general(
        wo_ref[...].astype(f32), g_bias_out, (((1,), (0,)), ((), ())),
        precision=highest, preferred_element_type=f32,
    )
    loss = jnp.broadcast_to(jnp.sum(loss_ref[...], axis=1, keepdims=True), (8, LANES))
    rest = HID - HSIZE - CLASSES - 8
    last = jnp.concatenate([g_bias_two, g_bias_out, loss, jnp.zeros((rest, LANES), f32)], axis=0)
    columns = columns + jnp.where(lane_wide == 4, last, 0.0)
    out_ref[ROW_MISC : ROW_MISC + 16, :] = parted(columns.T[0:8]).astype(bf16)
    out_ref[ROW_MISC + 16 :, :] = jnp.zeros((ROWS - ROW_MISC - 16, HID), bf16)
    core = jnp.bitwise_and(dom_ref[0], 1)
    width = ROWS // 2
    keep_ref[...] = out_ref[pl.ds(pl.multiple_of(core * width, width), width), :]
    send_out_ref[...] = out_ref[pl.ds(pl.multiple_of((1 - core) * width, width), width), :]


def run_model(
    section_id, dom_id, spot, features, src_all, labels, label_mask, send_index, pieces, shards, small_params
):
    nodes = features.shape[1]
    blocks = nodes // LANES
    scratch = [
        pltpu.VMEM((blocks, LANES, DEG * LANES), bf16),
        pltpu.VMEM((2, blocks, HID, SLOTS * LANES), bf16),
        pltpu.VMEM((2, blocks, 8, SLOTS * LANES), f32),
        pltpu.VMEM((2, blocks, HEADS, LANES, LANES), bf16),
        pltpu.VMEM((2, HID, nodes), bf16),
        pltpu.VMEM((2, HID, nodes), f32),
        pltpu.VMEM((3, 2 * HID, nodes), bf16),
        pltpu.VMEM((HID, nodes), bf16),
        pltpu.VMEM((HSIZE, nodes), bf16),
        pltpu.VMEM((CLASSES, nodes), bf16),
        pltpu.VMEM((WAYS, HID, SLOTS * LANES), bf16),
        pltpu.VMEM((WAYS, HEADS * 16, SLOTS * LANES), bf16),
        pltpu.VMEM((2, HID, LANES), f32),
        pltpu.VMEM((2, HID, LANES), f32),
        pltpu.VMEM((HID, LANES), f32),
        pltpu.VMEM((1, 4 * LANES), f32),
        pltpu.VMEM((nodes, FEAT), bf16),
        pltpu.VMEM((DEG, nodes), jnp.int32),
        pltpu.VMEM((8, nodes), jnp.int32),
        pltpu.VMEM((FEAT, HID), bf16),
        pltpu.VMEM((2, 2 * HID, HID), bf16),
        pltpu.VMEM((2, HID, 2 * HID), bf16),
        pltpu.VMEM((HSIZE, CLASSES), bf16),
        pltpu.VMEM((HSIZE, LANES), f32),
        pltpu.VMEM((2, 16, HID), bf16),
        pltpu.VMEM((ROWS, HID), bf16),
        pltpu.VMEM((LANES, DEG * LANES), bf16),
        pltpu.VMEM((GROUPS, 32, HID), bf16),
    ]
    def body(*refs):
        ahead, cut = (8, 8 + len(pieces))
        after = cut + len(shards)
        head = refs[:ahead] + (refs[ahead:cut], refs[cut:after]) + refs[after:]
        pl.run_scoped(lambda *buffers: model_kernel(*head, *buffers), *scratch)

    grid_spec = pltpu.PrefetchScalarGridSpec(
        num_scalar_prefetch=3,
        grid=(1,),
        in_specs=[
            pl.BlockSpec((1, nodes, FEAT), lambda i, m, d, p: (m[0], 0, 0)),
            pl.BlockSpec((1, DEG, nodes), lambda i, m, d, p: (m[0], 0, 0)),
        ]
        + vmem(4 + len(pieces) + len(shards)),
        out_specs=vmem(2),
    )
    return pl.pallas_call(
        body,
        grid_spec=grid_spec,
        out_shape=[jax.ShapeDtypeStruct((ROWS // 2, HID), bf16)] * 2,
        compiler_params=pltpu.CompilerParams(vmem_limit_bytes=50 * 1024 * 1024),
        name="model",
    )(section_id, dom_id, spot, features, src_all, labels, label_mask, send_index, *pieces, *shards, small_params)


def settled(total, is_last):
    base = ROW_MISC % PIECE
    block = total[base : base + 16]
    block = jnp.where(is_last == 1, parted(block[0:8] + block[8:16]), block)
    return jnp.concatenate([total[:base], block, total[base + 16 :]], axis=0).astype(bf16)


def last_piece(core, section):
    return jnp.where((core == 1) & (section == 3), 1, 0)


def split_kernel(section_ref, dom_ref, keep_ref, got_ref, *out_refs):
    section = section_ref[0]
    core = jnp.bitwise_and(dom_ref[0], 1)
    for j, out_ref in enumerate(out_refs):
        part = jnp.bitwise_xor(section, j)
        at = pl.ds(pl.multiple_of(part * PIECE, PIECE), PIECE)
        total = keep_ref[at, :].astype(f32) + got_ref[at, :].astype(f32)
        out_ref[...] = settled(total, last_piece(core, part))


def join_kernel(section_ref, dom_ref, own_ref, one_ref, two_ref, three_ref, out_ref):
    pair = own_ref[...].astype(f32) + one_ref[...].astype(f32)
    other = two_ref[...].astype(f32) + three_ref[...].astype(f32)
    core = jnp.bitwise_and(dom_ref[0], 1)
    out_ref[...] = settled(pair + other, last_piece(core, section_ref[0]))


def small_call(kernel, name, ids, count, operands):
    shape = jax.ShapeDtypeStruct((PIECE, HID), bf16)
    return pl.pallas_call(
        kernel,
        out_shape=[shape] * count if count > 1 else shape,
        in_specs=[pl.BlockSpec(memory_space=pltpu.SMEM)] * 2 + vmem(len(operands)),
        out_specs=vmem(count) if count > 1 else vmem(1)[0],
        compiler_params=pltpu.CompilerParams(vmem_limit_bytes=8 * 1024 * 1024),
        name=name,
    )(*ids, *operands)


def sum_gradients(ids, keep, send):
    if lax.axis_size("dom") == 8 and lax.axis_size("section") == 4:
        got = crossed(send, "dom", 1)
        parts = small_call(split_kernel, "split", ids, 4, (keep, got))
        came = [crossed(parts[j], "section", j) for j in range(1, 4)]
        mine = small_call(join_kernel, "join", ids, 1, (parts[0], *came))
        came = [crossed(mine, "dom", 2 * j) for j in range(1, 4)]
        mine = small_call(join_kernel, "join", ids, 1, (mine, *came))
        near = [mine] + [crossed(mine, "section", j) for j in range(1, 4)]
        return near + [crossed(piece, "dom", 1) for piece in near], ids
    all_size = lax.axis_size("dom") * lax.axis_size("section")
    swap = jnp.bitwise_and(ids[1][0], 1) == 1
    partial = jnp.concatenate([jnp.where(swap, send, keep), jnp.where(swap, keep, send)], axis=0)
    parts = lax.all_to_all(partial.reshape(all_size, -1, HID), ("section", "dom"), 0, 0)
    mine = jnp.sum(parts.astype(f32), axis=0)
    shared = jnp.broadcast_to(mine.astype(bf16)[None], (all_size,) + mine.shape)
    summed = lax.all_to_all(shared, ("section", "dom"), 0, 0).reshape(8, PIECE, HID)
    return [summed[j] for j in range(8)], (ids[0] * 0, ids[1] * 0)


def adamw_step(parameter, gradient, moment_one, moment_two):
    moment_one = beta_one * moment_one + (1.0 - beta_one) * gradient
    moment_two = beta_two * moment_two + (1.0 - beta_two) * gradient * gradient
    corr_one = 1.0 - beta_one**STEPS
    corr_two = 1.0 - beta_two**STEPS
    update = moment_one / corr_one / (jnp.sqrt(moment_two / corr_two) + adam_eps)
    return (parameter - adam_rate * (update + adam_decay * parameter), moment_one, moment_two)


def average(old_value, new_value):
    return ema_keep * old_value + (1.0 - ema_keep) * new_value


def dot_tn(a, b):
    return lax.dot_general(a, b, (((0,), (0,)), ((), ())), preferred_element_type=f32)


def halves(value):
    high = value.astype(bf16)
    return high, (value - high.astype(f32)).astype(bf16)


def wide_rows(total):
    return max(total, 16)


def own_rows(gradient, start, count):
    total = gradient.shape[0]
    row = lax.broadcasted_iota(jnp.int32, (wide_rows(count), total), 0) + start
    lane = lax.broadcasted_iota(jnp.int32, (wide_rows(count), total), 1)
    pick = jnp.where(row == lane, 1.0, 0.0).astype(bf16)
    return dot_nn(pick, gradient).astype(bf16)


def precondition(gradient, weight, stat_l, stat_r, root_l, root_r, ema, outs, scale, start):
    (new_w, new_l, new_r, new_ema) = outs
    count = weight.shape[0]
    square = (1.0 - shampoo_decay) * scale * scale
    mine = own_rows(gradient, start, count)
    new_l[...] = shampoo_decay * stat_l + square * dot_nt(mine, gradient)[0:count]
    new_r[...] = shampoo_decay * stat_r + square * dot_tn(gradient, gradient)
    high, low = halves(root_l)
    middle = dot_nn(high, gradient) + dot_nn(low, gradient)
    m_high, m_low = halves(middle * scale)
    r_high, r_low = halves(root_r)
    update = dot_nn(m_high, r_high) + dot_nn(m_low, r_high) + dot_nn(m_high, r_low)
    weight = weight - shampoo_rate * (update + weight_decay * weight)
    new_w[...] = weight
    new_ema[...] = average(ema, weight)


def update_kernel(
    dom_ref,
    section_ref,
    spot_ref,
    piece_0,
    piece_1,
    piece_2,
    piece_3,
    piece_4,
    piece_5,
    piece_6,
    piece_7,
    w_in,
    w_gat,
    w_out,
    small,
    l_in,
    r_in,
    l_gat,
    r_gat,
    l_out,
    r_out,
    rl_in,
    rr_in,
    rl_gat,
    rr_gat,
    rl_out,
    rr_out,
    first,
    second,
    e_in,
    e_gat,
    e_out,
    e_small,
    n_w_in,
    n_w_gat,
    n_w_out,
    n_small,
    n_l_in,
    n_r_in,
    n_l_gat,
    n_r_gat,
    n_l_out,
    n_r_out,
    n_first,
    n_second,
    n_e_in,
    n_e_gat,
    n_e_out,
    n_e_small,
    loss_ref,
    norm_ref,
    sum_ref,
):
    dom = dom_ref[0]
    core = jnp.bitwise_and(spot_ref[0], 1)
    pieces = (piece_0, piece_1, piece_2, piece_3, piece_4, piece_5, piece_6, piece_7)
    for j, piece in enumerate(pieces):
        spot = jnp.bitwise_xor(core, j >> 2) * 4 + jnp.bitwise_xor(section_ref[0], j & 3)
        sum_ref[pl.ds(pl.multiple_of(spot * PIECE, PIECE), PIECE), :] = piece[...]
    grads = sum_ref[0:ROW_MISC, :].astype(f32)
    squares = jnp.sum(grads * grads)
    misc = sum_ref[ROW_MISC : ROW_MISC + 16, :].astype(f32)
    misc = misc[0:8] + misc[8:16]
    row = lax.broadcasted_iota(jnp.int32, (8, HID), 0)
    lane = lax.broadcasted_iota(jnp.int32, (8, HID), 1)
    spot = HSIZE + CLASSES
    loss_ref[0] = jnp.sum(jnp.where((row == 4) & (lane == spot), misc, 0.0))
    small_part = jnp.where((row < 4) | ((row == 4) & (lane < spot)), misc, 0.0)
    squares = squares + jnp.sum(small_part * small_part)
    norm = jnp.sqrt(jnp.broadcast_to(squares, (1, 1)))
    scale = jnp.minimum(1.0, clip_norm / norm)
    norm_ref[0] = jnp.sum(norm)
    for layer in range(2):
        for side in range(2):
            at = (layer, side)
            begin = (2 * layer + side) * HID
            precondition(
                sum_ref[begin : begin + HID, :],
                w_gat[at],
                l_gat[at],
                r_gat[at],
                rl_gat[at],
                rr_gat[at],
                e_gat[at],
                (n_w_gat.at[at], n_l_gat.at[at], n_r_gat.at[at], n_e_gat.at[at]),
                scale,
                dom * w_gat.shape[2],
            )
    precondition(
        sum_ref[ROW_IN:ROW_OUT, :],
        w_in[...],
        l_in[...],
        r_in[...],
        rl_in[...],
        rr_in[...],
        e_in[...],
        (n_w_in, n_l_in, n_r_in, n_e_in),
        scale,
        dom * w_in.shape[0],
    )
    precondition(
        sum_ref[ROW_OUT:ROW_MISC, 0:CLASSES],
        w_out[...],
        l_out[...],
        r_out[...],
        rl_out[...],
        rr_out[...],
        e_out[...],
        (n_w_out, n_l_out, n_r_out, n_e_out),
        scale,
        dom * w_out.shape[0],
    )
    for place in range(5):
        width = HID if place < 4 else spot
        at = pl.ds(place * HID, width)
        gradient = misc[place : place + 1, 0:width] * scale

        def line(ref):
            return ref[at].reshape(1, width)

        new_value, moment_one, moment_two = adamw_step(line(small), gradient, line(first), line(second))
        n_small[at] = new_value.reshape(width)
        n_first[at] = moment_one.reshape(width)
        n_second[at] = moment_two.reshape(width)
        n_e_small[at] = average(line(e_small), new_value).reshape(width)


def per_device(
    features,
    sources,
    send_index,
    labels,
    label_mask,
    w_in,
    w_gat,
    w_out,
    small_params,
    stat_l_in,
    stat_r_in,
    stat_l_gat,
    stat_r_gat,
    stat_l_out,
    stat_r_out,
    root_l_in,
    root_r_in,
    root_l_gat,
    root_r_gat,
    root_l_out,
    root_r_out,
    adam_first,
    adam_second,
    ema_in,
    ema_gat,
    ema_out,
    ema_small,
):
    dom_id = lax.axis_index("dom").astype(jnp.int32).reshape(1)
    section_id = lax.axis_index("section").astype(jnp.int32).reshape(1)
    size = lax.axis_size("dom")
    src_all = jnp.swapaxes(sources, 1, 2)
    packed = pack_inputs(section_id, features, src_all, labels, label_mask, send_index, w_in, w_gat, w_out)
    pieces, spot = gather_weights(dom_id, packed, w_in, w_gat, w_out, label_mask)
    shards = ()
    if size == GROUPS:
        (pieces, shards) = (pieces[1:], (w_in, w_gat, w_out))
    keep, send = run_model(
        section_id,
        dom_id,
        spot,
        features,
        src_all,
        labels,
        label_mask,
        send_index,
        pieces,
        shards,
        small_params,
    )
    pieces, spots = sum_gradients((section_id, dom_id), keep, send)
    state = (
        w_in,
        w_gat,
        w_out,
        small_params,
        stat_l_in,
        stat_r_in,
        stat_l_gat,
        stat_r_gat,
        stat_l_out,
        stat_r_out,
        root_l_in,
        root_r_in,
        root_l_gat,
        root_r_gat,
        root_l_out,
        root_r_out,
        adam_first,
        adam_second,
        ema_in,
        ema_gat,
        ema_out,
        ema_small,
    )
    like = state[:10] + (adam_first, adam_second, ema_in, ema_gat, ema_out, ema_small)
    results = pl.pallas_call(
        update_kernel,
        out_shape=[jax.ShapeDtypeStruct(v.shape, f32) for v in like] + [jax.ShapeDtypeStruct((1,), f32)] * 2,
        in_specs=[pl.BlockSpec(memory_space=pltpu.SMEM)] * 3 + vmem(30),
        out_specs=vmem(16) + [pl.BlockSpec(memory_space=pltpu.SMEM)] * 2,
        scratch_shapes=[pltpu.VMEM((ROWS, HID), bf16)],
        compiler_params=pltpu.CompilerParams(vmem_limit_bytes=16 * 1024 * 1024),
        name="update",
    )(dom_id, *spots, *pieces, *state)
    return tuple(results[:16]) + (results[16].reshape(()), results[17].reshape(()))


def solution(mesh):
    placed = (
        P(None, "dom", None),
        P(None, "dom", None),
        P(None, "dom"),
        P(None, "dom"),
        P(None, "dom"),
        P("dom", None),
        P(None, None, "dom", None),
        P("dom", None),
        P(),
        P("dom", None),
        P(),
        P(None, None, "dom", None),
        P(),
        P("dom", None),
        P(),
        P("dom", None),
        P(),
        P(None, None, "dom", None),
        P(),
        P("dom", None),
        P(),
        P(),
        P(),
        P("dom", None),
        P(None, None, "dom", None),
        P("dom", None),
        P(),
    )
    return jax.shard_map(
        per_device,
        mesh=mesh,
        in_specs=placed,
        out_specs=(
            P("dom", None),
            P(None, None, "dom", None),
            P("dom", None),
            P(),
            P("dom", None),
            P(),
            P(None, None, "dom", None),
            P(),
            P("dom", None),
            P(),
            P(),
            P(),
            P("dom", None),
            P(None, None, "dom", None),
            P("dom", None),
            P(),
            P(),
            P(),
        ),
        check_vma=False,
    )
```
